256 devices in a mesh: light: 64 (over y, x_lo, z), tex: 4 (over x_hi, core).
Axes of the slice: x: 4 (x_hi: 2, x_lo: 2; x = x_hi * 2 + x_lo), y: 4, z: 8, core: 2. Of those that a mesh axis runs over, the one named last changes fastest.
Arguments:
- light_ids: int32 [128], P('light'), may hold values from 0 to 255
- tile_offsets: int32 [128], P('light'), may hold values from 0 to 4095
- light_table: bfloat16 [256, 512], replicated, may hold values from -6 to 6
- hyper_weight: bfloat16 [512, 1179648], P(None, ('light', 'tex')), may hold values from -0.25 to 0.25
- features: bfloat16 [128, 64, 48, 256], P('light', 'tex'), may hold values from -6 to 6
- upstream_grad: bfloat16 [128, 64, 48, 256], P('light', 'tex'), may hold values from -3 to 3
Outputs:
- relit: bfloat16 [128, 64, 48, 256], P('light', 'tex')
- feature_grad: bfloat16 [128, 64, 48, 256], P('light', 'tex')
- hyper_grad: bfloat16 [512, 1179648], P(None, ('light', 'tex'))
The draws below stay inside these ranges and needn't reach their ends.
All inputs are finite; a program needn't handle non-finite values.
Results may differ from the reference program's by a relative error of at most 0.02.
Values may be sent and summed in bfloat16 or wider, within the bound.
A program may use at most 128 MiB of HBM per device.

```python
import math
import jax
import jax.numpy as jnp
from jax import lax

Z = 512
C = 256
COLS = 48
TABLE = 256
LIGHTS = 128
TILE_ROWS = 64
P_SIZE = 1179648


def place_ends(entries, key, smallest, top_value):
    longest = entries.shape.index(max(entries.shape))
    spots = []
    for shift in (0, 1):
        where = [jax.random.randint(jax.random.fold_in(key, axis), (), 0, length) for axis, length in enumerate(entries.shape)]
        where[longest] = (where[longest] + shift) % entries.shape[longest]
        spots.append(tuple(where))
    return entries.at[spots[0]].set(smallest).at[spots[1]].set(top_value)


def block_levels(key, extent, shards, least, high):
    loudness, own = 1.0, jax.random.fold_in(key, 6)
    for position, shards_of in shards:
        draws = jnp.exp(jax.random.uniform(jax.random.fold_in(own, position), (shards_of,), jnp.float32, least / len(shards), high / len(shards)))
        loudness = loudness * jnp.repeat(draws, extent[position] // shards_of).reshape([-1 if axis == position else 1 for axis in range(len(extent))])
    return loudness


def bell_draw(own_key, shape, spread, most, cuts=(), kind=jnp.bfloat16):
    drawn = jax.random.normal(own_key, shape, jnp.float32) * spread
    if len(cuts) > 0:
        drawn = block_levels(own_key, shape, cuts, -0.22, 0.18) * drawn
    return jnp.clip(drawn, min=-most, max=most).astype(kind)


def setup_inputs(seed: int = 0) -> dict:
    arg_keys = jax.random.split(jax.random.key(seed), 7)
    return {
        "light_ids": place_ends(jax.random.randint(arg_keys[0], (LIGHTS,), 0, TABLE), jax.random.fold_in(arg_keys[0], 1), 0, TABLE - 1).astype(jnp.int32),
        "tile_offsets": place_ends(jax.random.randint(arg_keys[1], (LIGHTS,), 0, 4096), jax.random.fold_in(arg_keys[1], 1), 0, 4095).astype(jnp.int32),
        "light_table": bell_draw(arg_keys[2], (TABLE, Z), 1.0, 6.0),
        "hyper_weight": bell_draw(arg_keys[3], (Z, P_SIZE), Z ** -0.5, 0.25, ((1, 256),)),
        "features": bell_draw(arg_keys[4], (LIGHTS, TILE_ROWS, COLS, C), 1.0, 6.0, ((0, 64), (1, 4))),
        "upstream_grad": bell_draw(arg_keys[5], (LIGHTS, TILE_ROWS, COLS, C), 0.5, 3.0, ((0, 64), (1, 4))),
    }


def stored(values):
    return lax.optimization_barrier(values.astype(jnp.bfloat16))

def smooth_act(values):
    return values * jax.nn.sigmoid(values)

def smooth_slope(values):
    sig = jax.nn.sigmoid(values)
    return sig * (1.0 + values * (1.0 - sig))

def light_codes(light_ids, tile_offsets, light_table):
    halfway = light_table.shape[1] // 2
    onehot = (light_ids[:, None] == jnp.arange(light_table.shape[0], dtype=jnp.int32)[None, :]).astype(jnp.float32)
    looked = jnp.dot(onehot, light_table.astype(jnp.float32))
    rates = jnp.exp(-math.log(1000.0) * jnp.arange(halfway, dtype=jnp.float32) / halfway)
    angles = tile_offsets.astype(jnp.float32)[:, None] * rates[None, :]
    summed = looked + jnp.concatenate([jnp.sin(angles), jnp.cos(angles)], axis=1)
    return stored(summed * lax.rsqrt(lax.optimization_barrier(jnp.mean(summed * summed, axis=1, keepdims=True)) + 1e-06))

def tile_patches(padded, out_rows):
    columns = padded.shape[1]
    wide = jnp.pad(padded, ((0, 0), (1, 1), (0, 0)))
    pieces = [wide[row_tap:row_tap + out_rows, col_tap:col_tap + columns, :] for row_tap in range(3) for col_tap in range(3)]
    return jnp.concatenate(pieces, axis=2).astype(jnp.float32)

def tile_conv(patches, kernel):
    rows_out, columns, depth = patches.shape
    return jnp.dot(patches.reshape(rows_out * columns, depth), kernel).reshape(rows_out, columns, -1)

def tile_kgrad(patches, upstream):
    depth = patches.shape[2]
    return jnp.dot(patches.reshape(-1, depth).T, upstream.astype(jnp.float32).reshape(-1, upstream.shape[2]))

def flipped(kernel):
    channels = kernel.shape[1]
    return kernel.reshape(3, 3, channels, channels)[::-1, ::-1].swapaxes(2, 3).reshape(9 * channels, channels)

def row_pad(values):
    return jnp.pad(values, ((1, 1), (0, 0), (0, 0)))

def reference(light_ids, tile_offsets, light_table, hyper_weight, features, upstream_grad):
    scale = 1.0 / math.sqrt(9 * C)
    codes = light_codes(light_ids, tile_offsets, light_table)
    weights = stored(scale * jnp.dot(codes.astype(jnp.float32), hyper_weight.astype(jnp.float32)))
    kernel_len = 9 * C * C

    def one_light(inputs):
        kernel_row, feats, upstream = inputs
        kernel_row = kernel_row.astype(jnp.float32)
        first_kernel = kernel_row[:kernel_len].reshape(9 * C, C)
        second_kernel = kernel_row[kernel_len:].reshape(9 * C, C)
        input_patches = tile_patches(row_pad(feats), TILE_ROWS)
        first_pre = tile_conv(input_patches, first_kernel)
        hidden = stored(smooth_act(first_pre))
        hidden_patches = tile_patches(row_pad(hidden), TILE_ROWS)
        second_pre = tile_conv(hidden_patches, second_kernel)
        relit = smooth_act(second_pre).astype(jnp.bfloat16)
        second_grad = stored(upstream.astype(jnp.float32) * smooth_slope(second_pre))
        hidden_grad = tile_conv(tile_patches(row_pad(second_grad), TILE_ROWS), flipped(second_kernel))
        first_grad = stored(hidden_grad * smooth_slope(first_pre))
        feature_grad = tile_conv(tile_patches(row_pad(first_grad), TILE_ROWS), flipped(first_kernel)).astype(jnp.bfloat16)
        first_kgrad = tile_kgrad(input_patches, first_grad)
        second_kgrad = tile_kgrad(hidden_patches, second_grad)
        kgrad = jnp.concatenate([first_kgrad.reshape(-1), second_kgrad.reshape(-1)])
        return (relit, feature_grad, kgrad)
    relit, feature_grad, kgrad = lax.map(one_light, (weights, features, upstream_grad))
    rounded = stored(kgrad).astype(jnp.float32)
    hyper_grad = (scale * jnp.dot(codes.astype(jnp.float32).T, rounded)).astype(jnp.bfloat16)
    return (relit, feature_grad, hyper_grad)
```

```python
import math

import jax
import jax.numpy as jnp
from jax import lax
from jax.sharding import PartitionSpec as P


def padded_2(block, sides, width):
    for axis, dim in sides:
        count = lax.axis_size(axis)
        forward = [(i, i + 1) for i in range(count - 1)]
        backward = [(target, source) for source, target in forward]
        low = lax.ppermute(
            lax.slice_in_dim(block, block.shape[dim] - width, None, axis=dim), axis, forward
        )
        high = lax.ppermute(lax.slice_in_dim(block, 0, width, axis=dim), axis, backward)
        block = jnp.concatenate([low, block, high], axis=dim)
    return block


def smooth_act(values):
    return values * jax.nn.sigmoid(values)


def smooth_slope(values):
    sig = jax.nn.sigmoid(values)
    return sig * (1.0 + values * (1.0 - sig))


def light_codes(light_ids, tile_offsets, light_table):
    halfway = light_table.shape[1] // 2
    onehot = (
        light_ids[:, None] == jnp.arange(light_table.shape[0], dtype=jnp.int32)[None, :]
    ).astype(jnp.bfloat16)
    looked = jnp.dot(onehot, light_table, preferred_element_type=jnp.float32)
    rates = jnp.exp(-math.log(1000.0) * jnp.arange(halfway, dtype=jnp.float32) / halfway)
    angles = tile_offsets.astype(jnp.float32)[:, None] * rates[None, :]
    summed = looked + jnp.concatenate([jnp.sin(angles), jnp.cos(angles)], axis=1)
    return (summed * lax.rsqrt(jnp.mean(summed * summed, axis=1, keepdims=True) + 1e-06)).astype(
        jnp.bfloat16
    )


def build_patches(padded, out_rows):
    columns = padded.shape[2]
    wide = jnp.pad(padded, ((0, 0), (0, 0), (1, 1), (0, 0)))
    pieces = [
        wide[:, row_tap : row_tap + out_rows, col_tap : col_tap + columns, :]
        for row_tap in range(3)
        for col_tap in range(3)
    ]
    return jnp.concatenate(pieces, axis=3)


def apply_conv(patches, kernel):
    return jnp.einsum("lrck,lko->lrco", patches, kernel, preferred_element_type=jnp.float32)


def kernel_grad(patches, upstream):
    return jnp.einsum("lrck,lrco->lko", patches, upstream, preferred_element_type=jnp.float32)


def flipped(kernel):
    lights_here, depth, channels = kernel.shape
    shaped = kernel.reshape(lights_here, 3, 3, channels, channels)
    return shaped[:, ::-1, ::-1].swapaxes(3, 4).reshape(lights_here, depth, channels)


def shards(light_ids, tile_offsets, light_table, hyper_weight, features, upstream_grad):
    lights_dev, rows_dev, channels = (features.shape[0], features.shape[1], features.shape[3])
    scale = 1.0 / math.sqrt(9 * channels)
    kernel_len = 9 * channels * channels
    own_codes = light_codes(light_ids, tile_offsets, light_table)
    devices = lax.axis_size("light")
    quarters = lax.axis_size("tex")
    own_len = hyper_weight.shape[1]
    copies = jnp.broadcast_to(own_codes[None], (devices,) + own_codes.shape)
    all_codes = lax.all_to_all(copies, "light", split_axis=0, concat_axis=0, tiled=True).reshape(
        devices * lights_dev, -1
    )
    columns = (scale * jnp.dot(all_codes, hyper_weight, preferred_element_type=jnp.float32)).astype(
        jnp.bfloat16
    )
    mine = lax.all_to_all(
        columns.reshape(devices, lights_dev, own_len), "light", split_axis=0, concat_axis=0, tiled=True
    )
    weights = lax.all_gather(mine, "tex", axis=0)
    weights = weights.transpose(2, 1, 0, 3).reshape(lights_dev, 2 * kernel_len)
    first_kernel = weights[:, :kernel_len].reshape(lights_dev, 9 * channels, channels)
    second_kernel = weights[:, kernel_len:].reshape(lights_dev, 9 * channels, channels)
    padded_in = padded_2(features, (("tex", 1),), 1)
    input_patches = build_patches(padded_in, rows_dev)
    first_pre = apply_conv(input_patches, first_kernel)
    hidden = smooth_act(first_pre).astype(jnp.bfloat16)
    padded_hidden = padded_2(hidden, (("tex", 1),), 1)
    hidden_patches = build_patches(padded_hidden, rows_dev)
    second_pre = apply_conv(hidden_patches, second_kernel)
    relit = smooth_act(second_pre).astype(jnp.bfloat16)
    second_grad = (upstream_grad * smooth_slope(second_pre)).astype(jnp.bfloat16)
    padded_grad = padded_2(second_grad, (("tex", 1),), 1)
    hidden_grad = apply_conv(build_patches(padded_grad, rows_dev), flipped(second_kernel))
    first_grad = (hidden_grad * smooth_slope(first_pre)).astype(jnp.bfloat16)
    padded_first = padded_2(first_grad, (("tex", 1),), 1)
    feature_grad = apply_conv(build_patches(padded_first, rows_dev), flipped(first_kernel)).astype(
        jnp.bfloat16
    )
    first_kgrad = kernel_grad(input_patches, first_grad)
    second_kgrad = kernel_grad(hidden_patches, second_grad)
    grads = jnp.concatenate(
        [first_kgrad.reshape(lights_dev, -1), second_kgrad.reshape(lights_dev, -1)], axis=1
    )
    blocks = grads.astype(jnp.bfloat16).reshape(lights_dev, devices, quarters, own_len)
    mixed = lax.psum_scatter(
        blocks.transpose(2, 1, 0, 3), "tex", scatter_dimension=0, tiled=False
    )
    summed = lax.all_to_all(mixed, "light", split_axis=0, concat_axis=0, tiled=True).reshape(
        devices * lights_dev, own_len
    )
    hyper_grad = (
        scale * jnp.einsum("lz,ls->zs", all_codes, summed, preferred_element_type=jnp.float32)
    ).astype(jnp.bfloat16)
    return (relit, feature_grad, hyper_grad)


def solution(mesh):
    in_specs = (
        P("light"),
        P("light"),
        P(),
        P(None, ("light", "tex")),
        P("light", "tex", None, None),
        P("light", "tex", None, None),
    )
    out_specs = (
        P("light", "tex", None, None),
        P("light", "tex", None, None),
        P(None, ("light", "tex")),
    )
    return jax.shard_map(shards, mesh=mesh, in_specs=in_specs, out_specs=out_specs, check_vma=False)
```

```python
import functools
import math

import jax
import jax.numpy as jnp
from jax import lax
from jax.experimental import pallas as pl
from jax.experimental.pallas import tpu as pltpu
from jax.sharding import PartitionSpec as P

MESH = pl.DeviceIdType.MESH
LANES = 128
GROUP = 16


def smooth_act(values):
    return values * jax.nn.sigmoid(values)


def smooth_slope(values):
    sig = jax.nn.sigmoid(values)
    return sig * (1.0 + values * (1.0 - sig))


def light_codes(light_ids, tile_offsets, light_table):
    halfway = light_table.shape[1] // 2
    onehot = (
        light_ids[:, None] == jnp.arange(light_table.shape[0], dtype=jnp.int32)[None, :]
    ).astype(jnp.bfloat16)
    looked = jnp.dot(onehot, light_table, preferred_element_type=jnp.float32)
    rates = jnp.exp(-math.log(1000.0) * jnp.arange(halfway, dtype=jnp.float32) / halfway)
    angles = tile_offsets.astype(jnp.float32)[:, None] * rates[None, :]
    summed = looked + jnp.concatenate([jnp.sin(angles), jnp.cos(angles)], axis=1)
    return (summed * lax.rsqrt(jnp.mean(summed * summed, axis=1, keepdims=True) + 1e-06)).astype(
        jnp.bfloat16
    )


def place():
    light, tex = lax.axis_index("light"), lax.axis_index("tex")
    half, core = tex // 2, tex % 2
    return light, half, core, light * 2 + half


def peer(chip, core):
    return (chip // 2, (chip % 2) * 2 + core)


def await_bytes(ref, sem):
    pltpu.make_async_copy(ref, ref, sem).wait()


def swap_copies(src, dst, halo, send, recv, start):
    light, half, core, _ = place()
    rows = src.shape[1]

    def go(source, target, to_half, to_core, slot, number):
        here = jnp.logical_and(to_half == half, to_core == core)

        @pl.when(here)
        def _():
            if start:
                pltpu.make_async_copy(source, target, recv.at[slot]).start()

        @pl.when(jnp.logical_not(here))
        def _():
            copy = pltpu.make_async_remote_copy(
                src_ref=source,
                dst_ref=target,
                send_sem=send.at[number],
                recv_sem=recv.at[slot],
                device_id=(light, to_half * 2 + to_core),
                device_id_type=MESH,
            )
            if start:
                copy.start()
            else:
                copy.wait_send()

    for to_half in range(2):
        for own in range(2):

            @pl.when(core == own)
            def _():
                go(
                    src.at[to_half],
                    dst.at[pl.ds(own * rows + halo, rows)],
                    to_half,
                    half,
                    own,
                    to_half,
                )

        @pl.when(jnp.logical_and(half == 1, core == 0))
        def _():
            go(
                src.at[to_half, pl.ds(0, halo)],
                dst.at[pl.ds(2 * rows + halo, halo)],
                to_half,
                0,
                2,
                2 + to_half,
            )

        @pl.when(jnp.logical_and(half == 0, core == 1))
        def _():
            go(
                src.at[to_half, pl.ds(rows - halo, halo)],
                dst.at[pl.ds(0, halo)],
                to_half,
                1,
                2,
                2 + to_half,
            )


def swap_arrivals(src, dst, halo, recv):
    rows = src.shape[1]
    for slot, count in ((0, rows), (1, rows), (2, halo)):
        await_bytes(dst.at[pl.ds(0, count)], recv.at[slot])


def forward_kernel(
    scale,
    lights,
    codes_ref,
    hyper_ref,
    feat_ref,
    up_ref,
    blocks_ref,
    codes_out,
    feat_out,
    up_out,
    hyper,
    codes,
    wide,
    ready,
    hyper_sem,
    code_send,
    code_recv,
    own_sem,
    block_send,
    block_recv,
    pass_send,
    pass_recv,
    feat_send,
    feat_recv,
    up_send,
    up_recv,
):
    light, half, core, me = place()
    chips = 2 * lights
    groups = chips // GROUP
    load = pltpu.make_async_copy(hyper_ref, hyper, hyper_sem)
    load.start()

    codes[pl.ds(pl.multiple_of(light * 8, 8), 8), :] = codes_ref[...]

    def send_codes(step, _):
        other = lax.rem(light + step, lights)
        pltpu.make_async_remote_copy(
            src_ref=codes_ref,
            dst_ref=codes.at[pl.ds(pl.multiple_of(light * 8, 8), 8)],
            send_sem=code_send,
            recv_sem=code_recv,
            device_id=(other, half * 2 + core),
            device_id_type=MESH,
        ).start()
        return 0

    lax.fori_loop(1, lights, send_codes, 0)
    swap_copies(feat_ref, feat_out, 4, feat_send, feat_recv, True)
    swap_copies(up_ref, up_out, 2, up_send, up_recv, True)
    arrived = codes.at[pl.ds(0, 8 * (lights - 1))]
    await_bytes(arrived, code_recv)
    parts = [codes[pl.ds(k, chips, stride=4), :] for k in range(4)]
    table = jnp.concatenate(parts, axis=1).astype(jnp.bfloat16)
    codes_out[...] = table
    load.wait()
    rows = hyper.shape[1] // (2 * LANES)
    for row in range(rows):
        product = scale * jnp.dot(
            table,
            hyper[:, row * 2 * LANES : (row + 1) * 2 * LANES],
            preferred_element_type=jnp.float32,
        )
        wide[pl.ds(row, chips, stride=40), :] = product[:, :LANES]
        wide[pl.ds(rows + row, chips, stride=40), :] = product[:, LANES:]

    def narrow(chip, _):
        ready[chip] = wide[pl.ds(pl.multiple_of(chip * 40, 8), 2 * rows), :].astype(jnp.bfloat16)
        return 0

    lax.fori_loop(0, chips, narrow, 0)

    keep = pltpu.make_async_copy(ready.at[me], blocks_ref.at[core, me], own_sem)
    keep.start()
    my_group, my_slot = me // GROUP, me % GROUP

    def send_block(step, _):
        group = lax.rem(my_group + step // GROUP, groups)
        slot = lax.rem(my_slot + step % GROUP, GROUP)
        other = group * GROUP + slot
        pltpu.make_async_remote_copy(
            src_ref=ready.at[other],
            dst_ref=blocks_ref.at[core, me],
            send_sem=block_send,
            recv_sem=block_recv.at[my_group],
            device_id=peer(other, core),
            device_id_type=MESH,
        ).start()
        return 0

    lax.fori_loop(1, chips, send_block, 0)

    def to_sibling(group):
        span = blocks_ref.at[core, pl.ds(group * GROUP, GROUP)]
        return pltpu.make_async_remote_copy(
            src_ref=span,
            dst_ref=span,
            send_sem=pass_send.at[group],
            recv_sem=pass_recv.at[group],
            device_id=(light, half * 2 + 1 - core),
            device_id_type=MESH,
        )

    keep.wait()
    await_bytes(blocks_ref.at[core, pl.ds(0, GROUP - 1)], block_recv.at[my_group])
    to_sibling(my_group).start()

    def pass_on(step, _):
        group = lax.rem(my_group + groups - step, groups)
        await_bytes(blocks_ref.at[core, pl.ds(0, GROUP)], block_recv.at[group])
        to_sibling(group).start()
        return 0

    lax.fori_loop(1, groups, pass_on, 0)

    def finish(group, _):
        to_sibling(group).wait()
        return 0

    lax.fori_loop(0, groups, finish, 0)
    await_bytes(ready.at[pl.ds(0, chips - 1)], block_send)
    await_bytes(arrived, code_send)
    swap_copies(feat_ref, feat_out, 4, feat_send, feat_recv, False)
    swap_copies(up_ref, up_out, 2, up_send, up_recv, False)
    swap_arrivals(feat_ref, feat_out, 4, feat_recv)
    swap_arrivals(up_ref, up_out, 2, up_recv)


def forward_exchange(scale, lights, codes, hyper_weight, features, upstream):
    chips = 2 * lights
    depth, own_len = hyper_weight.shape
    block_rows = own_len // LANES
    _, rows, columns, channels = features.shape
    dma = pltpu.SemaphoreType.DMA
    anywhere = pl.BlockSpec(memory_space=pl.ANY)
    vmem = pl.BlockSpec(memory_space=pltpu.VMEM)
    return pl.pallas_call(
        functools.partial(forward_kernel, scale, lights),
        out_shape=(
            jax.ShapeDtypeStruct((2, chips, block_rows, LANES), jnp.bfloat16),
            jax.ShapeDtypeStruct((chips, depth), jnp.bfloat16),
            jax.ShapeDtypeStruct((2 * rows + 8, columns, channels), jnp.bfloat16),
            jax.ShapeDtypeStruct((2 * rows + 4, columns, channels), jnp.bfloat16),
        ),
        in_specs=[vmem, anywhere, anywhere, anywhere],
        out_specs=(anywhere, vmem, anywhere, anywhere),
        scratch_shapes=[
            pltpu.VMEM((depth, own_len), jnp.bfloat16),
            pltpu.VMEM((8 * lights, LANES), jnp.float32),
            pltpu.VMEM((chips * 40, LANES), jnp.float32),
            pltpu.VMEM((chips, block_rows, LANES), jnp.bfloat16),
            dma,
            dma,
            dma,
            dma,
            dma,
            dma((chips // GROUP,)),
            dma((chips // GROUP,)),
            dma((chips // GROUP,)),
            dma((4,)),
            dma((3,)),
            dma((4,)),
            dma((3,)),
        ],
        compiler_params=pltpu.CompilerParams(
            has_side_effects=True, vmem_limit_bytes=40 * 1024 * 1024
        ),
    )(codes, hyper_weight, features, upstream)


def give_back(src, dst, send, recv, start):
    light, half, core, _ = place()
    rows = dst.shape[1]
    for piece in range(2):
        here = jnp.logical_and(core == half, piece == core)
        source = src.at[pl.ds(piece * rows, rows)]
        for own in range(2):

            @pl.when(jnp.logical_and(here, half == own))
            def _():
                if start:
                    pltpu.make_async_copy(source, dst.at[own], recv.at[own]).start()

            @pl.when(jnp.logical_and(jnp.logical_not(here), half == own))
            def _():
                copy = pltpu.make_async_remote_copy(
                    src_ref=source,
                    dst_ref=dst.at[own],
                    send_sem=send.at[piece],
                    recv_sem=recv.at[own],
                    device_id=(light, core * 2 + piece),
                    device_id_type=MESH,
                )
                if start:
                    copy.start()
                else:
                    copy.wait_send()


def backward_kernel(
    lights,
    parts_ref,
    relit_ref,
    grad_ref,
    sums_ref,
    relit_out,
    grad_out,
    mine,
    theirs,
    ready,
    mine_sem,
    core_send,
    core_recv,
    own_sem,
    block_send,
    block_recv,
    relit_send,
    relit_recv,
    grad_send,
    grad_recv,
):
    light, half, core, me = place()
    chips = 2 * lights
    groups = chips // GROUP
    my_group, my_slot = me // GROUP, me % GROUP
    load = pltpu.make_async_copy(parts_ref.at[core], mine, mine_sem)
    load.start()

    def to_sibling(group):
        return pltpu.make_async_remote_copy(
            src_ref=parts_ref.at[1 - core, pl.ds(group * GROUP, GROUP)],
            dst_ref=theirs.at[pl.ds(group * GROUP, GROUP)],
            send_sem=core_send.at[group],
            recv_sem=core_recv.at[group],
            device_id=(light, half * 2 + 1 - core),
            device_id_type=MESH,
        )

    def start_group(step, _):
        to_sibling(lax.rem(my_group + step, groups)).start()
        return 0

    lax.fori_loop(0, groups, start_group, 0)
    give_back(relit_ref, relit_out, relit_send, relit_recv, True)
    give_back(grad_ref, grad_out, grad_send, grad_recv, True)
    load.wait()

    def send_block(other):
        pltpu.make_async_remote_copy(
            src_ref=ready.at[other],
            dst_ref=sums_ref.at[me],
            send_sem=block_send,
            recv_sem=block_recv,
            device_id=peer(other, core),
            device_id_type=MESH,
        ).start()

    def do_group(step, _):
        group = lax.rem(my_group + step, groups)
        to_sibling(group).wait_recv()

        def do_block(slot, _):
            other = group * GROUP + lax.rem(my_slot + slot, GROUP)
            ready[other] = (
                mine[other].astype(jnp.float32) + theirs[other].astype(jnp.float32)
            ).astype(jnp.bfloat16)

            @pl.when(other != me)
            def _():
                send_block(other)

            return 0

        return lax.fori_loop(0, GROUP, do_block, 0)

    lax.fori_loop(0, groups, do_group, 0)
    keep = pltpu.make_async_copy(ready.at[me], sums_ref.at[me], own_sem)
    keep.start()
    keep.wait()

    def finish(group, _):
        to_sibling(group).wait_send()
        return 0

    lax.fori_loop(0, groups, finish, 0)
    give_back(relit_ref, relit_out, relit_send, relit_recv, False)
    give_back(grad_ref, grad_out, grad_send, grad_recv, False)
    for own in range(2):
        await_bytes(relit_out.at[own], relit_recv.at[own])
        await_bytes(grad_out.at[own], grad_recv.at[own])
    await_bytes(ready.at[pl.ds(0, chips - 1)], block_send)
    await_bytes(sums_ref.at[pl.ds(0, chips - 1)], block_recv)


def backward_exchange(lights, parts, relit, feature_grad):
    _, chips, block_rows, lanes = parts.shape
    rows, columns, channels = relit.shape
    dma = pltpu.SemaphoreType.DMA
    anywhere = pl.BlockSpec(memory_space=pl.ANY)
    image = jax.ShapeDtypeStruct((2, rows // 2, columns, channels), jnp.bfloat16)
    return pl.pallas_call(
        functools.partial(backward_kernel, lights),
        out_shape=(
            jax.ShapeDtypeStruct((chips, block_rows, lanes), jnp.bfloat16),
            image,
            image,
        ),
        in_specs=[anywhere] * 3,
        out_specs=(anywhere,) * 3,
        scratch_shapes=[
            pltpu.VMEM((chips, block_rows, lanes), jnp.bfloat16),
            pltpu.VMEM((chips, block_rows, lanes), jnp.bfloat16),
            pltpu.VMEM((chips, block_rows, lanes), jnp.bfloat16),
            dma,
            dma((chips // GROUP,)),
            dma((chips // GROUP,)),
            dma,
            dma,
            dma,
            dma((2,)),
            dma((2,)),
            dma((2,)),
            dma((2,)),
        ],
        compiler_params=pltpu.CompilerParams(
            has_side_effects=True, vmem_limit_bytes=40 * 1024 * 1024
        ),
    )(parts, relit, feature_grad)


def conv(image, kernel):
    return lax.conv_general_dilated(
        image[None],
        kernel,
        (1, 1),
        ((0, 0), (1, 1)),
        dimension_numbers=("NHWC", "HWIO", "NHWC"),
        preferred_element_type=jnp.float32,
    )[0]


def conv_back(image, kernel):
    return lax.conv_general_dilated(
        image[None],
        kernel[::-1, ::-1],
        (1, 1),
        ((0, 0), (1, 1)),
        dimension_numbers=("NHWC", "HWOI", "NHWC"),
        preferred_element_type=jnp.float32,
    )[0]


def kernel_grad(image, upstream):
    return lax.conv_general_dilated(
        image[None],
        upstream[None],
        (1, 1),
        ((0, 0), (1, 1)),
        dimension_numbers=("CHWN", "IHWO", "HWNC"),
        preferred_element_type=jnp.float32,
    )


def shards(light_ids, tile_offsets, light_table, hyper_weight, features, upstream_grad):
    rows_dev, channels = features.shape[1], features.shape[3]
    scale = 1.0 / math.sqrt(9 * channels)
    lights = lax.axis_size("light")
    rows = 2 * rows_dev
    core = lax.axis_index("tex") % 2
    own_codes = light_codes(light_ids, tile_offsets, light_table)
    blocks, codes, feats, upstream = forward_exchange(
        scale,
        lights,
        own_codes.astype(jnp.float32).reshape(8, LANES),
        hyper_weight,
        features,
        upstream_grad,
    )
    chips = 2 * lights
    taps = hyper_weight.shape[1] // channels
    kernels = (
        blocks.reshape(2, chips, 2, taps, LANES)
        .transpose(1, 0, 3, 2, 4)
        .reshape(2, 3, 3, channels, channels)
    )

    def inside(values, halo):
        spot = jnp.arange(rows + 2 * halo) + core * rows - halo
        kept = jnp.logical_and(spot >= 0, spot < 2 * rows)[:, None, None]
        return jnp.where(kept, values, jnp.zeros_like(values))

    feats = inside(feats, 4)
    first_pre = conv(feats, kernels[0])
    hidden = inside(smooth_act(first_pre), 3).astype(jnp.bfloat16)
    second_pre = conv(hidden, kernels[1])
    relit = smooth_act(second_pre[2 : rows + 2]).astype(jnp.bfloat16)
    second_grad = inside(upstream * smooth_slope(second_pre), 2).astype(jnp.bfloat16)
    hidden_grad = conv_back(second_grad, kernels[1])
    first_grad = inside(hidden_grad * smooth_slope(first_pre[2 : rows + 4]), 1).astype(
        jnp.bfloat16
    )
    feature_grad = conv_back(first_grad, kernels[0]).astype(jnp.bfloat16)
    first_kgrad = kernel_grad(feats[3 : rows + 5], first_grad[1 : rows + 1])
    second_kgrad = kernel_grad(hidden[2 : rows + 4], second_grad[2 : rows + 2])
    parts = (
        jnp.stack([first_kgrad, second_kgrad])
        .astype(jnp.bfloat16)
        .reshape(chips, 2, taps, 2, LANES)
        .transpose(1, 0, 3, 2, 4)
        .reshape(2, chips, 2 * taps, LANES)
    )
    sums, relit, feature_grad = backward_exchange(lights, parts, relit, feature_grad)
    summed = (
        sums.reshape(chips, 2, taps, LANES).transpose(0, 2, 1, 3).reshape(chips, taps * channels)
    )
    hyper_grad = (
        scale * jnp.einsum("lz,ls->zs", codes, summed, preferred_element_type=jnp.float32)
    ).astype(jnp.bfloat16)
    return (relit, feature_grad, hyper_grad)


def solution(mesh):
    in_specs = (
        P("light"),
        P("light"),
        P(),
        P(None, ("light", "tex")),
        P("light", "tex", None, None),
        P("light", "tex", None, None),
    )
    out_specs = (
        P("light", "tex", None, None),
        P("light", "tex", None, None),
        P(None, ("light", "tex")),
    )
    return jax.shard_map(shards, mesh=mesh, in_specs=in_specs, out_specs=out_specs, check_vma=False)
```

```python
import functools
import math

import jax
import jax.numpy as jnp
from jax import lax
from jax.experimental import pallas as pl
from jax.experimental.pallas import tpu as pltpu
from jax.sharding import PartitionSpec as P

MESH = pl.DeviceIdType.MESH
LANES = 128
GROUP = 16
HALO = 4
VMEM = 60 * 1024 * 1024


def light_codes(light_ids, tile_offsets, light_table):
    halfway = light_table.shape[1] // 2
    onehot = (
        light_ids[:, None] == jnp.arange(light_table.shape[0], dtype=jnp.int32)[None, :]
    ).astype(jnp.bfloat16)
    looked = jnp.dot(onehot, light_table, preferred_element_type=jnp.float32)
    rates = jnp.exp(-math.log(1000.0) * jnp.arange(halfway, dtype=jnp.float32) / halfway)
    angles = tile_offsets.astype(jnp.float32)[:, None] * rates[None, :]
    summed = looked + jnp.concatenate([jnp.sin(angles), jnp.cos(angles)], axis=1)
    return (summed * lax.rsqrt(jnp.mean(summed * summed, axis=1, keepdims=True) + 1e-06)).astype(
        jnp.bfloat16
    )


def place():
    light, tex = lax.axis_index("light"), lax.axis_index("tex")
    half, core = tex // 2, tex % 2
    return light, half, core, light * 2 + half


def peer(chip, core):
    return (chip // 2, (chip % 2) * 2 + core)


def greet():
    light, half, core, me = place()
    chips = 2 * lax.axis_size("light")
    barrier = pltpu.get_barrier_semaphore()

    def signal(target):
        pl.semaphore_signal(barrier, inc=1, device_id=target, device_id_type=MESH)

    def signal_chip(step, _):
        signal(peer(lax.rem(me + step, chips), core))
        return 0

    lax.fori_loop(1, chips, signal_chip, 0)
    signal((light, half * 2 + 1 - core))
    signal((light, (1 - half) * 2 + 1 - core))
    pl.semaphore_wait(barrier, chips + 1)


def await_bytes(ref, sem):
    pltpu.make_async_copy(ref, ref, sem).wait()


def swap_copies(src, dst, send, recv, start):
    light, half, core, _ = place()
    rows = src.shape[1]
    halo = dst.shape[0] - 2 * rows

    def go(source, target, to_half, to_core, slot, number):
        here = jnp.logical_and(to_half == half, to_core == core)

        @pl.when(here)
        def _():
            if start:
                pltpu.make_async_copy(source, target, recv.at[slot]).start()

        @pl.when(jnp.logical_not(here))
        def _():
            copy = pltpu.make_async_remote_copy(
                src_ref=source,
                dst_ref=target,
                send_sem=send.at[number],
                recv_sem=recv.at[slot],
                device_id=(light, to_half * 2 + to_core),
                device_id_type=MESH,
            )
            if start:
                copy.start()
            else:
                copy.wait_send()

    for to_half in range(2):
        for own in range(2):

            @pl.when(core == own)
            def _():
                go(
                    src.at[to_half],
                    dst.at[pl.ds(own * rows + halo * half, rows)],
                    to_half,
                    half,
                    own,
                    to_half,
                )

        @pl.when(jnp.logical_and(half == 1, core == 0))
        def _():
            go(
                src.at[to_half, pl.ds(0, halo)],
                dst.at[pl.ds(2 * rows, halo)],
                to_half,
                0,
                2,
                2 + to_half,
            )

        @pl.when(jnp.logical_and(half == 0, core == 1))
        def _():
            go(
                src.at[to_half, pl.ds(rows - halo, halo)],
                dst.at[pl.ds(0, halo)],
                to_half,
                1,
                2,
                2 + to_half,
            )


def swap_arrivals(src, dst, recv):
    rows = src.shape[1]
    halo = dst.shape[0] - 2 * rows
    for slot, count in ((0, rows), (1, rows), (2, halo)):
        await_bytes(dst.at[pl.ds(0, count)], recv.at[slot])


def forward_kernel(
    scale,
    lights,
    codes_ref,
    hyper_ref,
    feat_ref,
    up_ref,
    blocks_ref,
    codes_out,
    feat_out,
    up_out,
    hyper,
    codes,
    wide,
    ready,
    hyper_sem,
    code_send,
    code_recv,
    own_sem,
    block_send,
    block_recv,
    pass_send,
    pass_recv,
    feat_send,
    feat_recv,
    up_send,
    up_recv,
):
    light, half, core, me = place()
    chips = 2 * lights
    groups = chips // GROUP
    load = pltpu.make_async_copy(hyper_ref, hyper, hyper_sem)
    load.start()
    greet()

    codes[pl.ds(pl.multiple_of(light * 8, 8), 8), :] = codes_ref[...]

    def send_codes(step, _):
        other = lax.rem(light + step, lights)
        pltpu.make_async_remote_copy(
            src_ref=codes_ref,
            dst_ref=codes.at[pl.ds(pl.multiple_of(light * 8, 8), 8)],
            send_sem=code_send,
            recv_sem=code_recv,
            device_id=(other, half * 2 + core),
            device_id_type=MESH,
        ).start()
        return 0

    lax.fori_loop(1, lights, send_codes, 0)
    swap_copies(feat_ref, feat_out, feat_send, feat_recv, True)
    swap_copies(up_ref, up_out, up_send, up_recv, True)
    arrived = codes.at[pl.ds(0, 8 * (lights - 1))]
    await_bytes(arrived, code_recv)
    parts = [codes[pl.ds(k, chips, stride=4), :] for k in range(4)]
    table = jnp.concatenate(parts, axis=1).astype(jnp.bfloat16)
    codes_out[...] = table
    load.wait()
    rows = hyper.shape[1] // (2 * LANES)
    for row in range(rows):
        product = scale * jnp.dot(
            table,
            hyper[:, row * 2 * LANES : (row + 1) * 2 * LANES],
            preferred_element_type=jnp.float32,
        )
        wide[pl.ds(row, chips, stride=40), :] = product[:, :LANES]
        wide[pl.ds(rows + row, chips, stride=40), :] = product[:, LANES:]

    def narrow(chip):
        ready[chip] = wide[pl.ds(pl.multiple_of(chip * 40, 8), 2 * rows), :].astype(jnp.bfloat16)

    narrow(me)
    keep = pltpu.make_async_copy(ready.at[me], blocks_ref.at[core, me], own_sem)
    keep.start()
    my_group, my_slot = me // GROUP, me % GROUP

    def send_block(step, _):
        group = lax.rem(my_group + step // GROUP, groups)
        slot = lax.rem(my_slot + step % GROUP, GROUP)
        other = group * GROUP + slot
        narrow(other)
        pltpu.make_async_remote_copy(
            src_ref=ready.at[other],
            dst_ref=blocks_ref.at[core, me],
            send_sem=block_send,
            recv_sem=block_recv.at[my_group],
            device_id=peer(other, core),
            device_id_type=MESH,
        ).start()
        return 0

    lax.fori_loop(1, chips, send_block, 0)

    def to_sibling(group):
        span = blocks_ref.at[core, pl.ds(group * GROUP, GROUP)]
        return pltpu.make_async_remote_copy(
            src_ref=span,
            dst_ref=span,
            send_sem=pass_send.at[group],
            recv_sem=pass_recv.at[group],
            device_id=(light, half * 2 + 1 - core),
            device_id_type=MESH,
        )

    keep.wait()
    await_bytes(blocks_ref.at[core, pl.ds(0, GROUP - 1)], block_recv.at[my_group])
    to_sibling(my_group).start()

    def pass_on(step, _):
        group = lax.rem(my_group + groups - step, groups)
        await_bytes(blocks_ref.at[core, pl.ds(0, GROUP)], block_recv.at[group])
        to_sibling(group).start()
        return 0

    lax.fori_loop(1, groups, pass_on, 0)

    def finish(group, _):
        to_sibling(group).wait()
        return 0

    lax.fori_loop(0, groups, finish, 0)
    await_bytes(ready.at[pl.ds(0, chips - 1)], block_send)
    await_bytes(arrived, code_send)
    swap_copies(feat_ref, feat_out, feat_send, feat_recv, False)
    swap_copies(up_ref, up_out, up_send, up_recv, False)
    swap_arrivals(feat_ref, feat_out, feat_recv)
    swap_arrivals(up_ref, up_out, up_recv)


def forward_exchange(scale, lights, codes, hyper_weight, features, upstream):
    chips = 2 * lights
    depth, own_len = hyper_weight.shape
    block_rows = own_len // LANES
    _, rows, columns, channels = features.shape
    dma = pltpu.SemaphoreType.DMA
    anywhere = pl.BlockSpec(memory_space=pl.ANY)
    vmem = pl.BlockSpec(memory_space=pltpu.VMEM)
    return pl.pallas_call(
        functools.partial(forward_kernel, scale, lights),
        out_shape=(
            jax.ShapeDtypeStruct((2, chips, block_rows, LANES), jnp.bfloat16),
            jax.ShapeDtypeStruct((chips, depth), jnp.bfloat16),
            jax.ShapeDtypeStruct((2 * rows + HALO, columns, channels), jnp.bfloat16),
            jax.ShapeDtypeStruct((2 * rows + HALO, columns, channels), jnp.bfloat16),
        ),
        in_specs=[vmem, anywhere, anywhere, anywhere],
        out_specs=(anywhere, vmem, anywhere, anywhere),
        scratch_shapes=[
            pltpu.VMEM((depth, own_len), jnp.bfloat16),
            pltpu.VMEM((8 * lights, LANES), jnp.float32),
            pltpu.VMEM((chips * 40, LANES), jnp.float32),
            pltpu.VMEM((chips, block_rows, LANES), jnp.bfloat16),
            dma,
            dma,
            dma,
            dma,
            dma,
            dma((chips // GROUP,)),
            dma((chips // GROUP,)),
            dma((chips // GROUP,)),
            dma((4,)),
            dma((3,)),
            dma((4,)),
            dma((3,)),
        ],
        compiler_params=pltpu.CompilerParams(
            has_side_effects=True, collective_id=0, vmem_limit_bytes=VMEM
        ),
    )(codes, hyper_weight, features, upstream)


def give_back(src, dst, send, recv, start):
    light, half, core, _ = place()
    rows = dst.shape[1]
    for piece in range(2):
        here = jnp.logical_and(core == half, piece == core)
        source = src.at[pl.ds(piece * rows, rows)]
        for own in range(2):

            @pl.when(jnp.logical_and(here, half == own))
            def _():
                if start:
                    pltpu.make_async_copy(source, dst.at[own], recv.at[own]).start()

            @pl.when(jnp.logical_and(jnp.logical_not(here), half == own))
            def _():
                copy = pltpu.make_async_remote_copy(
                    src_ref=source,
                    dst_ref=dst.at[own],
                    send_sem=send.at[piece],
                    recv_sem=recv.at[own],
                    device_id=(light, core * 2 + piece),
                    device_id_type=MESH,
                )
                if start:
                    copy.start()
                else:
                    copy.wait_send()


def backward_kernel(
    lights,
    parts_ref,
    relit_ref,
    grad_ref,
    sums_ref,
    relit_out,
    grad_out,
    mine,
    theirs,
    ready,
    mine_sem,
    core_send,
    core_recv,
    own_sem,
    block_send,
    block_recv,
    relit_send,
    relit_recv,
    grad_send,
    grad_recv,
):
    light, half, core, me = place()
    chips = 2 * lights
    groups = chips // GROUP
    my_group, my_slot = me // GROUP, me % GROUP
    load = pltpu.make_async_copy(parts_ref.at[core], mine, mine_sem)
    load.start()
    greet()

    def to_sibling(group):
        return pltpu.make_async_remote_copy(
            src_ref=parts_ref.at[1 - core, pl.ds(group * GROUP, GROUP)],
            dst_ref=theirs.at[pl.ds(group * GROUP, GROUP)],
            send_sem=core_send.at[group],
            recv_sem=core_recv.at[group],
            device_id=(light, half * 2 + 1 - core),
            device_id_type=MESH,
        )

    def start_group(step, _):
        to_sibling(lax.rem(my_group + step, groups)).start()
        return 0

    lax.fori_loop(0, groups, start_group, 0)
    give_back(relit_ref, relit_out, relit_send, relit_recv, True)
    give_back(grad_ref, grad_out, grad_send, grad_recv, True)
    load.wait()

    def send_block(other):
        pltpu.make_async_remote_copy(
            src_ref=ready.at[other],
            dst_ref=sums_ref.at[me],
            send_sem=block_send,
            recv_sem=block_recv,
            device_id=peer(other, core),
            device_id_type=MESH,
        ).start()

    def do_group(step, _):
        group = lax.rem(my_group + step, groups)
        to_sibling(group).wait_recv()

        def do_block(slot, _):
            other = group * GROUP + lax.rem(my_slot + slot, GROUP)
            ready[other] = (
                mine[other].astype(jnp.float32) + theirs[other].astype(jnp.float32)
            ).astype(jnp.bfloat16)

            @pl.when(other != me)
            def _():
                send_block(other)

            return 0

        return lax.fori_loop(0, GROUP, do_block, 0)

    lax.fori_loop(0, groups, do_group, 0)
    keep = pltpu.make_async_copy(ready.at[me], sums_ref.at[me], own_sem)
    keep.start()
    keep.wait()

    def finish(group, _):
        to_sibling(group).wait_send()
        return 0

    lax.fori_loop(0, groups, finish, 0)
    give_back(relit_ref, relit_out, relit_send, relit_recv, False)
    give_back(grad_ref, grad_out, grad_send, grad_recv, False)
    for own in range(2):
        await_bytes(relit_out.at[own], relit_recv.at[own])
        await_bytes(grad_out.at[own], grad_recv.at[own])
    await_bytes(ready.at[pl.ds(0, chips - 1)], block_send)
    await_bytes(sums_ref.at[pl.ds(0, chips - 1)], block_recv)


def backward_exchange(lights, parts, relit, feature_grad):
    _, chips, block_rows, lanes = parts.shape
    rows, columns, channels = relit.shape
    dma = pltpu.SemaphoreType.DMA
    anywhere = pl.BlockSpec(memory_space=pl.ANY)
    image = jax.ShapeDtypeStruct((2, rows // 2, columns, channels), jnp.bfloat16)
    return pl.pallas_call(
        functools.partial(backward_kernel, lights),
        out_shape=(
            jax.ShapeDtypeStruct((chips, block_rows, lanes), jnp.bfloat16),
            image,
            image,
        ),
        in_specs=[anywhere] * 3,
        out_specs=(anywhere,) * 3,
        scratch_shapes=[
            pltpu.VMEM((chips, block_rows, lanes), jnp.bfloat16),
            pltpu.VMEM((chips, block_rows, lanes), jnp.bfloat16),
            pltpu.VMEM((chips, block_rows, lanes), jnp.bfloat16),
            dma,
            dma((chips // GROUP,)),
            dma((chips // GROUP,)),
            dma,
            dma,
            dma,
            dma((2,)),
            dma((2,)),
            dma((2,)),
            dma((2,)),
        ],
        compiler_params=pltpu.CompilerParams(
            has_side_effects=True, collective_id=1, vmem_limit_bytes=VMEM
        ),
    )(parts, relit, feature_grad)


def local_kernel(
    columns,
    blocks_ref,
    feat_ref,
    up_ref,
    relit_ref,
    grad_ref,
    parts_ref,
    wide,
    line,
    kernels,
    feats,
    hidden,
    grads,
    slope,
    total,
):
    core = lax.axis_index("tex") % 2
    frame, channels = feat_ref.shape
    own = relit_ref.shape[0]
    rows = frame // columns
    chips, block_rows = blocks_ref.shape[1], blocks_ref.shape[2]
    taps = block_rows // 2
    depth = 9 * channels
    chunk = total.shape[0]
    chunk_rows = chunk // columns
    first_own = pl.multiple_of(core * (frame - own), 16)

    def gather(owner, _):
        line[...] = blocks_ref[lax.rem(owner, 2), lax.div(owner, 2)].astype(jnp.float32)

        def move(side, _):
            wide[side, pl.ds(owner * taps, taps), :] = line[pl.ds(side * taps, taps), :]
            return 0

        return lax.fori_loop(0, 2, move, 0)

    lax.fori_loop(0, 2 * chips, gather, 0)

    def narrow(step, _):
        span = pl.ds(pl.multiple_of(step * channels, channels), channels)
        kernels[span, :LANES] = wide[0, span, :].astype(jnp.bfloat16)
        kernels[span, LANES:] = wide[1, span, :].astype(jnp.bfloat16)
        return 0

    lax.fori_loop(0, 2 * depth // channels, narrow, 0)

    for image in (feats, hidden, grads):
        edge = jnp.zeros((columns, image.shape[1]), image.dtype)
        image[:columns] = edge
        image[frame + columns :] = edge

    def spread(image, row, values):
        span = pl.ds(pl.multiple_of((row + 1) * columns, 16), columns)
        none = jnp.zeros((1, channels), jnp.float32)
        before = jnp.concatenate([none, values[:-1]], axis=0)
        after = jnp.concatenate([values[1:], none], axis=0)
        image[span, :channels] = before.astype(image.dtype)
        image[span, channels : 2 * channels] = values.astype(image.dtype)
        image[span, 2 * channels :] = after.astype(image.dtype)

    def row_span(row):
        return pl.ds(pl.multiple_of(row * columns, 16), columns)

    def place_feats(row, _):
        spread(feats, row, feat_ref[row_span(row), :].astype(jnp.float32))
        return 0

    lax.fori_loop(0, rows, place_feats, 0)

    def conv(image, base, start):
        out = None
        for tap in range(3):
            span = pl.ds(pl.multiple_of(start + tap * columns, 16), chunk)
            piece = jnp.dot(
                image[span, :],
                kernels[base + tap * 3 * channels : base + (tap + 1) * 3 * channels, :],
                preferred_element_type=jnp.float32,
            )
            out = piece if out is None else out + piece
        total[...] = out

    def conv_back(image, base, start):
        out = None
        for row_tap in range(3):
            span = pl.ds(pl.multiple_of(start + (2 - row_tap) * columns, 16), chunk)
            for col_tap in range(3):
                at = base + (row_tap * 3 + col_tap) * channels
                piece = lax.dot_general(
                    image[span, (2 - col_tap) * channels : (3 - col_tap) * channels],
                    kernels[at : at + channels, :],
                    (((1,), (1,)), ((), ())),
                    preferred_element_type=jnp.float32,
                )
                out = piece if out is None else out + piece
        total[...] = out

    def each_chunk(compute, finish_row):
        def do_chunk(step, _):
            compute(step * chunk)

            def do_row(row, _):
                finish_row(step * chunk_rows + row, total[row_span(row), :])
                return 0

            return lax.fori_loop(0, chunk_rows, do_row, 0)

        lax.fori_loop(0, frame // chunk, do_chunk, 0)

    def store_own(ref, row, values):
        local = row - core * (frame - own) // columns

        @pl.when(jnp.logical_and(local >= 0, local < own // columns))
        def _():
            ref[row_span(local), :] = values.astype(ref.dtype)

    def end_first(row, pre):
        sig = jax.nn.sigmoid(pre)
        slope[row_span(row), :] = sig * (1.0 + pre * (1.0 - sig))
        spread(hidden, row, pre * sig)

    def end_second(row, pre):
        sig = jax.nn.sigmoid(pre)
        store_own(relit_ref, row, pre * sig)
        up = up_ref[row_span(row), :].astype(jnp.float32)
        spread(grads, row, up * (sig * (1.0 + pre * (1.0 - sig))))

    def kernel_grad(image, base):
        upstream = grads[pl.ds(first_own + columns, own), channels : 2 * channels].T

        def do_tap(tap, _):
            span = pl.ds(pl.multiple_of(first_own + tap * columns, 16), own)
            for col_tap in range(3):
                piece = jnp.dot(
                    upstream,
                    image[span, col_tap * channels : (col_tap + 1) * channels],
                    preferred_element_type=jnp.float32,
                )
                at = pl.multiple_of(base + (tap * 3 + col_tap) * channels, channels)
                wide[0, pl.ds(at, channels), :] = piece[:LANES].T
                wide[1, pl.ds(at, channels), :] = piece[LANES:].T
            return 0

        lax.fori_loop(0, 3, do_tap, 0)

    def end_grad(row, back):
        slope[row_span(row), :] = slope[row_span(row), :] * back

    each_chunk(lambda start: conv(feats, 0, start), end_first)
    each_chunk(lambda start: conv(hidden, depth, start), end_second)
    each_chunk(lambda start: conv_back(grads, depth, start), end_grad)
    kernel_grad(hidden, depth)

    def place_grad(row, _):
        spread(grads, row, slope[row_span(row), :])
        return 0

    lax.fori_loop(0, rows, place_grad, 0)
    kernel_grad(feats, 0)
    each_chunk(
        lambda start: conv_back(grads, 0, start),
        lambda row, back: store_own(grad_ref, row, back),
    )

    def scatter(owner, _):
        def move(side, _):
            line[pl.ds(side * taps, taps), :] = wide[side, pl.ds(owner * taps, taps), :]
            return 0

        lax.fori_loop(0, 2, move, 0)
        parts_ref[lax.rem(owner, 2), lax.div(owner, 2)] = line[...].astype(parts_ref.dtype)
        return 0

    lax.fori_loop(0, 2 * chips, scatter, 0)


def local_work(blocks, feats, upstream, columns):
    frame, channels = feats.shape
    own = frame - HALO * columns
    depth = 9 * channels
    shifted = pltpu.VMEM((frame + 2 * columns, 3 * channels), jnp.bfloat16)
    image = jax.ShapeDtypeStruct((own, channels), jnp.bfloat16)
    return pl.pallas_call(
        functools.partial(local_kernel, columns),
        out_shape=(image, image, jax.ShapeDtypeStruct(blocks.shape, jnp.bfloat16)),
        in_specs=[pl.BlockSpec(memory_space=pltpu.VMEM)] * 3,
        out_specs=(pl.BlockSpec(memory_space=pltpu.VMEM),) * 3,
        scratch_shapes=[
            pltpu.VMEM((2, 2 * depth, LANES), jnp.float32),
            pltpu.VMEM(blocks.shape[2:], jnp.float32),
            pltpu.VMEM((2 * depth, channels), jnp.bfloat16),
            shifted,
            shifted,
            shifted,
            pltpu.VMEM((frame, channels), jnp.float32),
            pltpu.VMEM((9 * columns, channels), jnp.float32),
        ],
        compiler_params=pltpu.CompilerParams(vmem_limit_bytes=VMEM),
    )(blocks, feats, upstream)


def shards(light_ids, tile_offsets, light_table, hyper_weight, features, upstream_grad):
    rows_dev, channels = features.shape[1], features.shape[3]
    scale = 1.0 / math.sqrt(9 * channels)
    lights = lax.axis_size("light")
    own_codes = light_codes(light_ids, tile_offsets, light_table)
    blocks, codes, feats, upstream = forward_exchange(
        scale,
        lights,
        own_codes.astype(jnp.float32).reshape(8, LANES),
        hyper_weight,
        features,
        upstream_grad,
    )
    chips = 2 * lights
    taps = hyper_weight.shape[1] // channels
    columns = feats.shape[1]
    relit, feature_grad, parts = local_work(
        blocks, feats.reshape(-1, channels), upstream.reshape(-1, channels), columns
    )
    relit = relit.reshape(2 * rows_dev, columns, channels)
    feature_grad = feature_grad.reshape(2 * rows_dev, columns, channels)
    sums, relit, feature_grad = backward_exchange(lights, parts, relit, feature_grad)
    summed = (
        sums.reshape(chips, 2, taps, LANES).transpose(0, 2, 1, 3).reshape(chips, taps * channels)
    )
    hyper_grad = (
        scale * jnp.einsum("lz,ls->zs", codes, summed, preferred_element_type=jnp.float32)
    ).astype(jnp.bfloat16)
    return (relit, feature_grad, hyper_grad)


def solution(mesh):
    in_specs = (
        P("light"),
        P("light"),
        P(),
        P(None, ("light", "tex")),
        P("light", "tex", None, None),
        P("light", "tex", None, None),
    )
    out_specs = (
        P("light", "tex", None, None),
        P("light", "tex", None, None),
        P(None, ("light", "tex")),
    )
    return jax.shard_map(shards, mesh=mesh, in_specs=in_specs, out_specs=out_specs, check_vma=False)
```

```python
import functools
import math

import jax
import jax.numpy as jnp
from jax import lax
from jax.experimental import pallas as pl
from jax.experimental.pallas import tpu as pltpu
from jax.sharding import PartitionSpec as P

MESH = pl.DeviceIdType.MESH
LANES = 128
GROUP = 16
HALO = 4
VMEM = 60 * 1024 * 1024


def light_codes(light_ids, tile_offsets, light_table):
    halfway = light_table.shape[1] // 2
    onehot = (
        light_ids[:, None] == jnp.arange(light_table.shape[0], dtype=jnp.int32)[None, :]
    ).astype(jnp.bfloat16)
    looked = jnp.dot(onehot, light_table, preferred_element_type=jnp.float32)
    rates = jnp.exp(-math.log(1000.0) * jnp.arange(halfway, dtype=jnp.float32) / halfway)
    angles = tile_offsets.astype(jnp.float32)[:, None] * rates[None, :]
    summed = looked + jnp.concatenate([jnp.sin(angles), jnp.cos(angles)], axis=1)
    return (summed * lax.rsqrt(jnp.mean(summed * summed, axis=1, keepdims=True) + 1e-06)).astype(
        jnp.bfloat16
    )


def place():
    light, tex = lax.axis_index("light"), lax.axis_index("tex")
    half, core = tex // 2, tex % 2
    return light, half, core, light * 2 + half


def peer(chip, core):
    return (chip // 2, (chip % 2) * 2 + core)


def greet():
    light, half, core, me = place()
    chips = 2 * lax.axis_size("light")
    barrier = pltpu.get_barrier_semaphore()

    def signal(target):
        pl.semaphore_signal(barrier, inc=1, device_id=target, device_id_type=MESH)

    def signal_chip(step, _):
        signal(peer(lax.rem(me + step, chips), core))
        return 0

    lax.fori_loop(1, chips, signal_chip, 0)
    signal((light, half * 2 + 1 - core))
    signal((light, (1 - half) * 2 + 1 - core))
    pl.semaphore_wait(barrier, chips + 1)


def await_bytes(ref, sem):
    pltpu.make_async_copy(ref, ref, sem).wait()


def swap_copies(src, dst, send, recv, start):
    light, half, core, _ = place()
    rows = src.shape[1]
    halo = dst.shape[0] - 2 * rows

    def go(source, target, to_half, to_core, slot, number):
        here = jnp.logical_and(to_half == half, to_core == core)

        @pl.when(here)
        def _():
            if start:
                pltpu.make_async_copy(source, target, recv.at[slot]).start()

        @pl.when(jnp.logical_not(here))
        def _():
            copy = pltpu.make_async_remote_copy(
                src_ref=source,
                dst_ref=target,
                send_sem=send.at[number],
                recv_sem=recv.at[slot],
                device_id=(light, to_half * 2 + to_core),
                device_id_type=MESH,
            )
            if start:
                copy.start()
            else:
                copy.wait_send()

    for to_half in range(2):
        for own in range(2):

            @pl.when(core == own)
            def _():
                go(
                    src.at[to_half],
                    dst.at[pl.ds(own * rows + halo * half, rows)],
                    to_half,
                    half,
                    own,
                    to_half,
                )

        @pl.when(jnp.logical_and(half == 1, core == 0))
        def _():
            go(
                src.at[to_half, pl.ds(0, halo)],
                dst.at[pl.ds(2 * rows, halo)],
                to_half,
                0,
                2,
                2 + to_half,
            )

        @pl.when(jnp.logical_and(half == 0, core == 1))
        def _():
            go(
                src.at[to_half, pl.ds(rows - halo, halo)],
                dst.at[pl.ds(0, halo)],
                to_half,
                1,
                2,
                2 + to_half,
            )


def swap_arrivals(src, dst, recv):
    rows = src.shape[1]
    halo = dst.shape[0] - 2 * rows
    for slot, count in ((0, rows), (1, rows), (2, halo)):
        await_bytes(dst.at[pl.ds(0, count)], recv.at[slot])


def give_back(src, dst, send, recv, start):
    light, half, core, _ = place()
    rows = dst.shape[1]
    for piece in range(2):
        here = jnp.logical_and(core == half, piece == core)
        source = src.at[pl.ds(piece * rows, rows)]
        for own in range(2):

            @pl.when(jnp.logical_and(here, half == own))
            def _():
                if start:
                    pltpu.make_async_copy(source, dst.at[own], recv.at[own]).start()

            @pl.when(jnp.logical_and(jnp.logical_not(here), half == own))
            def _():
                copy = pltpu.make_async_remote_copy(
                    src_ref=source,
                    dst_ref=dst.at[own],
                    send_sem=send.at[piece],
                    recv_sem=recv.at[own],
                    device_id=(light, core * 2 + piece),
                    device_id_type=MESH,
                )
                if start:
                    copy.start()
                else:
                    copy.wait_send()


def whole_kernel(
    scale,
    lights,
    codes_ref,
    hyper_ref,
    feat_ref,
    up_ref,
    codes_out,
    sums_ref,
    relit_out,
    grad_out,
    hyper,
    codes,
    table,
    ready,
    blocks,
    wide,
    line,
    kernels,
    feat,
    up,
    feats,
    hidden,
    grads,
    slope,
    total,
    relit,
    grad,
    parts,
    theirs,
    added,
    hyper_sem,
    code_send,
    code_recv,
    own_sem,
    block_send,
    block_recv,
    pass_send,
    pass_recv,
    feat_send,
    feat_recv,
    up_send,
    up_recv,
    core_send,
    core_recv,
    sum_send,
    sum_recv,
    relit_send,
    relit_recv,
    grad_send,
    grad_recv,
):
    light, half, core, me = place()
    chips = 2 * lights
    groups = chips // GROUP
    my_group, my_slot = me // GROUP, me % GROUP
    sibling = (light, half * 2 + 1 - core)
    block_rows = ready.shape[1]
    taps = block_rows // 2
    rows, columns, channels = feat.shape
    own_rows = relit.shape[0]
    frame, own = rows * columns, own_rows * columns
    depth = 9 * channels
    chunk = total.shape[0]
    chunk_rows = chunk // columns
    inner = rows - own_rows
    first_own = pl.multiple_of(core * inner * columns, 16)

    load = pltpu.make_async_copy(hyper_ref, hyper, hyper_sem)
    load.start()
    greet()

    mine = pl.ds(pl.multiple_of(light * 8, 8), 8)
    codes[mine, :] = codes_ref[...]

    def send_codes(step, _):
        pltpu.make_async_remote_copy(
            src_ref=codes_ref,
            dst_ref=codes.at[mine],
            send_sem=code_send,
            recv_sem=code_recv,
            device_id=(lax.rem(light + step, lights), half * 2 + core),
            device_id_type=MESH,
        ).start()
        return 0

    lax.fori_loop(1, lights, send_codes, 0)
    swap_copies(feat_ref, feat, feat_send, feat_recv, True)
    swap_copies(up_ref, up, up_send, up_recv, True)
    for image in (feats, hidden, grads):
        edge = jnp.zeros((columns, image.shape[1]), image.dtype)
        image[:columns] = edge
        image[frame + columns :] = edge
    arrived = codes.at[pl.ds(0, 8 * (lights - 1))]
    await_bytes(arrived, code_recv)
    all_codes = jnp.concatenate(
        [codes[pl.ds(k, chips, stride=4), :] for k in range(4)], axis=1
    ).astype(jnp.bfloat16)
    codes_out[...] = all_codes
    load.wait()

    for row in range(taps):
        product = scale * jnp.dot(
            all_codes,
            hyper[:, row * 2 * LANES : (row + 1) * 2 * LANES],
            preferred_element_type=jnp.float32,
        )
        table[pl.ds(row, chips, stride=40), :] = product[:, :LANES]
        table[pl.ds(taps + row, chips, stride=40), :] = product[:, LANES:]

    def narrow(chip):
        ready[chip] = table[pl.ds(pl.multiple_of(chip * 40, 8), block_rows), :].astype(
            jnp.bfloat16
        )

    narrow(me)
    keep = pltpu.make_async_copy(ready.at[me], blocks.at[core, me], own_sem)
    keep.start()

    def send_block(step, _):
        group = lax.rem(my_group + step // GROUP, groups)
        other = group * GROUP + lax.rem(my_slot + step % GROUP, GROUP)
        narrow(other)
        pltpu.make_async_remote_copy(
            src_ref=ready.at[other],
            dst_ref=blocks.at[core, me],
            send_sem=block_send,
            recv_sem=block_recv.at[my_group],
            device_id=peer(other, core),
            device_id_type=MESH,
        ).start()
        return 0

    lax.fori_loop(1, chips, send_block, 0)

    def row_span(row):
        return pl.ds(pl.multiple_of(row * columns, 16), columns)

    def spread(image, row, values):
        span = row_span(row + 1)
        none = jnp.zeros((1, channels), jnp.float32)
        before = jnp.concatenate([none, values[:-1]], axis=0)
        after = jnp.concatenate([values[1:], none], axis=0)
        image[span, :channels] = before.astype(image.dtype)
        image[span, channels : 2 * channels] = values.astype(image.dtype)
        image[span, 2 * channels :] = after.astype(image.dtype)

    swap_arrivals(feat_ref, feat, feat_recv)
    swap_arrivals(up_ref, up, up_recv)

    def place_feats(row, _):
        spread(feats, row, feat[row].astype(jnp.float32))
        return 0

    lax.fori_loop(0, rows, place_feats, 0)

    def to_sibling(group):
        span = blocks.at[core, pl.ds(group * GROUP, GROUP)]
        return pltpu.make_async_remote_copy(
            src_ref=span,
            dst_ref=span,
            send_sem=pass_send.at[group],
            recv_sem=pass_recv.at[group],
            device_id=sibling,
            device_id_type=MESH,
        )

    def gather(group, from_core):
        def block(slot, _):
            chip = group * GROUP + slot
            line[...] = blocks[from_core, chip].astype(jnp.float32)

            def move(side, _):
                wide[side, pl.ds((2 * chip + from_core) * taps, taps), :] = line[
                    pl.ds(side * taps, taps), :
                ]
                return 0

            return lax.fori_loop(0, 2, move, 0)

        lax.fori_loop(0, GROUP, block, 0)

    def end_group(group):
        to_sibling(group).wait_recv()
        gather(group, 1 - core)
        count = 2 * GROUP * taps
        span = pl.ds(pl.multiple_of(group * count, 16), count)
        kernels[span, :LANES] = wide[0, span, :].astype(jnp.bfloat16)
        kernels[span, LANES:] = wide[1, span, :].astype(jnp.bfloat16)

    keep.wait()
    await_bytes(blocks.at[core, pl.ds(0, GROUP - 1)], block_recv.at[my_group])
    to_sibling(my_group).start()
    gather(my_group, core)

    def take_group(step, _):
        group = lax.rem(my_group + groups - step, groups)
        await_bytes(blocks.at[core, pl.ds(0, GROUP)], block_recv.at[group])
        to_sibling(group).start()
        gather(group, core)
        end_group(lax.rem(group + 1, groups))
        return 0

    lax.fori_loop(1, groups, take_group, 0)
    end_group(lax.rem(my_group + 1, groups))

    def conv(image, base, start):
        out = None
        for tap in range(3):
            span = pl.ds(pl.multiple_of(start + tap * columns, 16), chunk)
            piece = jnp.dot(
                image[span, :],
                kernels[base + tap * 3 * channels : base + (tap + 1) * 3 * channels, :],
                preferred_element_type=jnp.float32,
            )
            out = piece if out is None else out + piece
        total[...] = out

    def conv_back(image, base, start):
        out = None
        for row_tap in range(3):
            span = pl.ds(pl.multiple_of(start + (2 - row_tap) * columns, 16), chunk)
            for col_tap in range(3):
                at = base + (row_tap * 3 + col_tap) * channels
                piece = lax.dot_general(
                    image[span, (2 - col_tap) * channels : (3 - col_tap) * channels],
                    kernels[at : at + channels, :],
                    (((1,), (1,)), ((), ())),
                    preferred_element_type=jnp.float32,
                )
                out = piece if out is None else out + piece
        total[...] = out

    def each_chunk(compute, finish_row):
        def do_chunk(step, _):
            compute(step * chunk)

            def do_row(row, _):
                finish_row(step * chunk_rows + row, total[row_span(row), :])
                return 0

            return lax.fori_loop(0, chunk_rows, do_row, 0)

        lax.fori_loop(0, frame // chunk, do_chunk, 0)

    def store_own(ref, row, values):
        local = row - core * inner

        @pl.when(jnp.logical_and(local >= 0, local < own_rows))
        def _():
            ref[local] = values.astype(ref.dtype)

    def end_first(row, pre):
        sig = jax.nn.sigmoid(pre)
        slope[row_span(row), :] = sig * (1.0 + pre * (1.0 - sig))
        spread(hidden, row, pre * sig)

    def end_second(row, pre):
        sig = jax.nn.sigmoid(pre)
        store_own(relit, row, pre * sig)
        spread(grads, row, up[row].astype(jnp.float32) * (sig * (1.0 + pre * (1.0 - sig))))

    def kernel_grad(image, base):
        upstream = grads[pl.ds(first_own + columns, own), channels : 2 * channels].T

        def do_tap(tap, _):
            span = pl.ds(pl.multiple_of(first_own + tap * columns, 16), own)
            for col_tap in range(3):
                piece = jnp.dot(
                    upstream,
                    image[span, col_tap * channels : (col_tap + 1) * channels],
                    preferred_element_type=jnp.float32,
                )
                at = pl.multiple_of(base + (tap * 3 + col_tap) * channels, channels)
                wide[0, pl.ds(at, channels), :] = piece[:LANES].T
                wide[1, pl.ds(at, channels), :] = piece[LANES:].T
            return 0

        lax.fori_loop(0, 3, do_tap, 0)

    def end_grad(row, back):
        slope[row_span(row), :] = slope[row_span(row), :] * back

    def part_copy(group):
        return pltpu.make_async_remote_copy(
            src_ref=parts.at[pl.ds(group * GROUP, GROUP)],
            dst_ref=theirs.at[pl.ds(group * GROUP, GROUP)],
            send_sem=core_send.at[group],
            recv_sem=core_recv.at[group],
            device_id=sibling,
            device_id_type=MESH,
        )

    def pick(owner):
        def move(side, _):
            line[pl.ds(side * taps, taps), :] = wide[side, pl.ds(owner * taps, taps), :]
            return 0

        lax.fori_loop(0, 2, move, 0)
        return line[...]

    def send_grad(first):
        some = groups // 2

        def group_at(step):
            return first + lax.rem(my_group + step, some)

        def share(step):
            group = group_at(step)

            def block(slot, _):
                chip = group * GROUP + slot
                parts[chip] = pick(2 * chip + 1 - core).astype(parts.dtype)
                return 0

            lax.fori_loop(0, GROUP, block, 0)
            part_copy(group).start()

        def add(step):
            group = group_at(step)
            part_copy(group).wait_recv()

            def block(slot, _):
                other = group * GROUP + lax.rem(my_slot + slot, GROUP)
                added[other] = (
                    pick(2 * other + core) + theirs[other].astype(jnp.float32)
                ).astype(added.dtype)

                @pl.when(other != me)
                def _():
                    pltpu.make_async_remote_copy(
                        src_ref=added.at[other],
                        dst_ref=sums_ref.at[me],
                        send_sem=sum_send,
                        recv_sem=sum_recv,
                        device_id=peer(other, core),
                        device_id_type=MESH,
                    ).start()

                return 0

            lax.fori_loop(0, GROUP, block, 0)

        share(0)

        def both(step, _):
            share(step)
            add(step - 1)
            return 0

        lax.fori_loop(1, some, both, 0)
        add(some - 1)

    each_chunk(lambda start: conv(feats, 0, start), end_first)
    each_chunk(lambda start: conv(hidden, depth, start), end_second)
    kernel_grad(hidden, depth)
    send_grad(groups // 2)
    give_back(relit, relit_out, relit_send, relit_recv, True)
    each_chunk(lambda start: conv_back(grads, depth, start), end_grad)

    def place_grad(row, _):
        spread(grads, row, slope[row_span(row), :])
        return 0

    lax.fori_loop(0, rows, place_grad, 0)
    kernel_grad(feats, 0)
    send_grad(0)
    each_chunk(
        lambda start: conv_back(grads, 0, start),
        lambda row, back: store_own(grad, row, back),
    )
    give_back(grad, grad_out, grad_send, grad_recv, True)
    last = pltpu.make_async_copy(added.at[me], sums_ref.at[me], own_sem)
    last.start()

    def finish(group, _):
        to_sibling(group).wait_send()
        part_copy(group).wait_send()
        return 0

    lax.fori_loop(0, groups, finish, 0)
    await_bytes(ready.at[pl.ds(0, chips - 1)], block_send)
    await_bytes(arrived, code_send)
    swap_copies(feat_ref, feat, feat_send, feat_recv, False)
    swap_copies(up_ref, up, up_send, up_recv, False)
    give_back(relit, relit_out, relit_send, relit_recv, False)
    give_back(grad, grad_out, grad_send, grad_recv, False)
    for slot in range(2):
        await_bytes(relit_out.at[slot], relit_recv.at[slot])
        await_bytes(grad_out.at[slot], grad_recv.at[slot])
    last.wait()
    await_bytes(added.at[pl.ds(0, chips - 1)], sum_send)
    await_bytes(sums_ref.at[pl.ds(0, chips - 1)], sum_recv)


def whole(scale, lights, codes, hyper_weight, features, upstream):
    chips = 2 * lights
    groups = chips // GROUP
    width, own_len = hyper_weight.shape
    block_rows = own_len // LANES
    _, rows_dev, columns, channels = features.shape
    depth = 9 * channels
    own_rows = 2 * rows_dev
    rows = own_rows + HALO
    frame = rows * columns
    dma = pltpu.SemaphoreType.DMA
    anywhere = pl.BlockSpec(memory_space=pl.ANY)
    vmem = pl.BlockSpec(memory_space=pltpu.VMEM)
    image = jax.ShapeDtypeStruct(features.shape, jnp.bfloat16)
    block = pltpu.VMEM((chips, block_rows, LANES), jnp.bfloat16)
    shifted = pltpu.VMEM((frame + 2 * columns, 3 * channels), jnp.bfloat16)
    return pl.pallas_call(
        functools.partial(whole_kernel, scale, lights),
        out_shape=(
            jax.ShapeDtypeStruct((chips, width), jnp.bfloat16),
            jax.ShapeDtypeStruct((chips, block_rows, LANES), jnp.bfloat16),
            image,
            image,
        ),
        in_specs=[vmem, anywhere, anywhere, anywhere],
        out_specs=(vmem, anywhere, anywhere, anywhere),
        scratch_shapes=[
            pltpu.VMEM((width, own_len), jnp.bfloat16),
            pltpu.VMEM((8 * lights, LANES), jnp.float32),
            pltpu.VMEM((chips * 40, LANES), jnp.float32),
            block,
            pltpu.VMEM((2, chips, block_rows, LANES), jnp.bfloat16),
            pltpu.VMEM((2, 2 * depth, LANES), jnp.float32),
            pltpu.VMEM((block_rows, LANES), jnp.float32),
            pltpu.VMEM((2 * depth, channels), jnp.bfloat16),
            pltpu.VMEM((rows, columns, channels), jnp.bfloat16),
            pltpu.VMEM((rows, columns, channels), jnp.bfloat16),
            shifted,
            shifted,
            shifted,
            pltpu.VMEM((frame, channels), jnp.float32),
            pltpu.VMEM((9 * columns, channels), jnp.float32),
            pltpu.VMEM((own_rows, columns, channels), jnp.bfloat16),
            pltpu.VMEM((own_rows, columns, channels), jnp.bfloat16),
            block,
            block,
            block,
            dma,
            dma,
            dma,
            dma,
            dma,
            dma((groups,)),
            dma((groups,)),
            dma((groups,)),
            dma((4,)),
            dma((3,)),
            dma((4,)),
            dma((3,)),
            dma((groups,)),
            dma((groups,)),
            dma,
            dma,
            dma((2,)),
            dma((2,)),
            dma((2,)),
            dma((2,)),
        ],
        compiler_params=pltpu.CompilerParams(
            has_side_effects=True, collective_id=0, vmem_limit_bytes=VMEM
        ),
    )(codes, hyper_weight, features, upstream)


def shards(light_ids, tile_offsets, light_table, hyper_weight, features, upstream_grad):
    channels = features.shape[3]
    scale = 1.0 / math.sqrt(9 * channels)
    lights = lax.axis_size("light")
    own_codes = light_codes(light_ids, tile_offsets, light_table)
    codes, sums, relit, feature_grad = whole(
        scale,
        lights,
        own_codes.astype(jnp.float32).reshape(8, LANES),
        hyper_weight,
        features,
        upstream_grad,
    )
    chips = 2 * lights
    taps = hyper_weight.shape[1] // channels
    summed = (
        sums.reshape(chips, 2, taps, LANES).transpose(0, 2, 1, 3).reshape(chips, taps * channels)
    )
    hyper_grad = (
        scale * jnp.einsum("lz,ls->zs", codes, summed, preferred_element_type=jnp.float32)
    ).astype(jnp.bfloat16)
    return (relit, feature_grad, hyper_grad)


def solution(mesh):
    in_specs = (
        P("light"),
        P("light"),
        P(),
        P(None, ("light", "tex")),
        P("light", "tex", None, None),
        P("light", "tex", None, None),
    )
    out_specs = (
        P("light", "tex", None, None),
        P("light", "tex", None, None),
        P(None, ("light", "tex")),
    )
    return jax.shard_map(shards, mesh=mesh, in_specs=in_specs, out_specs=out_specs, check_vma=False)
```

```python
import functools
import math

import jax
import jax.numpy as jnp
from jax import lax
from jax.experimental import pallas as pl
from jax.experimental.pallas import tpu as pltpu
from jax.sharding import PartitionSpec as P

MESH = pl.DeviceIdType.MESH
LANES = 128
GROUP = 16
HALO = 4
PIECES = 4
CHUNK_ROWS = 18
VMEM = 60 * 1024 * 1024


def light_codes(light_ids, tile_offsets, light_table):
    halfway = light_table.shape[1] // 2
    onehot = (
        light_ids[:, None] == jnp.arange(light_table.shape[0], dtype=jnp.int32)[None, :]
    ).astype(jnp.bfloat16)
    looked = jnp.dot(onehot, light_table, preferred_element_type=jnp.float32)
    rates = jnp.exp(-math.log(1000.0) * jnp.arange(halfway, dtype=jnp.float32) / halfway)
    angles = tile_offsets.astype(jnp.float32)[:, None] * rates[None, :]
    summed = looked + jnp.concatenate([jnp.sin(angles), jnp.cos(angles)], axis=1)
    return (summed * lax.rsqrt(jnp.mean(summed * summed, axis=1, keepdims=True) + 1e-06)).astype(
        jnp.bfloat16
    )


def place():
    light, tex = lax.axis_index("light"), lax.axis_index("tex")
    half, core = tex // 2, tex % 2
    return light, half, core, light * 2 + half


def peer(chip, core):
    return (chip // 2, (chip % 2) * 2 + core)


def greet():
    light, half, core, me = place()
    chips = 2 * lax.axis_size("light")
    barrier = pltpu.get_barrier_semaphore()

    def signal(target):
        pl.semaphore_signal(barrier, inc=1, device_id=target, device_id_type=MESH)

    def signal_chip(step, _):
        signal(peer(lax.rem(me + step, chips), core))
        return 0

    lax.fori_loop(1, chips, signal_chip, 0)
    signal((light, half * 2 + 1 - core))
    signal((light, (1 - half) * 2 + 1 - core))
    pl.semaphore_wait(barrier, chips + 1)


def await_bytes(ref, sem):
    pltpu.make_async_copy(ref, ref, sem).wait()


def swap_copies(src, dst, send, recv, start):
    light, half, core, _ = place()
    rows = src.shape[1]
    halo = dst.shape[0] - 2 * rows

    def go(source, target, to_half, to_core, slot, number):
        here = jnp.logical_and(to_half == half, to_core == core)

        @pl.when(here)
        def _():
            if start:
                pltpu.make_async_copy(source, target, recv.at[slot]).start()

        @pl.when(jnp.logical_not(here))
        def _():
            copy = pltpu.make_async_remote_copy(
                src_ref=source,
                dst_ref=target,
                send_sem=send.at[number],
                recv_sem=recv.at[slot],
                device_id=(light, to_half * 2 + to_core),
                device_id_type=MESH,
            )
            if start:
                copy.start()
            else:
                copy.wait_send()

    for to_half in range(2):
        for own in range(2):

            @pl.when(core == own)
            def _():
                go(
                    src.at[to_half],
                    dst.at[pl.ds(own * rows + halo * half, rows)],
                    to_half,
                    half,
                    own,
                    to_half,
                )

        @pl.when(jnp.logical_and(half == 1, core == 0))
        def _():
            go(
                src.at[to_half, pl.ds(0, halo)],
                dst.at[pl.ds(2 * rows, halo)],
                to_half,
                0,
                2,
                2 + to_half,
            )

        @pl.when(jnp.logical_and(half == 0, core == 1))
        def _():
            go(
                src.at[to_half, pl.ds(rows - halo, halo)],
                dst.at[pl.ds(0, halo)],
                to_half,
                1,
                2,
                2 + to_half,
            )


def swap_arrivals(src, dst, recv):
    rows = src.shape[1]
    halo = dst.shape[0] - 2 * rows
    for slot, count in ((0, rows), (1, rows), (2, halo)):
        await_bytes(dst.at[pl.ds(0, count)], recv.at[slot])


def give_back(src, dst, send, recv, piece, start):
    light, half, core, _ = place()
    count = src.shape[0] // PIECES
    to_core, part = piece // (PIECES // 2), piece % (PIECES // 2)
    here = jnp.logical_and(core == half, to_core == core)
    source = src.at[pl.ds(piece * count, count)]
    target = dst.at[half, pl.ds(part * count, count)]
    slot = half * (PIECES // 2) + part

    @pl.when(here)
    def _():
        if start:
            pltpu.make_async_copy(source, target, recv.at[slot]).start()

    @pl.when(jnp.logical_not(here))
    def _():
        copy = pltpu.make_async_remote_copy(
            src_ref=source,
            dst_ref=target,
            send_sem=send.at[piece],
            recv_sem=recv.at[slot],
            device_id=(light, core * 2 + to_core),
            device_id_type=MESH,
        )
        if start:
            copy.start()
        else:
            copy.wait_send()


def whole_kernel(
    scale,
    lights,
    codes_ref,
    hyper_ref,
    feat_ref,
    up_ref,
    codes_out,
    summed_out,
    relit_out,
    grad_out,
    hyper,
    codes,
    table,
    ready,
    blocks,
    wide,
    line,
    kernels,
    feat,
    up,
    feats,
    hidden,
    grads,
    slope,
    total,
    relit,
    grad,
    parts,
    theirs,
    added,
    sums,
    hyper_sem,
    code_send,
    code_recv,
    own_sem,
    block_send,
    block_recv,
    pass_send,
    pass_recv,
    feat_send,
    feat_recv,
    up_send,
    up_recv,
    core_send,
    core_recv,
    sum_send,
    sum_recv,
    relit_send,
    relit_recv,
    grad_send,
    grad_recv,
):
    light, half, core, me = place()
    chips = 2 * lights
    groups = chips // GROUP
    my_group, my_slot = me // GROUP, me % GROUP
    sibling = (light, half * 2 + 1 - core)
    block_rows = ready.shape[1]
    taps = block_rows // 2
    rows, columns, channels = feat.shape
    own_rows = relit.shape[0]
    frame, own = rows * columns, own_rows * columns
    depth = 9 * channels
    chunk = total.shape[0]
    chunk_rows = chunk // columns
    inner = rows - own_rows
    first_own = pl.multiple_of(core * inner * columns, 16)

    load = pltpu.make_async_copy(hyper_ref, hyper, hyper_sem)
    load.start()
    greet()

    mine = pl.ds(pl.multiple_of(light * 8, 8), 8)
    codes[mine, :] = codes_ref[...]

    def send_codes(step, _):
        pltpu.make_async_remote_copy(
            src_ref=codes_ref,
            dst_ref=codes.at[mine],
            send_sem=code_send,
            recv_sem=code_recv,
            device_id=(lax.rem(light + step, lights), half * 2 + core),
            device_id_type=MESH,
        ).start()
        return 0

    lax.fori_loop(1, lights, send_codes, 0)
    swap_copies(feat_ref, feat, feat_send, feat_recv, True)
    swap_copies(up_ref, up, up_send, up_recv, True)
    for image in (feats, hidden, grads):
        edge = jnp.zeros((columns, image.shape[1]), image.dtype)
        image[:columns] = edge
        image[frame + columns :] = edge
    arrived = codes.at[pl.ds(0, 8 * (lights - 1))]
    await_bytes(arrived, code_recv)
    all_codes = jnp.concatenate(
        [codes[pl.ds(k, chips, stride=4), :] for k in range(4)], axis=1
    ).astype(jnp.bfloat16)
    codes_out[...] = all_codes
    load.wait()

    for row in range(taps):
        product = scale * jnp.dot(
            all_codes,
            hyper[:, row * 2 * LANES : (row + 1) * 2 * LANES],
            preferred_element_type=jnp.float32,
        )
        table[pl.ds(row, chips, stride=40), :] = product[:, :LANES]
        table[pl.ds(taps + row, chips, stride=40), :] = product[:, LANES:]

    def narrow(chip):
        ready[chip] = table[pl.ds(pl.multiple_of(chip * 40, 8), block_rows), :].astype(
            jnp.bfloat16
        )

    narrow(me)
    keep = pltpu.make_async_copy(ready.at[me], blocks.at[core, me], own_sem)
    keep.start()

    def send_block(step, _):
        group = lax.rem(my_group + step // GROUP, groups)
        other = group * GROUP + lax.rem(my_slot + step % GROUP, GROUP)
        narrow(other)
        pltpu.make_async_remote_copy(
            src_ref=ready.at[other],
            dst_ref=blocks.at[core, me],
            send_sem=block_send,
            recv_sem=block_recv.at[my_group],
            device_id=peer(other, core),
            device_id_type=MESH,
        ).start()
        return 0

    lax.fori_loop(1, chips, send_block, 0)

    def row_span(row):
        return pl.ds(pl.multiple_of(row * columns, 16), columns)

    def spread(image, row, values):
        span = row_span(row + 1)
        none = jnp.zeros((1, channels), jnp.float32)
        before = jnp.concatenate([none, values[:-1]], axis=0)
        after = jnp.concatenate([values[1:], none], axis=0)
        image[span, :channels] = before.astype(image.dtype)
        image[span, channels : 2 * channels] = values.astype(image.dtype)
        image[span, 2 * channels :] = after.astype(image.dtype)

    swap_arrivals(feat_ref, feat, feat_recv)
    swap_arrivals(up_ref, up, up_recv)

    def place_feats(row, _):
        spread(feats, row, feat[row].astype(jnp.float32))
        return 0

    lax.fori_loop(0, rows, place_feats, 0)

    def to_sibling(group):
        span = blocks.at[core, pl.ds(group * GROUP, GROUP)]
        return pltpu.make_async_remote_copy(
            src_ref=span,
            dst_ref=span,
            send_sem=pass_send.at[group],
            recv_sem=pass_recv.at[group],
            device_id=sibling,
            device_id_type=MESH,
        )

    def gather(group, from_core):
        def block(slot, _):
            chip = group * GROUP + slot
            line[...] = blocks[from_core, chip].astype(jnp.float32)

            def move(side, _):
                wide[side, pl.ds((2 * chip + from_core) * taps, taps), :] = line[
                    pl.ds(side * taps, taps), :
                ]
                return 0

            return lax.fori_loop(0, 2, move, 0)

        lax.fori_loop(0, GROUP, block, 0)

    def end_group(group):
        to_sibling(group).wait_recv()
        gather(group, 1 - core)
        count = 2 * GROUP * taps
        span = pl.ds(pl.multiple_of(group * count, 16), count)
        kernels[span, :LANES] = wide[0, span, :].astype(jnp.bfloat16)
        kernels[span, LANES:] = wide[1, span, :].astype(jnp.bfloat16)

    keep.wait()
    await_bytes(blocks.at[core, pl.ds(0, GROUP - 1)], block_recv.at[my_group])
    to_sibling(my_group).start()
    gather(my_group, core)

    def take_group(step, _):
        group = lax.rem(my_group + groups - step, groups)
        await_bytes(blocks.at[core, pl.ds(0, GROUP)], block_recv.at[group])
        to_sibling(group).start()
        gather(group, core)
        end_group(lax.rem(group + 1, groups))
        return 0

    lax.fori_loop(1, groups, take_group, 0)
    end_group(lax.rem(my_group + 1, groups))

    def conv(image, base, start):
        out = None
        for tap in range(3):
            span = pl.ds(pl.multiple_of(start + tap * columns, 16), chunk)
            piece = jnp.dot(
                image[span, :],
                kernels[base + tap * 3 * channels : base + (tap + 1) * 3 * channels, :],
                preferred_element_type=jnp.float32,
            )
            out = piece if out is None else out + piece
        total[...] = out

    def conv_back(image, base, start, count):
        out = None
        for row_tap in range(3):
            span = pl.ds(pl.multiple_of(start + (2 - row_tap) * columns, 16), count)
            for col_tap in range(3):
                at = base + (row_tap * 3 + col_tap) * channels
                piece = lax.dot_general(
                    image[span, (2 - col_tap) * channels : (3 - col_tap) * channels],
                    kernels[at : at + channels, :],
                    (((1,), (1,)), ((), ())),
                    preferred_element_type=jnp.float32,
                )
                out = piece if out is None else out + piece
        total[:count] = out

    def each_chunk(compute, finish_row):
        def do_chunk(step, _):
            compute(step * chunk)

            def do_row(row, _):
                finish_row(step * chunk_rows + row, total[row_span(row), :])
                return 0

            return lax.fori_loop(0, chunk_rows, do_row, 0)

        lax.fori_loop(0, frame // chunk, do_chunk, 0)

    def store_own(ref, row, values):
        local = row - core * inner

        @pl.when(jnp.logical_and(local >= 0, local < own_rows))
        def _():
            ref[local] = values.astype(ref.dtype)

    def end_first(row, pre):
        sig = jax.nn.sigmoid(pre)
        slope[row_span(row), :] = sig * (1.0 + pre * (1.0 - sig))
        spread(hidden, row, pre * sig)

    def end_second(row, pre):
        sig = jax.nn.sigmoid(pre)
        store_own(relit, row, pre * sig)
        spread(grads, row, up[row].astype(jnp.float32) * (sig * (1.0 + pre * (1.0 - sig))))

    def kernel_grad(image, base):
        upstream = grads[pl.ds(first_own + columns, own), channels : 2 * channels].T

        def do_tap(tap, _):
            span = pl.ds(pl.multiple_of(first_own + tap * columns, 16), own)
            for col_tap in range(3):
                piece = jnp.dot(
                    upstream,
                    image[span, col_tap * channels : (col_tap + 1) * channels],
                    preferred_element_type=jnp.float32,
                )
                at = pl.multiple_of(base + (tap * 3 + col_tap) * channels, channels)
                wide[0, pl.ds(at, channels), :] = piece[:LANES].T
                wide[1, pl.ds(at, channels), :] = piece[LANES:].T
            return 0

        lax.fori_loop(0, 3, do_tap, 0)

    def end_grad(row, back):
        slope[row_span(row), :] = slope[row_span(row), :] * back

    def part_copy(group):
        return pltpu.make_async_remote_copy(
            src_ref=parts.at[pl.ds(group * GROUP, GROUP)],
            dst_ref=theirs.at[pl.ds(group * GROUP, GROUP)],
            send_sem=core_send.at[group],
            recv_sem=core_recv.at[group],
            device_id=sibling,
            device_id_type=MESH,
        )

    def pick(owner):
        def move(side, _):
            line[pl.ds(side * taps, taps), :] = wide[side, pl.ds(owner * taps, taps), :]
            return 0

        lax.fori_loop(0, 2, move, 0)
        return line[...]

    def send_grad(first, between):
        some = groups // 2

        def group_at(step):
            return first + lax.rem(my_group + step, some)

        def share(step):
            group = group_at(step)

            def block(slot, _):
                chip = group * GROUP + slot
                parts[chip] = pick(2 * chip + 1 - core).astype(parts.dtype)
                return 0

            lax.fori_loop(0, GROUP, block, 0)
            part_copy(group).start()

        def add(step):
            group = group_at(step)
            part_copy(group).wait_recv()

            def block(slot, _):
                other = group * GROUP + lax.rem(my_slot + slot, GROUP)
                added[other] = (
                    pick(2 * other + core) + theirs[other].astype(jnp.float32)
                ).astype(added.dtype)

                @pl.when(other == me)
                def _():
                    pltpu.make_async_copy(added.at[me], sums.at[me], own_sem).start()

                @pl.when(other != me)
                def _():
                    pltpu.make_async_remote_copy(
                        src_ref=added.at[other],
                        dst_ref=sums.at[me],
                        send_sem=sum_send,
                        recv_sem=sum_recv.at[my_group],
                        device_id=peer(other, core),
                        device_id_type=MESH,
                    ).start()

                return 0

            lax.fori_loop(0, GROUP, block, 0)

        share(0)

        def both(step, _):
            share(step)
            add(step - 1)
            between(step - 1)
            return 0

        lax.fori_loop(1, some, both, 0)
        add(some - 1)
        between(some - 1)

    def feature_piece(piece):
        count = own // PIECES
        conv_back(grads, 0, pl.multiple_of(first_own + piece * count, 16), count)

        def store(row, _):
            grad[piece * (own_rows // PIECES) + row] = total[row_span(row), :].astype(grad.dtype)
            return 0

        lax.fori_loop(0, own_rows // PIECES, store, 0)
        give_back(grad, grad_out, grad_send, grad_recv, piece, True)

    def relit_piece(piece):
        give_back(relit, relit_out, relit_send, relit_recv, piece, True)

    each_chunk(lambda start: conv(feats, 0, start), end_first)
    each_chunk(lambda start: conv(hidden, depth, start), end_second)
    kernel_grad(hidden, depth)
    send_grad(groups // 2, relit_piece)
    each_chunk(lambda start: conv_back(grads, depth, start, chunk), end_grad)

    def place_grad(row, _):
        spread(grads, row, slope[row_span(row), :])
        return 0

    lax.fori_loop(0, rows, place_grad, 0)
    kernel_grad(feats, 0)
    send_grad(0, feature_piece)

    def finish(group, _):
        to_sibling(group).wait_send()
        part_copy(group).wait_send()
        return 0

    lax.fori_loop(0, groups, finish, 0)
    await_bytes(ready.at[pl.ds(0, chips - 1)], block_send)
    await_bytes(arrived, code_send)
    swap_copies(feat_ref, feat, feat_send, feat_recv, False)
    swap_copies(up_ref, up, up_send, up_recv, False)

    def finish_piece(piece, _):
        give_back(relit, relit_out, relit_send, relit_recv, piece, False)
        give_back(grad, grad_out, grad_send, grad_recv, piece, False)
        return 0

    lax.fori_loop(0, PIECES, finish_piece, 0)

    def widen(group):
        def block(slot, _):
            chip = group * GROUP + slot
            table[pl.ds(pl.multiple_of(chip * 40, 8), block_rows), :] = sums[chip].astype(
                jnp.float32
            )
            return 0

        lax.fori_loop(0, GROUP, block, 0)

    pltpu.make_async_copy(added.at[me], sums.at[me], own_sem).wait()
    await_bytes(sums.at[pl.ds(0, GROUP - 1)], sum_recv.at[my_group])
    widen(my_group)

    def take_sums(step, _):
        group = lax.rem(my_group + groups - step, groups)
        await_bytes(sums.at[pl.ds(0, GROUP)], sum_recv.at[group])
        widen(group)
        return 0

    lax.fori_loop(1, groups, take_sums, 0)
    for row in range(taps):
        for side in range(2):
            at = (2 * row + side) * LANES
            summed_out[:, at : at + LANES] = table[
                pl.ds(side * taps + row, chips, stride=40), :
            ].astype(summed_out.dtype)
    await_bytes(added.at[pl.ds(0, chips - 1)], sum_send)
    piece_rows = own_rows // PIECES
    for slot in range(PIECES):
        await_bytes(relit_out.at[0, pl.ds(0, piece_rows)], relit_recv.at[slot])
        await_bytes(grad_out.at[0, pl.ds(0, piece_rows)], grad_recv.at[slot])


def whole(scale, lights, codes, hyper_weight, features, upstream):
    chips = 2 * lights
    groups = chips // GROUP
    width, own_len = hyper_weight.shape
    block_rows = own_len // LANES
    _, rows_dev, columns, channels = features.shape
    depth = 9 * channels
    own_rows = 2 * rows_dev
    rows = own_rows + HALO
    frame = rows * columns
    dma = pltpu.SemaphoreType.DMA
    anywhere = pl.BlockSpec(memory_space=pl.ANY)
    vmem = pl.BlockSpec(memory_space=pltpu.VMEM)
    image = jax.ShapeDtypeStruct(features.shape, jnp.bfloat16)
    block = pltpu.VMEM((chips, block_rows, LANES), jnp.bfloat16)
    shifted = pltpu.VMEM((frame + 2 * columns, 3 * channels), jnp.bfloat16)
    return pl.pallas_call(
        functools.partial(whole_kernel, scale, lights),
        out_shape=(
            jax.ShapeDtypeStruct((chips, width), jnp.bfloat16),
            jax.ShapeDtypeStruct((chips, own_len), jnp.bfloat16),
            image,
            image,
        ),
        in_specs=[vmem, anywhere, anywhere, anywhere],
        out_specs=(vmem, vmem, anywhere, anywhere),
        scratch_shapes=[
            pltpu.VMEM((width, own_len), jnp.bfloat16),
            pltpu.VMEM((8 * lights, LANES), jnp.float32),
            pltpu.VMEM((chips * 40, LANES), jnp.float32),
            block,
            pltpu.VMEM((2, chips, block_rows, LANES), jnp.bfloat16),
            pltpu.VMEM((2, 2 * depth, LANES), jnp.float32),
            pltpu.VMEM((block_rows, LANES), jnp.float32),
            pltpu.VMEM((2 * depth, channels), jnp.bfloat16),
            pltpu.VMEM((rows, columns, channels), jnp.bfloat16),
            pltpu.VMEM((rows, columns, channels), jnp.bfloat16),
            shifted,
            shifted,
            shifted,
            pltpu.VMEM((frame, channels), jnp.float32),
            pltpu.VMEM((CHUNK_ROWS * columns, channels), jnp.float32),
            pltpu.VMEM((own_rows, columns, channels), jnp.bfloat16),
            pltpu.VMEM((own_rows, columns, channels), jnp.bfloat16),
            block,
            block,
            block,
            block,
            dma,
            dma,
            dma,
            dma,
            dma,
            dma((groups,)),
            dma((groups,)),
            dma((groups,)),
            dma((4,)),
            dma((3,)),
            dma((4,)),
            dma((3,)),
            dma((groups,)),
            dma((groups,)),
            dma,
            dma((groups,)),
            dma((PIECES,)),
            dma((PIECES,)),
            dma((PIECES,)),
            dma((PIECES,)),
        ],
        compiler_params=pltpu.CompilerParams(
            has_side_effects=True, collective_id=0, vmem_limit_bytes=VMEM
        ),
    )(codes, hyper_weight, features, upstream)


def last_kernel(
    scale, codes_ref, summed_ref, relit_ref, grad_ref, hyper_out, relit_out, grad_out, ready, sems, out_sems
):
    copies = [
        pltpu.make_async_copy(relit_ref, relit_out, sems.at[0]),
        pltpu.make_async_copy(grad_ref, grad_out, sems.at[1]),
    ]
    for copy in copies:
        copy.start()
    codes = codes_ref[...].T
    steps = ready.shape[0]
    width = ready.shape[2]
    for step in range(steps):
        span = pl.ds(step * width, width)
        ready[step] = (
            scale * jnp.dot(codes, summed_ref[:, span], preferred_element_type=jnp.float32)
        ).astype(ready.dtype)
        copy = pltpu.make_async_copy(ready.at[step], hyper_out.at[:, span], out_sems.at[step])
        copy.start()
        copies.append(copy)
    for copy in copies:
        copy.wait()


def last_step(scale, codes, summed, relit, feature_grad):
    chips, depth = codes.shape
    own_len = summed.shape[1]
    steps = 9
    anywhere = pl.BlockSpec(memory_space=pl.ANY)
    vmem = pl.BlockSpec(memory_space=pltpu.VMEM)
    return pl.pallas_call(
        functools.partial(last_kernel, scale),
        out_shape=(
            jax.ShapeDtypeStruct((depth, own_len), jnp.bfloat16),
            jax.ShapeDtypeStruct(relit.shape, jnp.bfloat16),
            jax.ShapeDtypeStruct(feature_grad.shape, jnp.bfloat16),
        ),
        in_specs=[vmem, vmem, anywhere, anywhere],
        out_specs=(anywhere,) * 3,
        scratch_shapes=[
            pltpu.VMEM((steps, depth, own_len // steps), jnp.bfloat16),
            pltpu.SemaphoreType.DMA((2,)),
            pltpu.SemaphoreType.DMA((steps,)),
        ],
        compiler_params=pltpu.CompilerParams(vmem_limit_bytes=VMEM),
    )(codes, summed, relit, feature_grad)


def shards(light_ids, tile_offsets, light_table, hyper_weight, features, upstream_grad):
    channels = features.shape[3]
    scale = 1.0 / math.sqrt(9 * channels)
    lights = lax.axis_size("light")
    own_codes = light_codes(light_ids, tile_offsets, light_table)
    codes, summed, relit, feature_grad = whole(
        scale,
        lights,
        own_codes.astype(jnp.float32).reshape(8, LANES),
        hyper_weight,
        features,
        upstream_grad,
    )
    hyper_grad, relit, feature_grad = last_step(scale, codes, summed, relit, feature_grad)
    return (relit, feature_grad, hyper_grad)


def solution(mesh):
    in_specs = (
        P("light"),
        P("light"),
        P(),
        P(None, ("light", "tex")),
        P("light", "tex", None, None),
        P("light", "tex", None, None),
    )
    out_specs = (
        P("light", "tex", None, None),
        P("light", "tex", None, None),
        P(None, ("light", "tex")),
    )
    return jax.shard_map(shards, mesh=mesh, in_specs=in_specs, out_specs=out_specs, check_vma=False)
```

```python
import functools
import math

import jax
import jax.numpy as jnp
from jax import lax
from jax.experimental import pallas as pl
from jax.experimental.pallas import tpu as pltpu
from jax.sharding import PartitionSpec as P

MESH = pl.DeviceIdType.MESH
LANES = 128
GROUP = 16
HALO = 4
PIECES = 4
AT_ONCE = 4
CHUNK_ROWS = 18
VMEM = 60 * 1024 * 1024


def light_codes(light_ids, tile_offsets, light_table):
    halfway = light_table.shape[1] // 2
    onehot = (
        light_ids[:, None] == jnp.arange(light_table.shape[0], dtype=jnp.int32)[None, :]
    ).astype(jnp.bfloat16)
    looked = jnp.dot(onehot, light_table, preferred_element_type=jnp.float32)
    rates = jnp.exp(-math.log(1000.0) * jnp.arange(halfway, dtype=jnp.float32) / halfway)
    angles = tile_offsets.astype(jnp.float32)[:, None] * rates[None, :]
    summed = looked + jnp.concatenate([jnp.sin(angles), jnp.cos(angles)], axis=1)
    return (summed * lax.rsqrt(jnp.mean(summed * summed, axis=1, keepdims=True) + 1e-06)).astype(
        jnp.bfloat16
    )


def place():
    light, tex = lax.axis_index("light"), lax.axis_index("tex")
    half, core = tex // 2, tex % 2
    return light, half, core, light * 2 + half


def peer(chip, core):
    return (chip // 2, (chip % 2) * 2 + core)


def greet():
    light, half, core, me = place()
    chips = 2 * lax.axis_size("light")
    barrier = pltpu.get_barrier_semaphore()

    def signal(target):
        pl.semaphore_signal(barrier, inc=1, device_id=target, device_id_type=MESH)

    def signal_chip(step, _):
        signal(peer(lax.rem(me + step, chips), core))
        return 0

    lax.fori_loop(1, chips, signal_chip, 0)
    signal((light, half * 2 + 1 - core))
    signal((light, (1 - half) * 2 + 1 - core))
    pl.semaphore_wait(barrier, chips + 1)


def await_bytes(ref, sem):
    pltpu.make_async_copy(ref, ref, sem).wait()


def swap_copies(src, dst, send, recv, start):
    light, half, core, _ = place()
    rows = src.shape[1]
    halo = dst.shape[0] - 2 * rows

    def go(source, target, to_half, to_core, slot, number):
        here = jnp.logical_and(to_half == half, to_core == core)

        @pl.when(here)
        def _():
            if start:
                pltpu.make_async_copy(source, target, recv.at[slot]).start()

        @pl.when(jnp.logical_not(here))
        def _():
            copy = pltpu.make_async_remote_copy(
                src_ref=source,
                dst_ref=target,
                send_sem=send.at[number],
                recv_sem=recv.at[slot],
                device_id=(light, to_half * 2 + to_core),
                device_id_type=MESH,
            )
            if start:
                copy.start()
            else:
                copy.wait_send()

    for to_half in range(2):
        for own in range(2):

            @pl.when(core == own)
            def _():
                go(
                    src.at[to_half],
                    dst.at[pl.ds(own * rows + halo * half, rows)],
                    to_half,
                    half,
                    own,
                    to_half,
                )

        @pl.when(jnp.logical_and(half == 1, core == 0))
        def _():
            go(
                src.at[to_half, pl.ds(0, halo)],
                dst.at[pl.ds(2 * rows, halo)],
                to_half,
                0,
                2,
                2 + to_half,
            )

        @pl.when(jnp.logical_and(half == 0, core == 1))
        def _():
            go(
                src.at[to_half, pl.ds(rows - halo, halo)],
                dst.at[pl.ds(0, halo)],
                to_half,
                1,
                2,
                2 + to_half,
            )


def swap_arrivals(src, dst, recv):
    rows = src.shape[1]
    halo = dst.shape[0] - 2 * rows
    for slot, count in ((0, rows), (1, rows), (2, halo)):
        await_bytes(dst.at[pl.ds(0, count)], recv.at[slot])


def give_back(src, dst, send, recv, piece, start):
    light, half, core, _ = place()
    count = src.shape[0] // PIECES
    to_core, part = piece // (PIECES // 2), piece % (PIECES // 2)
    here = jnp.logical_and(core == half, to_core == core)
    source = src.at[pl.ds(piece * count, count)]
    target = dst.at[half, pl.ds(part * count, count)]
    slot = half * (PIECES // 2) + part

    @pl.when(here)
    def _():
        if start:
            pltpu.make_async_copy(source, target, recv.at[slot]).start()

    @pl.when(jnp.logical_not(here))
    def _():
        copy = pltpu.make_async_remote_copy(
            src_ref=source,
            dst_ref=target,
            send_sem=send.at[piece],
            recv_sem=recv.at[slot],
            device_id=(light, core * 2 + to_core),
            device_id_type=MESH,
        )
        if start:
            copy.start()
        else:
            copy.wait_send()


def whole_kernel(
    scale,
    lights,
    codes_ref,
    hyper_ref,
    feat_ref,
    up_ref,
    codes_out,
    summed_out,
    relit_out,
    grad_out,
    hyper,
    codes,
    table,
    ready,
    blocks,
    wide,
    line,
    kernels,
    feat,
    up,
    feats,
    hidden,
    grads,
    slope,
    total,
    relit,
    grad,
    parts,
    theirs,
    added,
    sums,
    hyper_sem,
    code_send,
    code_recv,
    own_sem,
    block_send,
    block_recv,
    pass_send,
    pass_recv,
    feat_send,
    feat_recv,
    up_send,
    up_recv,
    core_send,
    core_recv,
    sum_send,
    sum_recv,
    relit_send,
    relit_recv,
    grad_send,
    grad_recv,
):
    light, half, core, me = place()
    chips = 2 * lights
    groups = chips // GROUP
    my_group, my_slot = me // GROUP, me % GROUP
    sibling = (light, half * 2 + 1 - core)
    block_rows = ready.shape[1]
    taps = block_rows // 2
    rows, columns, channels = feat.shape
    own_rows = relit.shape[0]
    frame, own = rows * columns, own_rows * columns
    depth = 9 * channels
    chunk = total.shape[0]
    chunk_rows = chunk // columns
    inner = rows - own_rows
    first_own = pl.multiple_of(core * inner * columns, 16)

    load = pltpu.make_async_copy(hyper_ref, hyper, hyper_sem)
    load.start()
    greet()

    mine = pl.ds(pl.multiple_of(light * 8, 8), 8)
    codes[mine, :] = codes_ref[...]

    def send_codes(step, _):
        pltpu.make_async_remote_copy(
            src_ref=codes_ref,
            dst_ref=codes.at[mine],
            send_sem=code_send,
            recv_sem=code_recv,
            device_id=(lax.rem(light + step, lights), half * 2 + core),
            device_id_type=MESH,
        ).start()
        return 0

    lax.fori_loop(1, lights, send_codes, 0)
    swap_copies(feat_ref, feat, feat_send, feat_recv, True)
    swap_copies(up_ref, up, up_send, up_recv, True)
    for image in (feats, hidden, grads):
        edge = jnp.zeros((columns, image.shape[1]), image.dtype)
        image[:columns] = edge
        image[frame + columns :] = edge
    arrived = codes.at[pl.ds(0, 8 * (lights - 1))]
    await_bytes(arrived, code_recv)
    all_codes = jnp.concatenate(
        [codes[pl.ds(k, chips, stride=4), :] for k in range(4)], axis=1
    ).astype(jnp.bfloat16)
    codes_out[...] = all_codes
    load.wait()

    for row in range(taps):
        product = scale * jnp.dot(
            all_codes,
            hyper[:, row * 2 * LANES : (row + 1) * 2 * LANES],
            preferred_element_type=jnp.float32,
        )
        table[pl.ds(row, chips, stride=40), :] = product[:, :LANES]
        table[pl.ds(taps + row, chips, stride=40), :] = product[:, LANES:]

    def narrow(chip):
        ready[chip] = table[pl.ds(pl.multiple_of(chip * 40, 8), block_rows), :].astype(
            jnp.bfloat16
        )

    narrow(me)
    keep = pltpu.make_async_copy(ready.at[me], blocks.at[core, me], own_sem)
    keep.start()

    def send_block(step, _):
        group = lax.rem(my_group + step // GROUP, groups)
        other = group * GROUP + lax.rem(my_slot + step % GROUP, GROUP)
        narrow(other)
        pltpu.make_async_remote_copy(
            src_ref=ready.at[other],
            dst_ref=blocks.at[core, me],
            send_sem=block_send,
            recv_sem=block_recv.at[my_group],
            device_id=peer(other, core),
            device_id_type=MESH,
        ).start()
        return 0

    lax.fori_loop(1, chips, send_block, 0)

    def row_span(row):
        return pl.ds(pl.multiple_of(row * columns, 16), columns)

    def spread(image, row, values):
        span = row_span(row + 1)
        none = jnp.zeros((1, channels), jnp.float32)
        before = jnp.concatenate([none, values[:-1]], axis=0)
        after = jnp.concatenate([values[1:], none], axis=0)
        image[span, :channels] = before.astype(image.dtype)
        image[span, channels : 2 * channels] = values.astype(image.dtype)
        image[span, 2 * channels :] = after.astype(image.dtype)

    swap_arrivals(feat_ref, feat, feat_recv)
    swap_arrivals(up_ref, up, up_recv)

    def place_feats(row, _):
        spread(feats, row, feat[row].astype(jnp.float32))
        return 0

    lax.fori_loop(0, rows, place_feats, 0)

    def to_sibling(group):
        span = blocks.at[core, pl.ds(group * GROUP, GROUP)]
        return pltpu.make_async_remote_copy(
            src_ref=span,
            dst_ref=span,
            send_sem=pass_send.at[group],
            recv_sem=pass_recv.at[group],
            device_id=sibling,
            device_id_type=MESH,
        )

    def gather(group, from_core):
        def block(step, _):
            several = [group * GROUP + step * AT_ONCE + k for k in range(AT_ONCE)]
            for k, chip in enumerate(several):
                line[k] = blocks[from_core, chip].astype(jnp.float32)
            for k, chip in enumerate(several):

                def move(side, _):
                    wide[side, pl.ds((2 * chip + from_core) * taps, taps), :] = line[
                        k, pl.ds(side * taps, taps), :
                    ]
                    return 0

                lax.fori_loop(0, 2, move, 0)
            return 0

        lax.fori_loop(0, GROUP // AT_ONCE, block, 0)

    def end_group(group):
        to_sibling(group).wait_recv()
        gather(group, 1 - core)
        count = 2 * GROUP * taps
        span = pl.ds(pl.multiple_of(group * count, 16), count)
        kernels[span, :LANES] = wide[0, span, :].astype(jnp.bfloat16)
        kernels[span, LANES:] = wide[1, span, :].astype(jnp.bfloat16)

    keep.wait()
    await_bytes(blocks.at[core, pl.ds(0, GROUP - 1)], block_recv.at[my_group])
    to_sibling(my_group).start()
    gather(my_group, core)

    def take_group(step, _):
        group = lax.rem(my_group + groups - step, groups)
        await_bytes(blocks.at[core, pl.ds(0, GROUP)], block_recv.at[group])
        to_sibling(group).start()
        gather(group, core)
        end_group(lax.rem(group + 1, groups))
        return 0

    lax.fori_loop(1, groups, take_group, 0)
    end_group(lax.rem(my_group + 1, groups))

    def conv(image, base, start):
        out = None
        for tap in range(3):
            span = pl.ds(pl.multiple_of(start + tap * columns, 16), chunk)
            piece = jnp.dot(
                image[span, :],
                kernels[base + tap * 3 * channels : base + (tap + 1) * 3 * channels, :],
                preferred_element_type=jnp.float32,
            )
            out = piece if out is None else out + piece
        total[...] = out

    def conv_back(image, base, start, count):
        out = None
        for row_tap in range(3):
            span = pl.ds(pl.multiple_of(start + (2 - row_tap) * columns, 16), count)
            for col_tap in range(3):
                at = base + (row_tap * 3 + col_tap) * channels
                piece = lax.dot_general(
                    image[span, (2 - col_tap) * channels : (3 - col_tap) * channels],
                    kernels[at : at + channels, :],
                    (((1,), (1,)), ((), ())),
                    preferred_element_type=jnp.float32,
                )
                out = piece if out is None else out + piece
        total[:count] = out

    def each_chunk(compute, finish_row):
        def do_chunk(step, _):
            compute(step * chunk)

            def do_row(row, _):
                finish_row(step * chunk_rows + row, total[row_span(row), :])
                return 0

            return lax.fori_loop(0, chunk_rows, do_row, 0)

        lax.fori_loop(0, frame // chunk, do_chunk, 0)

    def store_own(ref, row, values):
        local = row - core * inner

        @pl.when(jnp.logical_and(local >= 0, local < own_rows))
        def _():
            ref[local] = values.astype(ref.dtype)

    def end_first(row, pre):
        sig = jax.nn.sigmoid(pre)
        slope[row_span(row), :] = sig * (1.0 + pre * (1.0 - sig))
        spread(hidden, row, pre * sig)

    def end_second(row, pre):
        sig = jax.nn.sigmoid(pre)
        store_own(relit, row, pre * sig)
        spread(grads, row, up[row].astype(jnp.float32) * (sig * (1.0 + pre * (1.0 - sig))))

    def kernel_grad(image, base):
        upstream = grads[pl.ds(first_own + columns, own), channels : 2 * channels].T

        def do_tap(tap, _):
            span = pl.ds(pl.multiple_of(first_own + tap * columns, 16), own)
            for col_tap in range(3):
                piece = jnp.dot(
                    upstream,
                    image[span, col_tap * channels : (col_tap + 1) * channels],
                    preferred_element_type=jnp.float32,
                )
                at = pl.multiple_of(base + (tap * 3 + col_tap) * channels, channels)
                wide[0, pl.ds(at, channels), :] = piece[:LANES].T
                wide[1, pl.ds(at, channels), :] = piece[LANES:].T
            return 0

        lax.fori_loop(0, 3, do_tap, 0)

    def end_grad(row, back):
        slope[row_span(row), :] = slope[row_span(row), :] * back

    def part_copy(group):
        return pltpu.make_async_remote_copy(
            src_ref=parts.at[pl.ds(group * GROUP, GROUP)],
            dst_ref=theirs.at[pl.ds(group * GROUP, GROUP)],
            send_sem=core_send.at[group],
            recv_sem=core_recv.at[group],
            device_id=sibling,
            device_id_type=MESH,
        )

    def pick(slot, owner):
        for side in range(2):
            line[slot, side * taps : (side + 1) * taps, :] = wide[
                side, pl.ds(owner * taps, taps), :
            ]

    def send_sum(other):
        @pl.when(other == me)
        def _():
            pltpu.make_async_copy(added.at[me], sums.at[me], own_sem).start()

        @pl.when(other != me)
        def _():
            pltpu.make_async_remote_copy(
                src_ref=added.at[other],
                dst_ref=sums.at[me],
                send_sem=sum_send,
                recv_sem=sum_recv.at[my_group],
                device_id=peer(other, core),
                device_id_type=MESH,
            ).start()

    def send_grad(first, between):
        some = groups // 2

        def group_at(step):
            return first + lax.rem(my_group + step, some)

        def share(step):
            group = group_at(step)

            def block(step, _):
                several = [group * GROUP + step * AT_ONCE + k for k in range(AT_ONCE)]
                for k, chip in enumerate(several):
                    pick(k, 2 * chip + 1 - core)
                for k, chip in enumerate(several):
                    parts[chip] = line[k].astype(parts.dtype)
                return 0

            lax.fori_loop(0, GROUP // AT_ONCE, block, 0)
            part_copy(group).start()

        def add(step):
            group = group_at(step)
            part_copy(group).wait_recv()

            def block(step, _):
                several = [
                    group * GROUP + lax.rem(my_slot + step * AT_ONCE + k, GROUP)
                    for k in range(AT_ONCE)
                ]
                for k, other in enumerate(several):
                    pick(k, 2 * other + core)
                for k, other in enumerate(several):
                    added[other] = (line[k] + theirs[other].astype(jnp.float32)).astype(
                        added.dtype
                    )
                for other in several:
                    send_sum(other)
                return 0

            lax.fori_loop(0, GROUP // AT_ONCE, block, 0)

        share(0)

        def both(step, _):
            share(step)
            add(step - 1)
            between(step - 1)
            return 0

        lax.fori_loop(1, some, both, 0)
        add(some - 1)
        between(some - 1)

    def feature_piece(piece):
        count = own // PIECES
        conv_back(grads, 0, pl.multiple_of(first_own + piece * count, 16), count)

        def store(row, _):
            grad[piece * (own_rows // PIECES) + row] = total[row_span(row), :].astype(grad.dtype)
            return 0

        lax.fori_loop(0, own_rows // PIECES, store, 0)
        give_back(grad, grad_out, grad_send, grad_recv, piece, True)

    def relit_piece(piece, _):
        give_back(relit, relit_out, relit_send, relit_recv, piece, True)
        return 0

    each_chunk(lambda start: conv(feats, 0, start), end_first)
    each_chunk(lambda start: conv(hidden, depth, start), end_second)
    lax.fori_loop(0, PIECES, relit_piece, 0)
    kernel_grad(hidden, depth)
    send_grad(groups // 2, lambda step: None)
    each_chunk(lambda start: conv_back(grads, depth, start, chunk), end_grad)

    def place_grad(row, _):
        spread(grads, row, slope[row_span(row), :])
        return 0

    lax.fori_loop(0, rows, place_grad, 0)
    kernel_grad(feats, 0)
    send_grad(0, feature_piece)

    def finish(group, _):
        to_sibling(group).wait_send()
        part_copy(group).wait_send()
        return 0

    lax.fori_loop(0, groups, finish, 0)
    await_bytes(ready.at[pl.ds(0, chips - 1)], block_send)
    await_bytes(arrived, code_send)
    swap_copies(feat_ref, feat, feat_send, feat_recv, False)
    swap_copies(up_ref, up, up_send, up_recv, False)

    def finish_piece(piece, _):
        give_back(relit, relit_out, relit_send, relit_recv, piece, False)
        give_back(grad, grad_out, grad_send, grad_recv, piece, False)
        return 0

    lax.fori_loop(0, PIECES, finish_piece, 0)

    def widen(group):
        def block(slot, _):
            chip = group * GROUP + slot
            table[pl.ds(pl.multiple_of(chip * 40, 8), block_rows), :] = sums[chip].astype(
                jnp.float32
            )
            return 0

        lax.fori_loop(0, GROUP, block, 0)

    pltpu.make_async_copy(added.at[me], sums.at[me], own_sem).wait()
    await_bytes(sums.at[pl.ds(0, GROUP - 1)], sum_recv.at[my_group])
    widen(my_group)

    def take_sums(step, _):
        group = lax.rem(my_group + groups - step, groups)
        await_bytes(sums.at[pl.ds(0, GROUP)], sum_recv.at[group])
        widen(group)
        return 0

    lax.fori_loop(1, groups, take_sums, 0)
    for row in range(taps):
        for side in range(2):
            at = (2 * row + side) * LANES
            summed_out[:, at : at + LANES] = table[
                pl.ds(side * taps + row, chips, stride=40), :
            ].astype(summed_out.dtype)
    await_bytes(added.at[pl.ds(0, chips - 1)], sum_send)
    piece_rows = own_rows // PIECES
    for slot in range(PIECES):
        await_bytes(relit_out.at[0, pl.ds(0, piece_rows)], relit_recv.at[slot])
        await_bytes(grad_out.at[0, pl.ds(0, piece_rows)], grad_recv.at[slot])


def whole(scale, lights, codes, hyper_weight, features, upstream):
    chips = 2 * lights
    groups = chips // GROUP
    width, own_len = hyper_weight.shape
    block_rows = own_len // LANES
    _, rows_dev, columns, channels = features.shape
    depth = 9 * channels
    own_rows = 2 * rows_dev
    rows = own_rows + HALO
    frame = rows * columns
    dma = pltpu.SemaphoreType.DMA
    anywhere = pl.BlockSpec(memory_space=pl.ANY)
    vmem = pl.BlockSpec(memory_space=pltpu.VMEM)
    image = jax.ShapeDtypeStruct(features.shape, jnp.bfloat16)
    block = pltpu.VMEM((chips, block_rows, LANES), jnp.bfloat16)
    shifted = pltpu.VMEM((frame + 2 * columns, 3 * channels), jnp.bfloat16)
    return pl.pallas_call(
        functools.partial(whole_kernel, scale, lights),
        out_shape=(
            jax.ShapeDtypeStruct((chips, width), jnp.bfloat16),
            jax.ShapeDtypeStruct((chips, own_len), jnp.bfloat16),
            image,
            image,
        ),
        in_specs=[vmem, anywhere, anywhere, anywhere],
        out_specs=(vmem, vmem, anywhere, anywhere),
        scratch_shapes=[
            pltpu.VMEM((width, own_len), jnp.bfloat16),
            pltpu.VMEM((8 * lights, LANES), jnp.float32),
            pltpu.VMEM((chips * 40, LANES), jnp.float32),
            block,
            pltpu.VMEM((2, chips, block_rows, LANES), jnp.bfloat16),
            pltpu.VMEM((2, 2 * depth, LANES), jnp.float32),
            pltpu.VMEM((AT_ONCE, block_rows, LANES), jnp.float32),
            pltpu.VMEM((2 * depth, channels), jnp.bfloat16),
            pltpu.VMEM((rows, columns, channels), jnp.bfloat16),
            pltpu.VMEM((rows, columns, channels), jnp.bfloat16),
            shifted,
            shifted,
            shifted,
            pltpu.VMEM((frame, channels), jnp.float32),
            pltpu.VMEM((CHUNK_ROWS * columns, channels), jnp.float32),
            pltpu.VMEM((own_rows, columns, channels), jnp.bfloat16),
            pltpu.VMEM((own_rows, columns, channels), jnp.bfloat16),
            block,
            block,
            block,
            block,
            dma,
            dma,
            dma,
            dma,
            dma,
            dma((groups,)),
            dma((groups,)),
            dma((groups,)),
            dma((4,)),
            dma((3,)),
            dma((4,)),
            dma((3,)),
            dma((groups,)),
            dma((groups,)),
            dma,
            dma((groups,)),
            dma((PIECES,)),
            dma((PIECES,)),
            dma((PIECES,)),
            dma((PIECES,)),
        ],
        compiler_params=pltpu.CompilerParams(
            has_side_effects=True, collective_id=0, vmem_limit_bytes=VMEM
        ),
    )(codes, hyper_weight, features, upstream)


def last_kernel(
    scale,
    codes_ref,
    summed_ref,
    relit_ref,
    grad_ref,
    hyper_out,
    relit_out,
    grad_out,
    relit,
    grad,
    ready,
    in_sems,
    image_sems,
    out_sems,
):
    loads = [
        pltpu.make_async_copy(relit_ref, relit, in_sems.at[0]),
        pltpu.make_async_copy(grad_ref, grad, in_sems.at[1]),
    ]
    stores = [
        pltpu.make_async_copy(relit, relit_out, image_sems.at[0]),
        pltpu.make_async_copy(grad, grad_out, image_sems.at[1]),
    ]
    for load in loads:
        load.start()
    codes = codes_ref[...].T
    steps = ready.shape[0]
    width = ready.shape[2]
    pending = []
    for step in range(steps):
        span = pl.ds(step * width, width)
        ready[step] = (
            scale * jnp.dot(codes, summed_ref[:, span], preferred_element_type=jnp.float32)
        ).astype(ready.dtype)
        copy = pltpu.make_async_copy(ready.at[step], hyper_out.at[:, span], out_sems.at[step])
        copy.start()
        pending.append(copy)
        if step in (2, 4):
            loads[step // 2 - 1].wait()
            stores[step // 2 - 1].start()
    for copy in pending + stores:
        copy.wait()


def last_step(scale, codes, summed, relit, feature_grad):
    chips, depth = codes.shape
    own_len = summed.shape[1]
    steps = 9
    anywhere = pl.BlockSpec(memory_space=pl.ANY)
    vmem = pl.BlockSpec(memory_space=pltpu.VMEM)
    return pl.pallas_call(
        functools.partial(last_kernel, scale),
        out_shape=(
            jax.ShapeDtypeStruct((depth, own_len), jnp.bfloat16),
            jax.ShapeDtypeStruct(relit.shape, jnp.bfloat16),
            jax.ShapeDtypeStruct(feature_grad.shape, jnp.bfloat16),
        ),
        in_specs=[vmem, vmem, anywhere, anywhere],
        out_specs=(anywhere,) * 3,
        scratch_shapes=[
            pltpu.VMEM(relit.shape, jnp.bfloat16),
            pltpu.VMEM(feature_grad.shape, jnp.bfloat16),
            pltpu.VMEM((steps, depth, own_len // steps), jnp.bfloat16),
            pltpu.SemaphoreType.DMA((2,)),
            pltpu.SemaphoreType.DMA((2,)),
            pltpu.SemaphoreType.DMA((steps,)),
        ],
        compiler_params=pltpu.CompilerParams(vmem_limit_bytes=VMEM),
    )(codes, summed, relit, feature_grad)


def shards(light_ids, tile_offsets, light_table, hyper_weight, features, upstream_grad):
    channels = features.shape[3]
    scale = 1.0 / math.sqrt(9 * channels)
    lights = lax.axis_size("light")
    own_codes = light_codes(light_ids, tile_offsets, light_table)
    codes, summed, relit, feature_grad = whole(
        scale,
        lights,
        own_codes.astype(jnp.float32).reshape(8, LANES),
        hyper_weight,
        features,
        upstream_grad,
    )
    hyper_grad, relit, feature_grad = last_step(scale, codes, summed, relit, feature_grad)
    return (relit, feature_grad, hyper_grad)


def solution(mesh):
    in_specs = (
        P("light"),
        P("light"),
        P(),
        P(None, ("light", "tex")),
        P("light", "tex", None, None),
        P("light", "tex", None, None),
    )
    out_specs = (
        P("light", "tex", None, None),
        P("light", "tex", None, None),
        P(None, ("light", "tex")),
    )
    return jax.shard_map(shards, mesh=mesh, in_specs=in_specs, out_specs=out_specs, check_vma=False)
```

```python
import functools
import math

import jax
import jax.numpy as jnp
from jax import lax
from jax.experimental import pallas as pl
from jax.experimental.pallas import tpu as pltpu
from jax.sharding import PartitionSpec as P

MESH = pl.DeviceIdType.MESH
LANES = 128
GROUP = 8
LINE = 8
HALO = 4
PIECES = 4
AT_ONCE = 4
CHUNK_ROWS = 18
VMEM = 60 * 1024 * 1024


def light_codes(light_ids, tile_offsets, light_table):
    halfway = light_table.shape[1] // 2
    onehot = (
        light_ids[:, None] == jnp.arange(light_table.shape[0], dtype=jnp.int32)[None, :]
    ).astype(jnp.bfloat16)
    looked = jnp.dot(onehot, light_table, preferred_element_type=jnp.float32)
    rates = jnp.exp(-math.log(1000.0) * jnp.arange(halfway, dtype=jnp.float32) / halfway)
    angles = tile_offsets.astype(jnp.float32)[:, None] * rates[None, :]
    summed = looked + jnp.concatenate([jnp.sin(angles), jnp.cos(angles)], axis=1)
    return (summed * lax.rsqrt(jnp.mean(summed * summed, axis=1, keepdims=True) + 1e-06)).astype(
        jnp.bfloat16
    )


def place():
    light, tex = lax.axis_index("light"), lax.axis_index("tex")
    half, core = tex // 2, tex % 2
    return light, half, core, light * 2 + half


def peer(chip, core):
    return (chip // 2, (chip % 2) * 2 + core)


def line_peer(light, step):
    return light - light % LINE + lax.rem(light % LINE + step, LINE)


def plane_peer(light, step):
    return lax.rem(light + step * LINE, lax.axis_size("light"))


def greet():
    light, tex = lax.axis_index("light"), lax.axis_index("tex")
    lines = lax.axis_size("light") // LINE
    barrier = pltpu.get_barrier_semaphore()

    def signal(target):
        pl.semaphore_signal(barrier, inc=1, device_id=target, device_id_type=MESH)

    for step in range(1, LINE):
        signal((line_peer(light, step), tex))
    for step in range(1, lines):
        signal((plane_peer(light, step), tex))
    for step in range(1, 4):
        signal((light, lax.rem(tex + step, 4)))
    pl.semaphore_wait(barrier, LINE + lines + 1)


def await_bytes(ref, sem):
    pltpu.make_async_copy(ref, ref, sem).wait()


def swap_copies(src, dst, send, recv, start):
    light, half, core, _ = place()
    rows = src.shape[1]
    halo = dst.shape[0] - 2 * rows

    def go(source, target, to_half, to_core, slot, number):
        here = jnp.logical_and(to_half == half, to_core == core)

        @pl.when(here)
        def _():
            if start:
                pltpu.make_async_copy(source, target, recv.at[slot]).start()

        @pl.when(jnp.logical_not(here))
        def _():
            copy = pltpu.make_async_remote_copy(
                src_ref=source,
                dst_ref=target,
                send_sem=send.at[number],
                recv_sem=recv.at[slot],
                device_id=(light, to_half * 2 + to_core),
                device_id_type=MESH,
            )
            if start:
                copy.start()
            else:
                copy.wait_send()

    for to_half in range(2):
        for own in range(2):

            @pl.when(core == own)
            def _():
                go(
                    src.at[to_half],
                    dst.at[pl.ds(own * rows + halo * half, rows)],
                    to_half,
                    half,
                    own,
                    to_half,
                )

        @pl.when(jnp.logical_and(half == 1, core == 0))
        def _():
            go(
                src.at[to_half, pl.ds(0, halo)],
                dst.at[pl.ds(2 * rows, halo)],
                to_half,
                0,
                2,
                2 + to_half,
            )

        @pl.when(jnp.logical_and(half == 0, core == 1))
        def _():
            go(
                src.at[to_half, pl.ds(rows - halo, halo)],
                dst.at[pl.ds(0, halo)],
                to_half,
                1,
                2,
                2 + to_half,
            )


def swap_arrivals(src, dst, recv):
    rows = src.shape[1]
    halo = dst.shape[0] - 2 * rows
    for slot, count in ((0, rows), (1, rows), (2, halo)):
        await_bytes(dst.at[pl.ds(0, count)], recv.at[slot])


def give_back(src, dst, send, recv, piece, start):
    light, half, core, _ = place()
    count = src.shape[0] // PIECES
    to_core, part = piece // (PIECES // 2), piece % (PIECES // 2)
    here = jnp.logical_and(core == half, to_core == core)
    source = src.at[pl.ds(piece * count, count)]
    target = dst.at[half, pl.ds(part * count, count)]
    slot = half * (PIECES // 2) + part

    @pl.when(here)
    def _():
        if start:
            pltpu.make_async_copy(source, target, recv.at[slot]).start()

    @pl.when(jnp.logical_not(here))
    def _():
        copy = pltpu.make_async_remote_copy(
            src_ref=source,
            dst_ref=target,
            send_sem=send.at[piece],
            recv_sem=recv.at[slot],
            device_id=(light, core * 2 + to_core),
            device_id_type=MESH,
        )
        if start:
            copy.start()
        else:
            copy.wait_send()


def whole_kernel(
    scale,
    lights,
    codes_ref,
    hyper_ref,
    feat_ref,
    up_ref,
    codes_out,
    summed_out,
    relit_out,
    grad_out,
    hyper,
    codes,
    table,
    ready,
    blocks,
    wide,
    line,
    kernels,
    feat,
    up,
    feats,
    hidden,
    grads,
    slope,
    total,
    relit,
    grad,
    parts,
    theirs,
    added,
    sums,
    hyper_sem,
    code_send,
    code_recv,
    line_send,
    line_recv,
    own_sem,
    block_send,
    block_recv,
    pass_send,
    pass_recv,
    feat_send,
    feat_recv,
    up_send,
    up_recv,
    core_send,
    core_recv,
    sum_send,
    sum_recv,
    relit_send,
    relit_recv,
    grad_send,
    grad_recv,
):
    light, half, core, me = place()
    chips = 2 * lights
    groups = chips // GROUP
    my_group, my_slot = me // GROUP, me % GROUP
    sibling = (light, half * 2 + 1 - core)
    block_rows = ready.shape[1]
    taps = block_rows // 2
    rows, columns, channels = feat.shape
    own_rows = relit.shape[0]
    frame, own = rows * columns, own_rows * columns
    depth = 9 * channels
    chunk = total.shape[0]
    chunk_rows = chunk // columns
    inner = rows - own_rows
    first_own = pl.multiple_of(core * inner * columns, 16)

    load = pltpu.make_async_copy(hyper_ref, hyper, hyper_sem)
    load.start()
    greet()

    mine = pl.ds(pl.multiple_of(light * 8, 8), 8)
    codes[mine, :] = jnp.concatenate(
        [
            codes_ref[row : row + 1, k * LANES : (k + 1) * LANES]
            for row in range(2)
            for k in range(4)
        ],
        axis=0,
    )
    lines = lights // LINE
    whole_line = pl.ds(pl.multiple_of(light // LINE * (8 * LINE), 8 * LINE), 8 * LINE)

    def code_copy(span, target, send, recv):
        pltpu.make_async_remote_copy(
            src_ref=codes.at[span],
            dst_ref=codes.at[span],
            send_sem=send,
            recv_sem=recv,
            device_id=(target, half * 2 + core),
            device_id_type=MESH,
        ).start()

    for step in range(1, LINE):
        code_copy(mine, line_peer(light, step), code_send, code_recv)
    swap_copies(feat_ref, feat, feat_send, feat_recv, True)
    swap_copies(up_ref, up, up_send, up_recv, True)
    for image in (feats, hidden, grads):
        edge = jnp.zeros((columns, image.shape[1]), image.dtype)
        image[:columns] = edge
        image[frame + columns :] = edge
    near = codes.at[pl.ds(0, 8 * (LINE - 1))]
    far = codes.at[pl.ds(0, 8 * LINE * (lines - 1))]
    await_bytes(near, code_recv)
    for step in range(1, lines):
        code_copy(whole_line, plane_peer(light, step), line_send, line_recv)
    await_bytes(far, line_recv)
    all_codes = jnp.concatenate(
        [codes[pl.ds(k, chips, stride=4), :] for k in range(4)], axis=1
    ).astype(jnp.bfloat16)
    codes_out[...] = all_codes
    load.wait()

    for row in range(taps):
        product = scale * jnp.dot(
            all_codes,
            hyper[:, row * 2 * LANES : (row + 1) * 2 * LANES],
            preferred_element_type=jnp.float32,
        )
        table[pl.ds(row, chips, stride=40), :] = product[:, :LANES]
        table[pl.ds(taps + row, chips, stride=40), :] = product[:, LANES:]

    def narrow(chip):
        ready[chip] = table[pl.ds(pl.multiple_of(chip * 40, 8), block_rows), :].astype(
            jnp.bfloat16
        )

    narrow(me)
    keep = pltpu.make_async_copy(ready.at[me], blocks.at[core, me], own_sem)
    keep.start()

    def send_block(step, _):
        group = lax.rem(my_group + step // GROUP, groups)
        other = group * GROUP + lax.rem(my_slot + step % GROUP, GROUP)
        narrow(other)
        pltpu.make_async_remote_copy(
            src_ref=ready.at[other],
            dst_ref=blocks.at[core, me],
            send_sem=block_send,
            recv_sem=block_recv.at[my_group],
            device_id=peer(other, core),
            device_id_type=MESH,
        ).start()
        return 0

    lax.fori_loop(1, chips, send_block, 0)

    def row_span(row):
        return pl.ds(pl.multiple_of(row * columns, 16), columns)

    def spread(image, row, values):
        span = row_span(row + 1)
        none = jnp.zeros((1, channels), jnp.float32)
        before = jnp.concatenate([none, values[:-1]], axis=0)
        after = jnp.concatenate([values[1:], none], axis=0)
        image[span, :channels] = before.astype(image.dtype)
        image[span, channels : 2 * channels] = values.astype(image.dtype)
        image[span, 2 * channels :] = after.astype(image.dtype)

    swap_arrivals(feat_ref, feat, feat_recv)
    swap_arrivals(up_ref, up, up_recv)

    def place_feats(row, _):
        spread(feats, row, feat[row].astype(jnp.float32))
        return 0

    lax.fori_loop(0, rows, place_feats, 0)

    def to_sibling(group):
        span = blocks.at[core, pl.ds(group * GROUP, GROUP)]
        return pltpu.make_async_remote_copy(
            src_ref=span,
            dst_ref=span,
            send_sem=pass_send.at[group],
            recv_sem=pass_recv.at[group],
            device_id=sibling,
            device_id_type=MESH,
        )

    def gather(group, from_core):
        def block(step, _):
            several = [group * GROUP + step * AT_ONCE + k for k in range(AT_ONCE)]
            for k, chip in enumerate(several):
                line[k] = blocks[from_core, chip].astype(jnp.float32)
            for k, chip in enumerate(several):

                def move(side, _):
                    wide[side, pl.ds((2 * chip + from_core) * taps, taps), :] = line[
                        k, pl.ds(side * taps, taps), :
                    ]
                    return 0

                lax.fori_loop(0, 2, move, 0)
            return 0

        lax.fori_loop(0, GROUP // AT_ONCE, block, 0)

    def end_group(group):
        to_sibling(group).wait_recv()
        gather(group, 1 - core)
        count = 2 * GROUP * taps
        span = pl.ds(pl.multiple_of(group * count, 16), count)
        kernels[span, :LANES] = wide[0, span, :].astype(jnp.bfloat16)
        kernels[span, LANES:] = wide[1, span, :].astype(jnp.bfloat16)

    keep.wait()
    await_bytes(blocks.at[core, pl.ds(0, GROUP - 1)], block_recv.at[my_group])
    to_sibling(my_group).start()
    gather(my_group, core)

    def take_group(step, _):
        group = lax.rem(my_group + groups - step, groups)
        await_bytes(blocks.at[core, pl.ds(0, GROUP)], block_recv.at[group])
        to_sibling(group).start()
        gather(group, core)
        end_group(lax.rem(group + 1, groups))
        return 0

    lax.fori_loop(1, groups, take_group, 0)
    end_group(lax.rem(my_group + 1, groups))

    def conv(image, base, start):
        out = None
        for tap in range(3):
            span = pl.ds(pl.multiple_of(start + tap * columns, 16), chunk)
            piece = jnp.dot(
                image[span, :],
                kernels[base + tap * 3 * channels : base + (tap + 1) * 3 * channels, :],
                preferred_element_type=jnp.float32,
            )
            out = piece if out is None else out + piece
        total[...] = out

    def conv_back(image, base, start, count):
        out = None
        for row_tap in range(3):
            span = pl.ds(pl.multiple_of(start + (2 - row_tap) * columns, 16), count)
            for col_tap in range(3):
                at = base + (row_tap * 3 + col_tap) * channels
                piece = lax.dot_general(
                    image[span, (2 - col_tap) * channels : (3 - col_tap) * channels],
                    kernels[at : at + channels, :],
                    (((1,), (1,)), ((), ())),
                    preferred_element_type=jnp.float32,
                )
                out = piece if out is None else out + piece
        total[:count] = out

    def each_chunk(compute, finish_row):
        def do_chunk(step, _):
            compute(step * chunk)

            def do_row(row, _):
                finish_row(step * chunk_rows + row, total[row_span(row), :])
                return 0

            return lax.fori_loop(0, chunk_rows, do_row, 0)

        lax.fori_loop(0, frame // chunk, do_chunk, 0)

    def store_own(ref, row, values):
        local = row - core * inner

        @pl.when(jnp.logical_and(local >= 0, local < own_rows))
        def _():
            ref[local] = values.astype(ref.dtype)

    def end_first(row, pre):
        sig = jax.nn.sigmoid(pre)
        slope[row_span(row), :] = sig * (1.0 + pre * (1.0 - sig))
        spread(hidden, row, pre * sig)

    def end_second(row, pre):
        sig = jax.nn.sigmoid(pre)
        store_own(relit, row, pre * sig)
        spread(grads, row, up[row].astype(jnp.float32) * (sig * (1.0 + pre * (1.0 - sig))))

    def kernel_grad(image, base):
        upstream = grads[pl.ds(first_own + columns, own), channels : 2 * channels].T

        def do_tap(tap, _):
            span = pl.ds(pl.multiple_of(first_own + tap * columns, 16), own)
            for col_tap in range(3):
                piece = jnp.dot(
                    upstream,
                    image[span, col_tap * channels : (col_tap + 1) * channels],
                    preferred_element_type=jnp.float32,
                )
                at = pl.multiple_of(base + (tap * 3 + col_tap) * channels, channels)
                wide[0, pl.ds(at, channels), :] = piece[:LANES].T
                wide[1, pl.ds(at, channels), :] = piece[LANES:].T
            return 0

        lax.fori_loop(0, 3, do_tap, 0)

    def end_grad(row, back):
        slope[row_span(row), :] = slope[row_span(row), :] * back

    def part_copy(group):
        return pltpu.make_async_remote_copy(
            src_ref=parts.at[pl.ds(group * GROUP, GROUP)],
            dst_ref=theirs.at[pl.ds(group * GROUP, GROUP)],
            send_sem=core_send.at[group],
            recv_sem=core_recv.at[group],
            device_id=sibling,
            device_id_type=MESH,
        )

    def pick(slot, owner):
        for side in range(2):
            line[slot, side * taps : (side + 1) * taps, :] = wide[
                side, pl.ds(owner * taps, taps), :
            ]

    def send_sum(other):
        @pl.when(other == me)
        def _():
            pltpu.make_async_copy(added.at[me], sums.at[me], own_sem).start()

        @pl.when(other != me)
        def _():
            pltpu.make_async_remote_copy(
                src_ref=added.at[other],
                dst_ref=sums.at[me],
                send_sem=sum_send,
                recv_sem=sum_recv.at[my_group],
                device_id=peer(other, core),
                device_id_type=MESH,
            ).start()

    def send_grad(first, between):
        some = groups // 2

        def group_at(step):
            return first + lax.rem(my_group + step, some)

        def share(step):
            group = group_at(step)

            def block(step, _):
                several = [group * GROUP + step * AT_ONCE + k for k in range(AT_ONCE)]
                for k, chip in enumerate(several):
                    pick(k, 2 * chip + 1 - core)
                for k, chip in enumerate(several):
                    parts[chip] = line[k].astype(parts.dtype)
                return 0

            lax.fori_loop(0, GROUP // AT_ONCE, block, 0)
            part_copy(group).start()

        def add(step):
            group = group_at(step)
            part_copy(group).wait_recv()

            def block(step, _):
                several = [
                    group * GROUP + lax.rem(my_slot + step * AT_ONCE + k, GROUP)
                    for k in range(AT_ONCE)
                ]
                for k, other in enumerate(several):
                    pick(k, 2 * other + core)
                for k, other in enumerate(several):
                    added[other] = (line[k] + theirs[other].astype(jnp.float32)).astype(
                        added.dtype
                    )
                for other in several:
                    send_sum(other)
                return 0

            lax.fori_loop(0, GROUP // AT_ONCE, block, 0)

        share(0)

        def both(step, _):
            share(step)
            add(step - 1)
            between(step - 1)
            return 0

        lax.fori_loop(1, some, both, 0)
        add(some - 1)
        between(some - 1)

    def feature_piece(step):
        every = groups // 2 // PIECES

        @pl.when(step % every == every - 1)
        def _():
            feature_rows(step // every)

    def feature_rows(piece):
        count = own // PIECES
        conv_back(grads, 0, pl.multiple_of(first_own + piece * count, 16), count)

        def store(row, _):
            grad[piece * (own_rows // PIECES) + row] = total[row_span(row), :].astype(grad.dtype)
            return 0

        lax.fori_loop(0, own_rows // PIECES, store, 0)
        give_back(grad, grad_out, grad_send, grad_recv, piece, True)

    def relit_piece(piece, _):
        give_back(relit, relit_out, relit_send, relit_recv, piece, True)
        return 0

    each_chunk(lambda start: conv(feats, 0, start), end_first)
    each_chunk(lambda start: conv(hidden, depth, start), end_second)
    lax.fori_loop(0, PIECES, relit_piece, 0)
    kernel_grad(hidden, depth)
    send_grad(groups // 2, lambda step: None)
    each_chunk(lambda start: conv_back(grads, depth, start, chunk), end_grad)

    def place_grad(row, _):
        spread(grads, row, slope[row_span(row), :])
        return 0

    lax.fori_loop(0, rows, place_grad, 0)
    kernel_grad(feats, 0)
    send_grad(0, feature_piece)

    def finish(group, _):
        to_sibling(group).wait_send()
        part_copy(group).wait_send()
        return 0

    lax.fori_loop(0, groups, finish, 0)
    await_bytes(ready.at[pl.ds(0, chips - 1)], block_send)
    await_bytes(near, code_send)
    await_bytes(far, line_send)
    swap_copies(feat_ref, feat, feat_send, feat_recv, False)
    swap_copies(up_ref, up, up_send, up_recv, False)

    def finish_piece(piece, _):
        give_back(relit, relit_out, relit_send, relit_recv, piece, False)
        give_back(grad, grad_out, grad_send, grad_recv, piece, False)
        return 0

    lax.fori_loop(0, PIECES, finish_piece, 0)

    def widen(group):
        def block(slot, _):
            chip = group * GROUP + slot
            table[pl.ds(pl.multiple_of(chip * 40, 8), block_rows), :] = sums[chip].astype(
                jnp.float32
            )
            return 0

        lax.fori_loop(0, GROUP, block, 0)

    pltpu.make_async_copy(added.at[me], sums.at[me], own_sem).wait()
    await_bytes(sums.at[pl.ds(0, GROUP - 1)], sum_recv.at[my_group])
    widen(my_group)

    def take_sums(step, _):
        group = lax.rem(my_group + groups - step, groups)
        await_bytes(sums.at[pl.ds(0, GROUP)], sum_recv.at[group])
        widen(group)
        return 0

    lax.fori_loop(1, groups, take_sums, 0)
    for row in range(taps):
        for side in range(2):
            at = (2 * row + side) * LANES
            summed_out[:, at : at + LANES] = table[
                pl.ds(side * taps + row, chips, stride=40), :
            ].astype(summed_out.dtype)
    await_bytes(added.at[pl.ds(0, chips - 1)], sum_send)
    piece_rows = own_rows // PIECES
    for slot in range(PIECES):
        await_bytes(relit_out.at[0, pl.ds(0, piece_rows)], relit_recv.at[slot])
        await_bytes(grad_out.at[0, pl.ds(0, piece_rows)], grad_recv.at[slot])


def whole(scale, lights, codes, hyper_weight, features, upstream):
    chips = 2 * lights
    groups = chips // GROUP
    width, own_len = hyper_weight.shape
    block_rows = own_len // LANES
    _, rows_dev, columns, channels = features.shape
    depth = 9 * channels
    own_rows = 2 * rows_dev
    rows = own_rows + HALO
    frame = rows * columns
    dma = pltpu.SemaphoreType.DMA
    anywhere = pl.BlockSpec(memory_space=pl.ANY)
    vmem = pl.BlockSpec(memory_space=pltpu.VMEM)
    image = jax.ShapeDtypeStruct(features.shape, jnp.bfloat16)
    block = pltpu.VMEM((chips, block_rows, LANES), jnp.bfloat16)
    shifted = pltpu.VMEM((frame + 2 * columns, 3 * channels), jnp.bfloat16)
    return pl.pallas_call(
        functools.partial(whole_kernel, scale, lights),
        out_shape=(
            jax.ShapeDtypeStruct((chips, width), jnp.bfloat16),
            jax.ShapeDtypeStruct((chips, own_len), jnp.bfloat16),
            image,
            image,
        ),
        in_specs=[vmem, anywhere, anywhere, anywhere],
        out_specs=(vmem, vmem, anywhere, anywhere),
        scratch_shapes=[
            pltpu.VMEM((width, own_len), jnp.bfloat16),
            pltpu.VMEM((8 * lights, LANES), jnp.float32),
            pltpu.VMEM((chips * 40, LANES), jnp.float32),
            block,
            pltpu.VMEM((2, chips, block_rows, LANES), jnp.bfloat16),
            pltpu.VMEM((2, 2 * depth, LANES), jnp.float32),
            pltpu.VMEM((AT_ONCE, block_rows, LANES), jnp.float32),
            pltpu.VMEM((2 * depth, channels), jnp.bfloat16),
            pltpu.VMEM((rows, columns, channels), jnp.bfloat16),
            pltpu.VMEM((rows, columns, channels), jnp.bfloat16),
            shifted,
            shifted,
            shifted,
            pltpu.VMEM((frame, channels), jnp.float32),
            pltpu.VMEM((CHUNK_ROWS * columns, channels), jnp.float32),
            pltpu.VMEM((own_rows, columns, channels), jnp.bfloat16),
            pltpu.VMEM((own_rows, columns, channels), jnp.bfloat16),
            block,
            block,
            block,
            block,
            dma,
            dma,
            dma,
            dma,
            dma,
            dma,
            dma,
            dma((groups,)),
            dma((groups,)),
            dma((groups,)),
            dma((4,)),
            dma((3,)),
            dma((4,)),
            dma((3,)),
            dma((groups,)),
            dma((groups,)),
            dma,
            dma((groups,)),
            dma((PIECES,)),
            dma((PIECES,)),
            dma((PIECES,)),
            dma((PIECES,)),
        ],
        compiler_params=pltpu.CompilerParams(
            has_side_effects=True, collective_id=0, vmem_limit_bytes=VMEM
        ),
    )(codes, hyper_weight, features, upstream)


def last_kernel(
    scale,
    codes_ref,
    summed_ref,
    relit_ref,
    grad_ref,
    hyper_out,
    relit_out,
    grad_out,
    relit,
    grad,
    ready,
    in_sems,
    image_sems,
    out_sems,
):
    loads = [
        pltpu.make_async_copy(relit_ref, relit, in_sems.at[0]),
        pltpu.make_async_copy(grad_ref, grad, in_sems.at[1]),
    ]
    stores = [
        pltpu.make_async_copy(relit, relit_out, image_sems.at[0]),
        pltpu.make_async_copy(grad, grad_out, image_sems.at[1]),
    ]
    for load in loads:
        load.start()
    codes = codes_ref[...].T
    steps = ready.shape[0]
    width = ready.shape[2]
    pending = []
    for step in range(steps):
        span = pl.ds(step * width, width)
        ready[step] = (
            scale * jnp.dot(codes, summed_ref[:, span], preferred_element_type=jnp.float32)
        ).astype(ready.dtype)
        copy = pltpu.make_async_copy(ready.at[step], hyper_out.at[:, span], out_sems.at[step])
        copy.start()
        pending.append(copy)
        if step in (2, 4):
            loads[step // 2 - 1].wait()
            stores[step // 2 - 1].start()
    for copy in pending + stores:
        copy.wait()


def last_step(scale, codes, summed, relit, feature_grad):
    chips, depth = codes.shape
    own_len = summed.shape[1]
    steps = 9
    anywhere = pl.BlockSpec(memory_space=pl.ANY)
    vmem = pl.BlockSpec(memory_space=pltpu.VMEM)
    return pl.pallas_call(
        functools.partial(last_kernel, scale),
        out_shape=(
            jax.ShapeDtypeStruct((depth, own_len), jnp.bfloat16),
            jax.ShapeDtypeStruct(relit.shape, jnp.bfloat16),
            jax.ShapeDtypeStruct(feature_grad.shape, jnp.bfloat16),
        ),
        in_specs=[vmem, vmem, anywhere, anywhere],
        out_specs=(anywhere,) * 3,
        scratch_shapes=[
            pltpu.VMEM(relit.shape, jnp.bfloat16),
            pltpu.VMEM(feature_grad.shape, jnp.bfloat16),
            pltpu.VMEM((steps, depth, own_len // steps), jnp.bfloat16),
            pltpu.SemaphoreType.DMA((2,)),
            pltpu.SemaphoreType.DMA((2,)),
            pltpu.SemaphoreType.DMA((steps,)),
        ],
        compiler_params=pltpu.CompilerParams(vmem_limit_bytes=VMEM),
    )(codes, summed, relit, feature_grad)


def shards(light_ids, tile_offsets, light_table, hyper_weight, features, upstream_grad):
    channels = features.shape[3]
    scale = 1.0 / math.sqrt(9 * channels)
    lights = lax.axis_size("light")
    own_codes = light_codes(light_ids, tile_offsets, light_table)
    codes, summed, relit, feature_grad = whole(
        scale,
        lights,
        own_codes.astype(jnp.float32),
        hyper_weight,
        features,
        upstream_grad,
    )
    hyper_grad, relit, feature_grad = last_step(scale, codes, summed, relit, feature_grad)
    return (relit, feature_grad, hyper_grad)


def solution(mesh):
    in_specs = (
        P("light"),
        P("light"),
        P(),
        P(None, ("light", "tex")),
        P("light", "tex", None, None),
        P("light", "tex", None, None),
    )
    out_specs = (
        P("light", "tex", None, None),
        P("light", "tex", None, None),
        P(None, ("light", "tex")),
    )
    return jax.shard_map(shards, mesh=mesh, in_specs=in_specs, out_specs=out_specs, check_vma=False)
```

```python
import functools
import math

import jax
import jax.numpy as jnp
from jax import lax
from jax.experimental import pallas as pl
from jax.experimental.pallas import tpu as pltpu
from jax.sharding import PartitionSpec as P

MESH = pl.DeviceIdType.MESH
LANES = 128
GROUP = 16
LINE = 8
HALO = 4
PIECES = 4
AT_ONCE = 4
CHUNK_ROWS = 18
VMEM = 60 * 1024 * 1024


def light_codes(light_ids, tile_offsets, light_table):
    halfway = light_table.shape[1] // 2
    onehot = (
        light_ids[:, None] == jnp.arange(light_table.shape[0], dtype=jnp.int32)[None, :]
    ).astype(jnp.bfloat16)
    looked = jnp.dot(onehot, light_table, preferred_element_type=jnp.float32)
    rates = jnp.exp(-math.log(1000.0) * jnp.arange(halfway, dtype=jnp.float32) / halfway)
    angles = tile_offsets.astype(jnp.float32)[:, None] * rates[None, :]
    summed = looked + jnp.concatenate([jnp.sin(angles), jnp.cos(angles)], axis=1)
    return (summed * lax.rsqrt(jnp.mean(summed * summed, axis=1, keepdims=True) + 1e-06)).astype(
        jnp.bfloat16
    )


def place():
    light, tex = lax.axis_index("light"), lax.axis_index("tex")
    half, core = tex // 2, tex % 2
    return light, half, core, light * 2 + half


def peer(chip, core):
    return (chip // 2, (chip % 2) * 2 + core)


def line_peer(light, step):
    return light - light % LINE + lax.rem(light % LINE + step, LINE)


def plane_peer(light, step):
    return lax.rem(light + step * LINE, lax.axis_size("light"))


def greet():
    light, tex = lax.axis_index("light"), lax.axis_index("tex")
    lines = lax.axis_size("light") // LINE
    barrier = pltpu.get_barrier_semaphore()

    def signal(target):
        pl.semaphore_signal(barrier, inc=1, device_id=target, device_id_type=MESH)

    for step in range(1, LINE):
        signal((line_peer(light, step), tex))
    for step in range(1, lines):
        signal((plane_peer(light, step), tex))
    for step in range(1, 4):
        signal((light, lax.rem(tex + step, 4)))
    pl.semaphore_wait(barrier, LINE + lines + 1)


def await_bytes(ref, sem):
    pltpu.make_async_copy(ref, ref, sem).wait()


def swap_copies(src, dst, send, recv, start):
    light, half, core, _ = place()
    rows = src.shape[1]
    halo = dst.shape[0] - 2 * rows

    def go(source, target, to_half, to_core, slot, number):
        here = jnp.logical_and(to_half == half, to_core == core)

        @pl.when(here)
        def _():
            if start:
                pltpu.make_async_copy(source, target, recv.at[slot]).start()

        @pl.when(jnp.logical_not(here))
        def _():
            copy = pltpu.make_async_remote_copy(
                src_ref=source,
                dst_ref=target,
                send_sem=send.at[number],
                recv_sem=recv.at[slot],
                device_id=(light, to_half * 2 + to_core),
                device_id_type=MESH,
            )
            if start:
                copy.start()
            else:
                copy.wait_send()

    for to_half in range(2):
        for own in range(2):

            @pl.when(core == own)
            def _():
                go(
                    src.at[to_half],
                    dst.at[pl.ds(own * rows + halo * half, rows)],
                    to_half,
                    half,
                    own,
                    to_half,
                )

        @pl.when(jnp.logical_and(half == 1, core == 0))
        def _():
            go(
                src.at[to_half, pl.ds(0, halo)],
                dst.at[pl.ds(2 * rows, halo)],
                to_half,
                0,
                2,
                2 + to_half,
            )

        @pl.when(jnp.logical_and(half == 0, core == 1))
        def _():
            go(
                src.at[to_half, pl.ds(rows - halo, halo)],
                dst.at[pl.ds(0, halo)],
                to_half,
                1,
                2,
                2 + to_half,
            )


def swap_arrivals(src, dst, recv):
    rows = src.shape[1]
    halo = dst.shape[0] - 2 * rows
    for slot, count in ((0, rows), (1, rows), (2, halo)):
        await_bytes(dst.at[pl.ds(0, count)], recv.at[slot])


def give_back(src, dst, send, recv, piece, start):
    light, half, core, _ = place()
    count = src.shape[0] // PIECES
    to_core, part = piece // (PIECES // 2), piece % (PIECES // 2)
    here = jnp.logical_and(core == half, to_core == core)
    source = src.at[pl.ds(piece * count, count)]
    target = dst.at[half, pl.ds(part * count, count)]
    slot = half * (PIECES // 2) + part

    @pl.when(here)
    def _():
        if start:
            pltpu.make_async_copy(source, target, recv.at[slot]).start()

    @pl.when(jnp.logical_not(here))
    def _():
        copy = pltpu.make_async_remote_copy(
            src_ref=source,
            dst_ref=target,
            send_sem=send.at[piece],
            recv_sem=recv.at[slot],
            device_id=(light, core * 2 + to_core),
            device_id_type=MESH,
        )
        if start:
            copy.start()
        else:
            copy.wait_send()


def whole_kernel(
    scale,
    lights,
    codes_ref,
    hyper_ref,
    feat_ref,
    up_ref,
    codes_out,
    summed_out,
    relit_out,
    grad_out,
    hyper,
    codes,
    table,
    ready,
    blocks,
    wide,
    line,
    kernels,
    feat,
    up,
    feats,
    hidden,
    grads,
    slope,
    total,
    relit,
    grad,
    parts,
    theirs,
    added,
    sums,
    hyper_sem,
    code_send,
    code_recv,
    line_send,
    line_recv,
    own_sem,
    block_send,
    block_recv,
    pass_send,
    pass_recv,
    feat_send,
    feat_recv,
    up_send,
    up_recv,
    core_send,
    core_recv,
    sum_send,
    sum_recv,
    relit_send,
    relit_recv,
    grad_send,
    grad_recv,
):
    light, half, core, me = place()
    chips = 2 * lights
    groups = chips // GROUP
    my_group, my_slot = me // GROUP, me % GROUP
    sibling = (light, half * 2 + 1 - core)
    block_rows = ready.shape[1]
    taps = block_rows // 2
    rows, columns, channels = feat.shape
    own_rows = relit.shape[0]
    frame, own = rows * columns, own_rows * columns
    depth = 9 * channels
    chunk = total.shape[0]
    chunk_rows = chunk // columns
    inner = rows - own_rows
    first_own = pl.multiple_of(core * inner * columns, 16)

    load = pltpu.make_async_copy(hyper_ref, hyper, hyper_sem)
    load.start()
    greet()

    mine = pl.ds(pl.multiple_of(light * 8, 8), 8)
    codes[mine, :] = jnp.concatenate(
        [
            codes_ref[row : row + 1, k * LANES : (k + 1) * LANES]
            for row in range(2)
            for k in range(4)
        ],
        axis=0,
    )
    lines = lights // LINE
    whole_line = pl.ds(pl.multiple_of(light // LINE * (8 * LINE), 8 * LINE), 8 * LINE)

    def code_copy(span, target, send, recv):
        pltpu.make_async_remote_copy(
            src_ref=codes.at[span],
            dst_ref=codes.at[span],
            send_sem=send,
            recv_sem=recv,
            device_id=(target, half * 2 + core),
            device_id_type=MESH,
        ).start()

    for step in range(1, LINE):
        code_copy(mine, line_peer(light, step), code_send, code_recv)
    swap_copies(feat_ref, feat, feat_send, feat_recv, True)
    swap_copies(up_ref, up, up_send, up_recv, True)
    for image in (feats, hidden, grads):
        edge = jnp.zeros((columns, image.shape[1]), image.dtype)
        image[:columns] = edge
        image[frame + columns :] = edge
    near = codes.at[pl.ds(0, 8 * (LINE - 1))]
    far = codes.at[pl.ds(0, 8 * LINE * (lines - 1))]
    await_bytes(near, code_recv)
    for step in range(1, lines):
        code_copy(whole_line, plane_peer(light, step), line_send, line_recv)
    await_bytes(far, line_recv)
    all_codes = jnp.concatenate(
        [codes[pl.ds(k, chips, stride=4), :] for k in range(4)], axis=1
    ).astype(jnp.bfloat16)
    codes_out[...] = all_codes
    load.wait()

    for row in range(taps):
        product = scale * jnp.dot(
            all_codes,
            hyper[:, row * 2 * LANES : (row + 1) * 2 * LANES],
            preferred_element_type=jnp.float32,
        )
        table[pl.ds(row, chips, stride=40), :] = product[:, :LANES]
        table[pl.ds(taps + row, chips, stride=40), :] = product[:, LANES:]

    def narrow(chip):
        ready[chip] = table[pl.ds(pl.multiple_of(chip * 40, 8), block_rows), :].astype(
            jnp.bfloat16
        )

    narrow(me)
    keep = pltpu.make_async_copy(ready.at[me], blocks.at[core, me], own_sem)
    keep.start()

    def send_block(step, _):
        group = lax.rem(my_group + step // GROUP, groups)
        other = group * GROUP + lax.rem(my_slot + step % GROUP, GROUP)
        narrow(other)
        pltpu.make_async_remote_copy(
            src_ref=ready.at[other],
            dst_ref=blocks.at[core, me],
            send_sem=block_send,
            recv_sem=block_recv.at[my_group],
            device_id=peer(other, core),
            device_id_type=MESH,
        ).start()
        return 0

    lax.fori_loop(1, chips, send_block, 0)

    def row_span(row):
        return pl.ds(pl.multiple_of(row * columns, 16), columns)

    def spread(image, row, values):
        span = row_span(row + 1)
        none = jnp.zeros((1, channels), jnp.float32)
        before = jnp.concatenate([none, values[:-1]], axis=0)
        after = jnp.concatenate([values[1:], none], axis=0)
        image[span, :channels] = before.astype(image.dtype)
        image[span, channels : 2 * channels] = values.astype(image.dtype)
        image[span, 2 * channels :] = after.astype(image.dtype)

    swap_arrivals(feat_ref, feat, feat_recv)
    swap_arrivals(up_ref, up, up_recv)

    def place_feats(row, _):
        spread(feats, row, feat[row].astype(jnp.float32))
        return 0

    lax.fori_loop(0, rows, place_feats, 0)

    def to_sibling(group):
        span = blocks.at[core, pl.ds(group * GROUP, GROUP)]
        return pltpu.make_async_remote_copy(
            src_ref=span,
            dst_ref=span,
            send_sem=pass_send.at[group],
            recv_sem=pass_recv.at[group],
            device_id=sibling,
            device_id_type=MESH,
        )

    def gather(group, from_core):
        def block(step, _):
            several = [group * GROUP + step * AT_ONCE + k for k in range(AT_ONCE)]
            for k, chip in enumerate(several):
                line[k] = blocks[from_core, chip].astype(jnp.float32)
            for k, chip in enumerate(several):

                def move(side, _):
                    wide[side, pl.ds((2 * chip + from_core) * taps, taps), :] = line[
                        k, pl.ds(side * taps, taps), :
                    ]
                    return 0

                lax.fori_loop(0, 2, move, 0)
            return 0

        lax.fori_loop(0, GROUP // AT_ONCE, block, 0)

    def end_group(group):
        to_sibling(group).wait_recv()
        gather(group, 1 - core)
        count = 2 * GROUP * taps
        span = pl.ds(pl.multiple_of(group * count, 16), count)
        kernels[span, :LANES] = wide[0, span, :].astype(jnp.bfloat16)
        kernels[span, LANES:] = wide[1, span, :].astype(jnp.bfloat16)

    keep.wait()
    await_bytes(blocks.at[core, pl.ds(0, GROUP - 1)], block_recv.at[my_group])
    to_sibling(my_group).start()
    gather(my_group, core)

    def take_group(step, _):
        group = lax.rem(my_group + groups - step, groups)
        await_bytes(blocks.at[core, pl.ds(0, GROUP)], block_recv.at[group])
        to_sibling(group).start()
        gather(group, core)
        end_group(lax.rem(group + 1, groups))
        return 0

    lax.fori_loop(1, groups, take_group, 0)
    end_group(lax.rem(my_group + 1, groups))

    def conv(image, base, start):
        out = None
        for tap in range(3):
            span = pl.ds(pl.multiple_of(start + tap * columns, 16), chunk)
            piece = jnp.dot(
                image[span, :],
                kernels[base + tap * 3 * channels : base + (tap + 1) * 3 * channels, :],
                preferred_element_type=jnp.float32,
            )
            out = piece if out is None else out + piece
        total[...] = out

    def conv_back(image, base, start, count):
        out = None
        for row_tap in range(3):
            span = pl.ds(pl.multiple_of(start + (2 - row_tap) * columns, 16), count)
            for col_tap in range(3):
                at = base + (row_tap * 3 + col_tap) * channels
                piece = lax.dot_general(
                    image[span, (2 - col_tap) * channels : (3 - col_tap) * channels],
                    kernels[at : at + channels, :],
                    (((1,), (1,)), ((), ())),
                    preferred_element_type=jnp.float32,
                )
                out = piece if out is None else out + piece
        total[:count] = out

    def each_chunk(compute, finish_row):
        def do_chunk(step, _):
            compute(step * chunk)

            def do_row(row, _):
                finish_row(step * chunk_rows + row, total[row_span(row), :])
                return 0

            return lax.fori_loop(0, chunk_rows, do_row, 0)

        lax.fori_loop(0, frame // chunk, do_chunk, 0)

    def store_own(ref, row, values):
        local = row - core * inner

        @pl.when(jnp.logical_and(local >= 0, local < own_rows))
        def _():
            ref[local] = values.astype(ref.dtype)

    def end_first(row, pre):
        sig = jax.nn.sigmoid(pre)
        slope[row_span(row), :] = sig * (1.0 + pre * (1.0 - sig))
        spread(hidden, row, pre * sig)

    def end_second(row, pre):
        sig = jax.nn.sigmoid(pre)
        store_own(relit, row, pre * sig)
        spread(grads, row, up[row].astype(jnp.float32) * (sig * (1.0 + pre * (1.0 - sig))))

    def kernel_grad(image, base):
        upstream = grads[pl.ds(first_own + columns, own), channels : 2 * channels].T

        def do_tap(tap, _):
            span = pl.ds(pl.multiple_of(first_own + tap * columns, 16), own)
            for col_tap in range(3):
                piece = jnp.dot(
                    upstream,
                    image[span, col_tap * channels : (col_tap + 1) * channels],
                    preferred_element_type=jnp.float32,
                )
                at = pl.multiple_of(base + (tap * 3 + col_tap) * channels, channels)
                wide[0, pl.ds(at, channels), :] = piece[:LANES].T
                wide[1, pl.ds(at, channels), :] = piece[LANES:].T
            return 0

        lax.fori_loop(0, 3, do_tap, 0)

    def end_grad(row, back):
        slope[row_span(row), :] = slope[row_span(row), :] * back

    def part_copy(group):
        return pltpu.make_async_remote_copy(
            src_ref=parts.at[pl.ds(group * GROUP, GROUP)],
            dst_ref=theirs.at[pl.ds(group * GROUP, GROUP)],
            send_sem=core_send.at[group],
            recv_sem=core_recv.at[group],
            device_id=sibling,
            device_id_type=MESH,
        )

    def pick(slot, owner):
        for side in range(2):
            line[slot, side * taps : (side + 1) * taps, :] = wide[
                side, pl.ds(owner * taps, taps), :
            ]

    def send_sum(other):
        @pl.when(other == me)
        def _():
            pltpu.make_async_copy(added.at[me], sums.at[me], own_sem).start()

        @pl.when(other != me)
        def _():
            pltpu.make_async_remote_copy(
                src_ref=added.at[other],
                dst_ref=sums.at[me],
                send_sem=sum_send,
                recv_sem=sum_recv.at[my_group],
                device_id=peer(other, core),
                device_id_type=MESH,
            ).start()

    def send_grad(first, between):
        some = groups // 2

        def group_at(step):
            return first + lax.rem(my_group + step, some)

        def share(step):
            group = group_at(step)

            def block(step, _):
                several = [group * GROUP + step * AT_ONCE + k for k in range(AT_ONCE)]
                for k, chip in enumerate(several):
                    pick(k, 2 * chip + 1 - core)
                for k, chip in enumerate(several):
                    parts[chip] = line[k].astype(parts.dtype)
                return 0

            lax.fori_loop(0, GROUP // AT_ONCE, block, 0)
            part_copy(group).start()

        def add(step):
            group = group_at(step)
            part_copy(group).wait_recv()

            def block(step, _):
                several = [
                    group * GROUP + lax.rem(my_slot + step * AT_ONCE + k, GROUP)
                    for k in range(AT_ONCE)
                ]
                for k, other in enumerate(several):
                    pick(k, 2 * other + core)
                for k, other in enumerate(several):
                    added[other] = (line[k] + theirs[other].astype(jnp.float32)).astype(
                        added.dtype
                    )
                for other in several:
                    send_sum(other)
                return 0

            lax.fori_loop(0, GROUP // AT_ONCE, block, 0)

        share(0)

        def both(step, _):
            share(step)
            add(step - 1)
            between(step - 1)
            return 0

        lax.fori_loop(1, some, both, 0)
        add(some - 1)
        between(some - 1)

    def feature_piece(step):
        every = groups // 2 // PIECES

        @pl.when(step % every == every - 1)
        def _():
            feature_rows(step // every)

    def feature_rows(piece):
        count = own // PIECES
        conv_back(grads, 0, pl.multiple_of(first_own + piece * count, 16), count)

        def store(row, _):
            grad[piece * (own_rows // PIECES) + row] = total[row_span(row), :].astype(grad.dtype)
            return 0

        lax.fori_loop(0, own_rows // PIECES, store, 0)
        give_back(grad, grad_out, grad_send, grad_recv, piece, True)

    def relit_piece(piece, _):
        give_back(relit, relit_out, relit_send, relit_recv, piece, True)
        return 0

    each_chunk(lambda start: conv(feats, 0, start), end_first)
    each_chunk(lambda start: conv(hidden, depth, start), end_second)
    lax.fori_loop(0, PIECES, relit_piece, 0)
    kernel_grad(hidden, depth)
    send_grad(groups // 2, lambda step: None)
    each_chunk(lambda start: conv_back(grads, depth, start, chunk), end_grad)

    def place_grad(row, _):
        spread(grads, row, slope[row_span(row), :])
        return 0

    lax.fori_loop(0, rows, place_grad, 0)
    kernel_grad(feats, 0)
    send_grad(0, feature_piece)

    def finish(group, _):
        to_sibling(group).wait_send()
        part_copy(group).wait_send()
        return 0

    lax.fori_loop(0, groups, finish, 0)
    await_bytes(ready.at[pl.ds(0, chips - 1)], block_send)
    await_bytes(near, code_send)
    await_bytes(far, line_send)
    swap_copies(feat_ref, feat, feat_send, feat_recv, False)
    swap_copies(up_ref, up, up_send, up_recv, False)

    def finish_piece(piece, _):
        give_back(relit, relit_out, relit_send, relit_recv, piece, False)
        give_back(grad, grad_out, grad_send, grad_recv, piece, False)
        return 0

    lax.fori_loop(0, PIECES, finish_piece, 0)

    def widen(group):
        def block(slot, _):
            chip = group * GROUP + slot
            table[pl.ds(pl.multiple_of(chip * 40, 8), block_rows), :] = sums[chip].astype(
                jnp.float32
            )
            return 0

        lax.fori_loop(0, GROUP, block, 0)

    pltpu.make_async_copy(added.at[me], sums.at[me], own_sem).wait()
    await_bytes(sums.at[pl.ds(0, GROUP - 1)], sum_recv.at[my_group])
    widen(my_group)

    def take_sums(step, _):
        group = lax.rem(my_group + groups - step, groups)
        await_bytes(sums.at[pl.ds(0, GROUP)], sum_recv.at[group])
        widen(group)
        return 0

    lax.fori_loop(1, groups, take_sums, 0)
    for row in range(taps):
        for side in range(2):
            at = (2 * row + side) * LANES
            summed_out[:, at : at + LANES] = table[
                pl.ds(side * taps + row, chips, stride=40), :
            ].astype(summed_out.dtype)
    await_bytes(added.at[pl.ds(0, chips - 1)], sum_send)
    piece_rows = own_rows // PIECES
    for slot in range(PIECES):
        await_bytes(relit_out.at[0, pl.ds(0, piece_rows)], relit_recv.at[slot])
        await_bytes(grad_out.at[0, pl.ds(0, piece_rows)], grad_recv.at[slot])


def whole(scale, lights, codes, hyper_weight, features, upstream):
    chips = 2 * lights
    groups = chips // GROUP
    width, own_len = hyper_weight.shape
    block_rows = own_len // LANES
    _, rows_dev, columns, channels = features.shape
    depth = 9 * channels
    own_rows = 2 * rows_dev
    rows = own_rows + HALO
    frame = rows * columns
    dma = pltpu.SemaphoreType.DMA
    anywhere = pl.BlockSpec(memory_space=pl.ANY)
    vmem = pl.BlockSpec(memory_space=pltpu.VMEM)
    image = jax.ShapeDtypeStruct(features.shape, jnp.bfloat16)
    block = pltpu.VMEM((chips, block_rows, LANES), jnp.bfloat16)
    shifted = pltpu.VMEM((frame + 2 * columns, 3 * channels), jnp.bfloat16)
    return pl.pallas_call(
        functools.partial(whole_kernel, scale, lights),
        out_shape=(
            jax.ShapeDtypeStruct((chips, width), jnp.bfloat16),
            jax.ShapeDtypeStruct((chips, own_len), jnp.bfloat16),
            image,
            image,
        ),
        in_specs=[vmem, anywhere, anywhere, anywhere],
        out_specs=(vmem, vmem, anywhere, anywhere),
        scratch_shapes=[
            pltpu.VMEM((width, own_len), jnp.bfloat16),
            pltpu.VMEM((8 * lights, LANES), jnp.float32),
            pltpu.VMEM((chips * 40, LANES), jnp.float32),
            block,
            pltpu.VMEM((2, chips, block_rows, LANES), jnp.bfloat16),
            pltpu.VMEM((2, 2 * depth, LANES), jnp.float32),
            pltpu.VMEM((AT_ONCE, block_rows, LANES), jnp.float32),
            pltpu.VMEM((2 * depth, channels), jnp.bfloat16),
            pltpu.VMEM((rows, columns, channels), jnp.bfloat16),
            pltpu.VMEM((rows, columns, channels), jnp.bfloat16),
            shifted,
            shifted,
            shifted,
            pltpu.VMEM((frame, channels), jnp.float32),
            pltpu.VMEM((CHUNK_ROWS * columns, channels), jnp.float32),
            pltpu.VMEM((own_rows, columns, channels), jnp.bfloat16),
            pltpu.VMEM((own_rows, columns, channels), jnp.bfloat16),
            block,
            block,
            block,
            block,
            dma,
            dma,
            dma,
            dma,
            dma,
            dma,
            dma,
            dma((groups,)),
            dma((groups,)),
            dma((groups,)),
            dma((4,)),
            dma((3,)),
            dma((4,)),
            dma((3,)),
            dma((groups,)),
            dma((groups,)),
            dma,
            dma((groups,)),
            dma((PIECES,)),
            dma((PIECES,)),
            dma((PIECES,)),
            dma((PIECES,)),
        ],
        compiler_params=pltpu.CompilerParams(
            has_side_effects=True, collective_id=0, vmem_limit_bytes=VMEM
        ),
    )(codes, hyper_weight, features, upstream)


def last_kernel(
    scale,
    codes_ref,
    summed_ref,
    relit_ref,
    grad_ref,
    hyper_out,
    relit_out,
    grad_out,
    relit,
    grad,
    ready,
    in_sems,
    image_sems,
    out_sems,
):
    loads = [
        pltpu.make_async_copy(relit_ref, relit, in_sems.at[0]),
        pltpu.make_async_copy(grad_ref, grad, in_sems.at[1]),
    ]
    stores = [
        pltpu.make_async_copy(relit, relit_out, image_sems.at[0]),
        pltpu.make_async_copy(grad, grad_out, image_sems.at[1]),
    ]
    for load in loads:
        load.start()
    codes = codes_ref[...].T
    steps = ready.shape[0]
    width = ready.shape[2]
    pending = []
    for step in range(steps):
        span = pl.ds(step * width, width)
        ready[step] = (
            scale * jnp.dot(codes, summed_ref[:, span], preferred_element_type=jnp.float32)
        ).astype(ready.dtype)
        copy = pltpu.make_async_copy(ready.at[step], hyper_out.at[:, span], out_sems.at[step])
        copy.start()
        pending.append(copy)
        if step in (2, 4):
            loads[step // 2 - 1].wait()
            stores[step // 2 - 1].start()
    for copy in pending + stores:
        copy.wait()


def last_step(scale, codes, summed, relit, feature_grad):
    chips, depth = codes.shape
    own_len = summed.shape[1]
    steps = 9
    anywhere = pl.BlockSpec(memory_space=pl.ANY)
    vmem = pl.BlockSpec(memory_space=pltpu.VMEM)
    return pl.pallas_call(
        functools.partial(last_kernel, scale),
        out_shape=(
            jax.ShapeDtypeStruct((depth, own_len), jnp.bfloat16),
            jax.ShapeDtypeStruct(relit.shape, jnp.bfloat16),
            jax.ShapeDtypeStruct(feature_grad.shape, jnp.bfloat16),
        ),
        in_specs=[vmem, vmem, anywhere, anywhere],
        out_specs=(anywhere,) * 3,
        scratch_shapes=[
            pltpu.VMEM(relit.shape, jnp.bfloat16),
            pltpu.VMEM(feature_grad.shape, jnp.bfloat16),
            pltpu.VMEM((steps, depth, own_len // steps), jnp.bfloat16),
            pltpu.SemaphoreType.DMA((2,)),
            pltpu.SemaphoreType.DMA((2,)),
            pltpu.SemaphoreType.DMA((steps,)),
        ],
        compiler_params=pltpu.CompilerParams(vmem_limit_bytes=VMEM),
    )(codes, summed, relit, feature_grad)


def shards(light_ids, tile_offsets, light_table, hyper_weight, features, upstream_grad):
    channels = features.shape[3]
    scale = 1.0 / math.sqrt(9 * channels)
    lights = lax.axis_size("light")
    own_codes = light_codes(light_ids, tile_offsets, light_table)
    codes, summed, relit, feature_grad = whole(
        scale,
        lights,
        own_codes.astype(jnp.float32),
        hyper_weight,
        features,
        upstream_grad,
    )
    hyper_grad, relit, feature_grad = last_step(scale, codes, summed, relit, feature_grad)
    return (relit, feature_grad, hyper_grad)


def solution(mesh):
    in_specs = (
        P("light"),
        P("light"),
        P(),
        P(None, ("light", "tex")),
        P("light", "tex", None, None),
        P("light", "tex", None, None),
    )
    out_specs = (
        P("light", "tex", None, None),
        P("light", "tex", None, None),
        P(None, ("light", "tex")),
    )
    return jax.shard_map(shards, mesh=mesh, in_specs=in_specs, out_specs=out_specs, check_vma=False)
```

```python
import functools
import math

import jax
import jax.numpy as jnp
from jax import lax
from jax.experimental import pallas as pl
from jax.experimental.pallas import tpu as pltpu
from jax.sharding import PartitionSpec as P

MESH = pl.DeviceIdType.MESH
LANES = 128
GROUP = 16
LINE = 8
HALO = 4
PIECES = 4
AT_ONCE = 4
CHUNK_ROWS = 18
VMEM = 60 * 1024 * 1024


def light_codes(light_ids, tile_offsets, light_table):
    halfway = light_table.shape[1] // 2
    onehot = (
        light_ids[:, None] == jnp.arange(light_table.shape[0], dtype=jnp.int32)[None, :]
    ).astype(jnp.bfloat16)
    looked = jnp.dot(onehot, light_table, preferred_element_type=jnp.float32)
    rates = jnp.exp(-math.log(1000.0) * jnp.arange(halfway, dtype=jnp.float32) / halfway)
    angles = tile_offsets.astype(jnp.float32)[:, None] * rates[None, :]
    summed = looked + jnp.concatenate([jnp.sin(angles), jnp.cos(angles)], axis=1)
    return (summed * lax.rsqrt(jnp.mean(summed * summed, axis=1, keepdims=True) + 1e-06)).astype(
        jnp.bfloat16
    )


def place():
    light, tex = lax.axis_index("light"), lax.axis_index("tex")
    half, core = tex // 2, tex % 2
    return light, half, core, light * 2 + half


def peer(chip, core):
    return (chip // 2, (chip % 2) * 2 + core)


def line_peer(light, step):
    return light - light % LINE + lax.rem(light % LINE + step, LINE)


def plane_peer(light, step):
    return lax.rem(light + step * LINE, lax.axis_size("light"))


def greet():
    light, tex = lax.axis_index("light"), lax.axis_index("tex")
    lines = lax.axis_size("light") // LINE
    barrier = pltpu.get_barrier_semaphore()

    def signal(target):
        pl.semaphore_signal(barrier, inc=1, device_id=target, device_id_type=MESH)

    for step in range(1, LINE):
        signal((line_peer(light, step), tex))
    for step in range(1, lines):
        signal((plane_peer(light, step), tex))
    for step in range(1, 4):
        signal((light, lax.rem(tex + step, 4)))
    pl.semaphore_wait(barrier, LINE + lines + 1)


def await_bytes(ref, sem):
    pltpu.make_async_copy(ref, ref, sem).wait()


def swap_copies(src, dst, send, recv, start):
    light, half, core, _ = place()
    rows = src.shape[1]
    halo = dst.shape[0] - 2 * rows

    def go(source, target, to_half, to_core, slot, number):
        here = jnp.logical_and(to_half == half, to_core == core)

        @pl.when(here)
        def _():
            if start:
                pltpu.make_async_copy(source, target, recv.at[slot]).start()

        @pl.when(jnp.logical_not(here))
        def _():
            copy = pltpu.make_async_remote_copy(
                src_ref=source,
                dst_ref=target,
                send_sem=send.at[number],
                recv_sem=recv.at[slot],
                device_id=(light, to_half * 2 + to_core),
                device_id_type=MESH,
            )
            if start:
                copy.start()
            else:
                copy.wait_send()

    for to_half in range(2):
        for own in range(2):

            @pl.when(core == own)
            def _():
                go(
                    src.at[to_half],
                    dst.at[pl.ds(own * rows + halo * half, rows)],
                    to_half,
                    half,
                    own,
                    to_half,
                )

        @pl.when(jnp.logical_and(half == 1, core == 0))
        def _():
            go(
                src.at[to_half, pl.ds(0, halo)],
                dst.at[pl.ds(2 * rows, halo)],
                to_half,
                0,
                2,
                2 + to_half,
            )

        @pl.when(jnp.logical_and(half == 0, core == 1))
        def _():
            go(
                src.at[to_half, pl.ds(rows - halo, halo)],
                dst.at[pl.ds(0, halo)],
                to_half,
                1,
                2,
                2 + to_half,
            )


def swap_arrivals(src, dst, recv):
    rows = src.shape[1]
    halo = dst.shape[0] - 2 * rows
    for slot, count in ((0, rows), (1, rows), (2, halo)):
        await_bytes(dst.at[pl.ds(0, count)], recv.at[slot])


def give_back(src, dst, send, recv, piece, start):
    light, half, core, _ = place()
    count = src.shape[0] // PIECES
    to_core, part = piece // (PIECES // 2), piece % (PIECES // 2)
    here = jnp.logical_and(core == half, to_core == core)
    source = src.at[pl.ds(piece * count, count)]
    target = dst.at[half, pl.ds(part * count, count)]
    slot = half * (PIECES // 2) + part

    @pl.when(here)
    def _():
        if start:
            pltpu.make_async_copy(source, target, recv.at[slot]).start()

    @pl.when(jnp.logical_not(here))
    def _():
        copy = pltpu.make_async_remote_copy(
            src_ref=source,
            dst_ref=target,
            send_sem=send.at[piece],
            recv_sem=recv.at[slot],
            device_id=(light, core * 2 + to_core),
            device_id_type=MESH,
        )
        if start:
            copy.start()
        else:
            copy.wait_send()


def whole_kernel(
    scale,
    lights,
    codes_ref,
    hyper_ref,
    feat_ref,
    up_ref,
    codes_out,
    summed_out,
    relit_out,
    grad_out,
    hyper,
    codes,
    table,
    ready,
    blocks,
    wide,
    line,
    kernels,
    feat,
    up,
    feats,
    hidden,
    grads,
    slope,
    total,
    relit,
    grad,
    parts,
    theirs,
    added,
    sums,
    hyper_sem,
    code_send,
    code_recv,
    line_send,
    line_recv,
    own_sem,
    block_send,
    block_recv,
    pass_send,
    pass_recv,
    feat_send,
    feat_recv,
    up_send,
    up_recv,
    core_send,
    core_recv,
    sum_send,
    sum_recv,
    relit_send,
    relit_recv,
    grad_send,
    grad_recv,
):
    light, half, core, me = place()
    chips = 2 * lights
    groups = chips // GROUP
    my_group, my_slot = me // GROUP, me % GROUP
    sibling = (light, half * 2 + 1 - core)
    block_rows = ready.shape[1]
    taps = block_rows // 2
    rows, columns, channels = feat.shape
    own_rows = relit.shape[0]
    frame, own = rows * columns, own_rows * columns
    depth = 9 * channels
    chunk = total.shape[0]
    chunk_rows = chunk // columns
    inner = rows - own_rows
    first_own = pl.multiple_of(core * inner * columns, 16)

    load = pltpu.make_async_copy(hyper_ref, hyper, hyper_sem)
    load.start()
    greet()

    mine = pl.ds(pl.multiple_of(light * 8, 8), 8)
    codes[mine, :] = jnp.concatenate(
        [
            codes_ref[row : row + 1, k * LANES : (k + 1) * LANES]
            for row in range(2)
            for k in range(4)
        ],
        axis=0,
    )
    lines = lights // LINE
    whole_line = pl.ds(pl.multiple_of(light // LINE * (8 * LINE), 8 * LINE), 8 * LINE)

    def code_copy(span, target, send, recv):
        pltpu.make_async_remote_copy(
            src_ref=codes.at[span],
            dst_ref=codes.at[span],
            send_sem=send,
            recv_sem=recv,
            device_id=(target, half * 2 + core),
            device_id_type=MESH,
        ).start()

    for step in range(1, LINE):
        code_copy(mine, line_peer(light, step), code_send, code_recv)
    for image in (feats, hidden, grads):
        edge = jnp.zeros((columns, image.shape[1]), image.dtype)
        image[:columns] = edge
        image[frame + columns :] = edge
    near = codes.at[pl.ds(0, 8 * (LINE - 1))]
    far = codes.at[pl.ds(0, 8 * LINE * (lines - 1))]
    await_bytes(near, code_recv)
    for step in range(1, lines):
        code_copy(whole_line, plane_peer(light, step), line_send, line_recv)
    await_bytes(far, line_recv)
    all_codes = jnp.concatenate(
        [codes[pl.ds(k, chips, stride=4), :] for k in range(4)], axis=1
    ).astype(jnp.bfloat16)
    codes_out[...] = all_codes
    load.wait()

    for row in range(taps):
        product = scale * jnp.dot(
            all_codes,
            hyper[:, row * 2 * LANES : (row + 1) * 2 * LANES],
            preferred_element_type=jnp.float32,
        )
        table[pl.ds(row, chips, stride=40), :] = product[:, :LANES]
        table[pl.ds(taps + row, chips, stride=40), :] = product[:, LANES:]

    def narrow(chip):
        ready[chip] = table[pl.ds(pl.multiple_of(chip * 40, 8), block_rows), :].astype(
            jnp.bfloat16
        )

    narrow(me)
    keep = pltpu.make_async_copy(ready.at[me], blocks.at[core, me], own_sem)
    keep.start()

    def send_block(step, _):
        group = lax.rem(my_group + step // GROUP, groups)
        other = group * GROUP + lax.rem(my_slot + step % GROUP, GROUP)
        narrow(other)
        pltpu.make_async_remote_copy(
            src_ref=ready.at[other],
            dst_ref=blocks.at[core, me],
            send_sem=block_send,
            recv_sem=block_recv.at[my_group],
            device_id=peer(other, core),
            device_id_type=MESH,
        ).start()
        return 0

    lax.fori_loop(1, chips, send_block, 0)
    swap_copies(feat_ref, feat, feat_send, feat_recv, True)
    swap_copies(up_ref, up, up_send, up_recv, True)

    def row_span(row):
        return pl.ds(pl.multiple_of(row * columns, 16), columns)

    def spread(image, row, values):
        span = row_span(row + 1)
        none = jnp.zeros((1, channels), jnp.float32)
        before = jnp.concatenate([none, values[:-1]], axis=0)
        after = jnp.concatenate([values[1:], none], axis=0)
        image[span, :channels] = before.astype(image.dtype)
        image[span, channels : 2 * channels] = values.astype(image.dtype)
        image[span, 2 * channels :] = after.astype(image.dtype)


    def place_feats(row, _):
        spread(feats, row, feat[row].astype(jnp.float32))
        return 0


    def to_sibling(group):
        span = blocks.at[core, pl.ds(group * GROUP, GROUP)]
        return pltpu.make_async_remote_copy(
            src_ref=span,
            dst_ref=span,
            send_sem=pass_send.at[group],
            recv_sem=pass_recv.at[group],
            device_id=sibling,
            device_id_type=MESH,
        )

    def gather(group, from_core):
        def block(step, _):
            several = [group * GROUP + step * AT_ONCE + k for k in range(AT_ONCE)]
            for k, chip in enumerate(several):
                line[k] = blocks[from_core, chip].astype(jnp.float32)
            for k, chip in enumerate(several):

                def move(side, _):
                    wide[side, pl.ds((2 * chip + from_core) * taps, taps), :] = line[
                        k, pl.ds(side * taps, taps), :
                    ]
                    return 0

                lax.fori_loop(0, 2, move, 0)
            return 0

        lax.fori_loop(0, GROUP // AT_ONCE, block, 0)

    def end_group(group):
        to_sibling(group).wait_recv()
        gather(group, 1 - core)
        count = 2 * GROUP * taps
        span = pl.ds(pl.multiple_of(group * count, 16), count)
        kernels[span, :LANES] = wide[0, span, :].astype(jnp.bfloat16)
        kernels[span, LANES:] = wide[1, span, :].astype(jnp.bfloat16)

    keep.wait()
    await_bytes(blocks.at[core, pl.ds(0, GROUP - 1)], block_recv.at[my_group])
    to_sibling(my_group).start()
    gather(my_group, core)

    def take_group(step, _):
        group = lax.rem(my_group + groups - step, groups)
        await_bytes(blocks.at[core, pl.ds(0, GROUP)], block_recv.at[group])
        to_sibling(group).start()
        gather(group, core)
        end_group(lax.rem(group + 1, groups))
        return 0

    lax.fori_loop(1, groups, take_group, 0)
    swap_arrivals(feat_ref, feat, feat_recv)
    swap_arrivals(up_ref, up, up_recv)
    lax.fori_loop(0, rows, place_feats, 0)
    end_group(lax.rem(my_group + 1, groups))

    def conv(image, base, start):
        out = None
        for tap in range(3):
            span = pl.ds(pl.multiple_of(start + tap * columns, 16), chunk)
            piece = jnp.dot(
                image[span, :],
                kernels[base + tap * 3 * channels : base + (tap + 1) * 3 * channels, :],
                preferred_element_type=jnp.float32,
            )
            out = piece if out is None else out + piece
        total[...] = out

    def conv_back(image, base, start, count):
        out = None
        for row_tap in range(3):
            span = pl.ds(pl.multiple_of(start + (2 - row_tap) * columns, 16), count)
            for col_tap in range(3):
                at = base + (row_tap * 3 + col_tap) * channels
                piece = lax.dot_general(
                    image[span, (2 - col_tap) * channels : (3 - col_tap) * channels],
                    kernels[at : at + channels, :],
                    (((1,), (1,)), ((), ())),
                    preferred_element_type=jnp.float32,
                )
                out = piece if out is None else out + piece
        total[:count] = out

    def each_chunk(compute, finish_row):
        def do_chunk(step, _):
            compute(step * chunk)

            def do_row(row, _):
                finish_row(step * chunk_rows + row, total[row_span(row), :])
                return 0

            return lax.fori_loop(0, chunk_rows, do_row, 0)

        lax.fori_loop(0, frame // chunk, do_chunk, 0)

    def store_own(ref, row, values):
        local = row - core * inner

        @pl.when(jnp.logical_and(local >= 0, local < own_rows))
        def _():
            ref[local] = values.astype(ref.dtype)

    def end_first(row, pre):
        sig = jax.nn.sigmoid(pre)
        slope[row_span(row), :] = sig * (1.0 + pre * (1.0 - sig))
        spread(hidden, row, pre * sig)

    def end_second(row, pre):
        sig = jax.nn.sigmoid(pre)
        store_own(relit, row, pre * sig)
        spread(grads, row, up[row].astype(jnp.float32) * (sig * (1.0 + pre * (1.0 - sig))))

    def kernel_grad(image, base):
        upstream = grads[pl.ds(first_own + columns, own), channels : 2 * channels].T

        def do_tap(tap, _):
            span = pl.ds(pl.multiple_of(first_own + tap * columns, 16), own)
            for col_tap in range(3):
                piece = jnp.dot(
                    upstream,
                    image[span, col_tap * channels : (col_tap + 1) * channels],
                    preferred_element_type=jnp.float32,
                )
                at = pl.multiple_of(base + (tap * 3 + col_tap) * channels, channels)
                wide[0, pl.ds(at, channels), :] = piece[:LANES].T
                wide[1, pl.ds(at, channels), :] = piece[LANES:].T
            return 0

        lax.fori_loop(0, 3, do_tap, 0)

    def end_grad(row, back):
        slope[row_span(row), :] = slope[row_span(row), :] * back

    def part_copy(group):
        return pltpu.make_async_remote_copy(
            src_ref=parts.at[pl.ds(group * GROUP, GROUP)],
            dst_ref=theirs.at[pl.ds(group * GROUP, GROUP)],
            send_sem=core_send.at[group],
            recv_sem=core_recv.at[group],
            device_id=sibling,
            device_id_type=MESH,
        )

    def pick(slot, owner):
        for side in range(2):
            line[slot, side * taps : (side + 1) * taps, :] = wide[
                side, pl.ds(owner * taps, taps), :
            ]

    def send_sum(other):
        @pl.when(other == me)
        def _():
            pltpu.make_async_copy(added.at[me], sums.at[me], own_sem).start()

        @pl.when(other != me)
        def _():
            pltpu.make_async_remote_copy(
                src_ref=added.at[other],
                dst_ref=sums.at[me],
                send_sem=sum_send,
                recv_sem=sum_recv.at[my_group],
                device_id=peer(other, core),
                device_id_type=MESH,
            ).start()

    def send_grad(first, between):
        some = groups // 2

        def group_at(step):
            return first + lax.rem(my_group + step, some)

        def share(step):
            group = group_at(step)

            def block(step, _):
                several = [group * GROUP + step * AT_ONCE + k for k in range(AT_ONCE)]
                for k, chip in enumerate(several):
                    pick(k, 2 * chip + 1 - core)
                for k, chip in enumerate(several):
                    parts[chip] = line[k].astype(parts.dtype)
                return 0

            lax.fori_loop(0, GROUP // AT_ONCE, block, 0)
            part_copy(group).start()

        def add(step):
            group = group_at(step)
            part_copy(group).wait_recv()

            def block(step, _):
                several = [
                    group * GROUP + lax.rem(my_slot + step * AT_ONCE + k, GROUP)
                    for k in range(AT_ONCE)
                ]
                for k, other in enumerate(several):
                    pick(k, 2 * other + core)
                for k, other in enumerate(several):
                    added[other] = (line[k] + theirs[other].astype(jnp.float32)).astype(
                        added.dtype
                    )
                for other in several:
                    send_sum(other)
                return 0

            lax.fori_loop(0, GROUP // AT_ONCE, block, 0)

        share(0)

        def both(step, _):
            share(step)
            add(step - 1)
            between(step - 1)
            return 0

        lax.fori_loop(1, some, both, 0)
        add(some - 1)
        between(some - 1)

    def feature_piece(step):
        every = groups // 2 // PIECES

        @pl.when(step % every == every - 1)
        def _():
            feature_rows(step // every)

    def feature_rows(piece):
        count = own // PIECES
        conv_back(grads, 0, pl.multiple_of(first_own + piece * count, 16), count)

        def store(row, _):
            grad[piece * (own_rows // PIECES) + row] = total[row_span(row), :].astype(grad.dtype)
            return 0

        lax.fori_loop(0, own_rows // PIECES, store, 0)
        give_back(grad, grad_out, grad_send, grad_recv, piece, True)

    def relit_piece(piece, _):
        give_back(relit, relit_out, relit_send, relit_recv, piece, True)
        return 0

    each_chunk(lambda start: conv(feats, 0, start), end_first)
    each_chunk(lambda start: conv(hidden, depth, start), end_second)
    lax.fori_loop(0, PIECES, relit_piece, 0)
    kernel_grad(hidden, depth)
    send_grad(groups // 2, lambda step: None)
    each_chunk(lambda start: conv_back(grads, depth, start, chunk), end_grad)

    def place_grad(row, _):
        spread(grads, row, slope[row_span(row), :])
        return 0

    lax.fori_loop(0, rows, place_grad, 0)
    kernel_grad(feats, 0)
    send_grad(0, feature_piece)

    def finish(group, _):
        to_sibling(group).wait_send()
        part_copy(group).wait_send()
        return 0

    lax.fori_loop(0, groups, finish, 0)
    await_bytes(ready.at[pl.ds(0, chips - 1)], block_send)
    await_bytes(near, code_send)
    await_bytes(far, line_send)
    swap_copies(feat_ref, feat, feat_send, feat_recv, False)
    swap_copies(up_ref, up, up_send, up_recv, False)

    def finish_piece(piece, _):
        give_back(relit, relit_out, relit_send, relit_recv, piece, False)
        give_back(grad, grad_out, grad_send, grad_recv, piece, False)
        return 0

    lax.fori_loop(0, PIECES, finish_piece, 0)

    def widen(group):
        def block(slot, _):
            chip = group * GROUP + slot
            table[pl.ds(pl.multiple_of(chip * 40, 8), block_rows), :] = sums[chip].astype(
                jnp.float32
            )
            return 0

        lax.fori_loop(0, GROUP, block, 0)

    pltpu.make_async_copy(added.at[me], sums.at[me], own_sem).wait()
    await_bytes(sums.at[pl.ds(0, GROUP - 1)], sum_recv.at[my_group])
    widen(my_group)

    def take_sums(step, _):
        group = lax.rem(my_group + groups - step, groups)
        await_bytes(sums.at[pl.ds(0, GROUP)], sum_recv.at[group])
        widen(group)
        return 0

    lax.fori_loop(1, groups, take_sums, 0)
    for row in range(taps):
        for side in range(2):
            at = (2 * row + side) * LANES
            summed_out[:, at : at + LANES] = table[
                pl.ds(side * taps + row, chips, stride=40), :
            ].astype(summed_out.dtype)
    await_bytes(added.at[pl.ds(0, chips - 1)], sum_send)
    piece_rows = own_rows // PIECES
    for slot in range(PIECES):
        await_bytes(relit_out.at[0, pl.ds(0, piece_rows)], relit_recv.at[slot])
        await_bytes(grad_out.at[0, pl.ds(0, piece_rows)], grad_recv.at[slot])


def whole(scale, lights, codes, hyper_weight, features, upstream):
    chips = 2 * lights
    groups = chips // GROUP
    width, own_len = hyper_weight.shape
    block_rows = own_len // LANES
    _, rows_dev, columns, channels = features.shape
    depth = 9 * channels
    own_rows = 2 * rows_dev
    rows = own_rows + HALO
    frame = rows * columns
    dma = pltpu.SemaphoreType.DMA
    anywhere = pl.BlockSpec(memory_space=pl.ANY)
    vmem = pl.BlockSpec(memory_space=pltpu.VMEM)
    image = jax.ShapeDtypeStruct(features.shape, jnp.bfloat16)
    block = pltpu.VMEM((chips, block_rows, LANES), jnp.bfloat16)
    shifted = pltpu.VMEM((frame + 2 * columns, 3 * channels), jnp.bfloat16)
    return pl.pallas_call(
        functools.partial(whole_kernel, scale, lights),
        out_shape=(
            jax.ShapeDtypeStruct((chips, width), jnp.bfloat16),
            jax.ShapeDtypeStruct((chips, own_len), jnp.bfloat16),
            image,
            image,
        ),
        in_specs=[vmem, anywhere, anywhere, anywhere],
        out_specs=(vmem, vmem, anywhere, anywhere),
        scratch_shapes=[
            pltpu.VMEM((width, own_len), jnp.bfloat16),
            pltpu.VMEM((8 * lights, LANES), jnp.float32),
            pltpu.VMEM((chips * 40, LANES), jnp.float32),
            block,
            pltpu.VMEM((2, chips, block_rows, LANES), jnp.bfloat16),
            pltpu.VMEM((2, 2 * depth, LANES), jnp.float32),
            pltpu.VMEM((AT_ONCE, block_rows, LANES), jnp.float32),
            pltpu.VMEM((2 * depth, channels), jnp.bfloat16),
            pltpu.VMEM((rows, columns, channels), jnp.bfloat16),
            pltpu.VMEM((rows, columns, channels), jnp.bfloat16),
            shifted,
            shifted,
            shifted,
            pltpu.VMEM((frame, channels), jnp.float32),
            pltpu.VMEM((CHUNK_ROWS * columns, channels), jnp.float32),
            pltpu.VMEM((own_rows, columns, channels), jnp.bfloat16),
            pltpu.VMEM((own_rows, columns, channels), jnp.bfloat16),
            block,
            block,
            block,
            block,
            dma,
            dma,
            dma,
            dma,
            dma,
            dma,
            dma,
            dma((groups,)),
            dma((groups,)),
            dma((groups,)),
            dma((4,)),
            dma((3,)),
            dma((4,)),
            dma((3,)),
            dma((groups,)),
            dma((groups,)),
            dma,
            dma((groups,)),
            dma((PIECES,)),
            dma((PIECES,)),
            dma((PIECES,)),
            dma((PIECES,)),
        ],
        compiler_params=pltpu.CompilerParams(
            has_side_effects=True, collective_id=0, vmem_limit_bytes=VMEM
        ),
    )(codes, hyper_weight, features, upstream)


def last_kernel(
    scale,
    codes_ref,
    summed_ref,
    relit_ref,
    grad_ref,
    hyper_out,
    relit_out,
    grad_out,
    relit,
    grad,
    ready,
    in_sems,
    image_sems,
    out_sems,
):
    loads = [
        pltpu.make_async_copy(relit_ref, relit, in_sems.at[0]),
        pltpu.make_async_copy(grad_ref, grad, in_sems.at[1]),
    ]
    stores = [
        pltpu.make_async_copy(relit, relit_out, image_sems.at[0]),
        pltpu.make_async_copy(grad, grad_out, image_sems.at[1]),
    ]
    for load in loads:
        load.start()
    codes = codes_ref[...].T
    steps = ready.shape[0]
    width = ready.shape[2]
    pending = []
    for step in range(steps):
        span = pl.ds(step * width, width)
        ready[step] = (
            scale * jnp.dot(codes, summed_ref[:, span], preferred_element_type=jnp.float32)
        ).astype(ready.dtype)
        copy = pltpu.make_async_copy(ready.at[step], hyper_out.at[:, span], out_sems.at[step])
        copy.start()
        pending.append(copy)
        if step in (2, 4):
            loads[step // 2 - 1].wait()
            stores[step // 2 - 1].start()
    for copy in pending + stores:
        copy.wait()


def last_step(scale, codes, summed, relit, feature_grad):
    chips, depth = codes.shape
    own_len = summed.shape[1]
    steps = 9
    anywhere = pl.BlockSpec(memory_space=pl.ANY)
    vmem = pl.BlockSpec(memory_space=pltpu.VMEM)
    return pl.pallas_call(
        functools.partial(last_kernel, scale),
        out_shape=(
            jax.ShapeDtypeStruct((depth, own_len), jnp.bfloat16),
            jax.ShapeDtypeStruct(relit.shape, jnp.bfloat16),
            jax.ShapeDtypeStruct(feature_grad.shape, jnp.bfloat16),
        ),
        in_specs=[vmem, vmem, anywhere, anywhere],
        out_specs=(anywhere,) * 3,
        scratch_shapes=[
            pltpu.VMEM(relit.shape, jnp.bfloat16),
            pltpu.VMEM(feature_grad.shape, jnp.bfloat16),
            pltpu.VMEM((steps, depth, own_len // steps), jnp.bfloat16),
            pltpu.SemaphoreType.DMA((2,)),
            pltpu.SemaphoreType.DMA((2,)),
            pltpu.SemaphoreType.DMA((steps,)),
        ],
        compiler_params=pltpu.CompilerParams(vmem_limit_bytes=VMEM),
    )(codes, summed, relit, feature_grad)


def shards(light_ids, tile_offsets, light_table, hyper_weight, features, upstream_grad):
    channels = features.shape[3]
    scale = 1.0 / math.sqrt(9 * channels)
    lights = lax.axis_size("light")
    own_codes = light_codes(light_ids, tile_offsets, light_table)
    codes, summed, relit, feature_grad = whole(
        scale,
        lights,
        own_codes.astype(jnp.float32),
        hyper_weight,
        features,
        upstream_grad,
    )
    hyper_grad, relit, feature_grad = last_step(scale, codes, summed, relit, feature_grad)
    return (relit, feature_grad, hyper_grad)


def solution(mesh):
    in_specs = (
        P("light"),
        P("light"),
        P(),
        P(None, ("light", "tex")),
        P("light", "tex", None, None),
        P("light", "tex", None, None),
    )
    out_specs = (
        P("light", "tex", None, None),
        P("light", "tex", None, None),
        P(None, ("light", "tex")),
    )
    return jax.shard_map(shards, mesh=mesh, in_specs=in_specs, out_specs=out_specs, check_vma=False)
```
